256 devices in a mesh: space: 8 (over x, core), spec: 32 (over z, y).
Axes of the slice: x: 4, y: 4, z: 8, core: 2. Of those that a mesh axis runs over, the one named last changes fastest.
Arguments:
- spectrum: float32 [32, 36, 512, 128], P('spec', None, 'space'), may hold values from 0.2 to 2
- sea_depth: float32 [512, 128], P('space'), may hold values from 5 to 200
- current: float32 [2, 512, 128], P(None, 'space'), may hold values from -3 to 3
- depth_slope: float32 [2, 512, 128], P(None, 'space'), may hold values from -2.5 to 2.5
- wind_forcing: float32 [512, 128], P('space'), may hold values from 0.2 to 2
- wind_angle: float32 [512, 128], P('space'), may hold values from -3.140625 to 3.140625
- land_sea: int32 [512, 128], P('space'), may hold values from 0 to 1, as said below
- quad_table: int32 [4, 1152], replicated, may hold values from 0 to 1151, as said below
- coupling: float32 [1152], replicated, may hold values from 0.01 to 0.04
Outputs:
- updated: float32 [32, 36, 512, 128], P('spec', None, 'space')
The draws below stay inside these ranges and needn't reach their ends.
Inputs may be any that keep to these rules, and one draw needn't show every extreme that they name: `land_sea`: each tile of 64 grid rows holds at most 4096 sea cells; some tile holds exactly that many. `quad_table`: quadruplet partners of bin i * 36 + j: rows 0 and 2 lie 2 or 3 frequencies above i, rows 1 and 3 lie 2 or 3 below, clamped to the frequency range; in direction row 0 lies 1 or 2 bins above j, row 2 1 or 2 below, row 1 3 or 4 below, row 3 3 or 4 above, periodic.
All inputs are finite; a program needn't handle non-finite values.
Results may differ from the reference program's by a relative error of at most 0.0001.
Values sent between devices are 32-bit elements; how exact they have to be, the bound alone decides.
A program may use at most 64 MiB of HBM per device.

```python
import math
import jax
import jax.numpy as jnp
from jax import lax

NFREQ = 32
NDIR = 36
NY = 128
RPS = 2
GX_DEV = 64
NX = 512
NBINS = 1152


def draw_land_sea(key, part):
    key = jax.random.fold_in(key, 11)
    key_limit, key_tile, key_rank = jax.random.split(key, 3)
    limits = jax.random.randint(key_limit, (NX,), NY // 8, NY // 2 + 1)
    chosen_tile = jax.random.randint(key_tile, (), 0, NX // GX_DEV)
    tile_of_row = jnp.arange(NX) // GX_DEV
    limits = jnp.where(tile_of_row == chosen_tile, NY // 2, limits)
    ranks = jax.vmap(lambda row_key: jax.random.permutation(row_key, NY))(jax.random.split(key_rank, NX))
    return (ranks < limits[:, None]).astype(jnp.int32)


def draw_quad_table(key, part):
    key = jax.random.fold_in(key, 23)
    key_freq, key_dir = jax.random.split(key, 2)
    bins = jnp.arange(NBINS).astype(jnp.int32)
    freq_of_bin = bins // NDIR
    dir_of_bin = bins % NDIR
    signs = jnp.array([1, -1, 1, -1], jnp.int32)
    freq_steps = jax.random.randint(key_freq, (4, NBINS), 2, 4) * signs[:, None]
    bases = jnp.array([1, -4, -2, 3], jnp.int32)
    dir_steps = jax.random.randint(key_dir, (4, NBINS), 0, 2) + bases[:, None]
    dir_steps = dir_steps.at[0, NBINS - 2].set(1)
    dir_steps = dir_steps.at[1, 3].set(-3)
    partner_freq = jnp.clip(freq_of_bin[None, :] + freq_steps, 0, NFREQ - 1)
    partner_dir = (dir_of_bin[None, :] + dir_steps) % NDIR
    return (partner_freq * NDIR + partner_dir).astype(jnp.int32)


def levels(key, dims, shards, low, largest):
    loudness, own = 1.0, jax.random.fold_in(key, 6)
    for dim, shards_of in shards:
        draws = jnp.exp(jax.random.uniform(jax.random.fold_in(own, dim), (shards_of,), jnp.float32, low / len(shards), largest / len(shards)))
        loudness = loudness * jnp.repeat(draws, dims[dim] // shards_of).reshape([-1 if axis == dim else 1 for axis in range(len(dims))])
    return loudness


def noise(own_key, dims, spread, reach, pieces=(), dtype=jnp.bfloat16):
    values = jax.random.normal(own_key, dims, jnp.float32) * spread
    if len(pieces) > 0:
        values = levels(own_key, dims, pieces, -0.22, 0.18) * values
    return jnp.clip(values, min=-reach, max=reach).astype(dtype)


def setup_inputs(seed: int = 0) -> dict:
    key_list = jax.random.split(jax.random.key(seed), 10)
    spectrum = jnp.clip(jnp.exp(math.log(2.0) - 2.3025851 * jax.random.uniform(key_list[0], (NFREQ, NDIR, NX, NY), jnp.float32) ** levels(key_list[0], (NFREQ, NDIR, NX, NY), ((0, 32), (2, 8)), -0.2, 0.2)), 0.2, 2.0)
    sea_depth = jnp.clip(jnp.exp(math.log(200.0) - 3.6888795 * jax.random.uniform(key_list[1], (NX, NY), jnp.float32) ** levels(key_list[1], (NX, NY), ((0, 8),), -0.2, 0.2)), 5.0, 200.0)
    current = noise(key_list[2], (2, NX, NY), 1.0, 3.0, ((1, 8),), jnp.float32)
    depth_slope = noise(key_list[3], (2, NX, NY), 1.0, 2.5, ((1, 8),), jnp.float32)
    wind_forcing = jnp.clip(jnp.exp(math.log(2.0) - 2.3025851 * jax.random.uniform(key_list[4], (NX, NY), jnp.float32) ** levels(key_list[4], (NX, NY), ((0, 8),), -0.2, 0.2)), 0.2, 2.0)
    wind_angle = jnp.clip(jax.random.uniform(key_list[5], (NX, NY), jnp.float32, -3.140625, 3.140625), -3.140625, 3.140625)
    land_sea = draw_land_sea(jax.random.fold_in(key_list[9], 71), 0)
    quad_table = draw_quad_table(jax.random.fold_in(key_list[9], 71), 0)
    coupling = jnp.clip(jnp.exp(jax.random.uniform(key_list[8], (NBINS,), jnp.float32, math.log(0.01), math.log(0.04))), 0.01, 0.04)
    return {"spectrum": spectrum, "sea_depth": sea_depth, "current": current, "depth_slope": depth_slope, "wind_forcing": wind_forcing, "wind_angle": wind_angle, "land_sea": land_sea, "quad_table": quad_table, "coupling": coupling}


def speeds(angular, heading, sea_depth, flow_u, flow_v, slope_x, slope_y):
    tanh_term = jnp.tanh(angular * angular / 9.81 * sea_depth)
    group_speed = 9.81 / (2.0 * angular) * tanh_term
    cosine = jnp.cos(heading)
    sine_part = jnp.sin(heading)
    along_x = 0.025 * (group_speed * cosine + flow_u)
    along_y = 0.025 * (group_speed * sine_part + flow_v)
    turning_rate = 0.2 * (1.0 - tanh_term) * (sine_part * slope_x - cosine * slope_y)
    return (along_x, along_y, turning_rate)

def fluxes(energy, velocity):
    return [(jnp.maximum(speed, 0.0) * energy, jnp.minimum(speed, 0.0) * energy) for speed in velocity]

def divergence(flows, preceding, following):
    (forward_x, backward_x), (forward_y, backward_y), (forward_t, backward_t) = flows
    prev_x = jnp.concatenate([preceding[:, :, None, :], forward_x[:, :, :-1, :]], axis=2)
    next_x = jnp.concatenate([backward_x[:, :, 1:, :], following[:, :, None, :]], axis=2)
    boundary = jnp.zeros_like(forward_y[..., :1])
    prev_y = jnp.concatenate([boundary, forward_y[..., :-1]], axis=-1)
    next_y = jnp.concatenate([backward_y[..., 1:], boundary], axis=-1)
    prev_t = jnp.roll(forward_t, 1, axis=1)
    next_t = jnp.roll(backward_t, -1, axis=1)
    return forward_x + next_x - (prev_x + backward_x) + (forward_y + next_y - (prev_y + backward_y)) + (forward_t + next_t - (prev_t + backward_t))

def source_terms(energy, frequency, heading, quad_table, coupling, forcing, wind_dir):
    part_a = jnp.take(energy, quad_table[0], axis=0)
    part_b = jnp.take(energy, quad_table[1], axis=0)
    part_c = jnp.take(energy, quad_table[2], axis=0)
    part_d = jnp.take(energy, quad_table[3], axis=0)
    weight = coupling[:, None]
    q_one = weight * (energy * energy * (part_a + part_b) - 2.0 * energy * part_a * part_b)
    q_two = weight * (energy * energy * (part_c + part_d) - 2.0 * energy * part_c * part_d)
    nonlinear = -2.0 * (q_one + q_two)
    nonlinear = nonlinear.at[quad_table[0]].add(q_one).at[quad_table[1]].add(q_one)
    nonlinear = nonlinear.at[quad_table[2]].add(q_two).at[quad_table[3]].add(q_two)
    wind_in = 0.05 * forcing[None, :] * jnp.maximum(jnp.cos(heading - wind_dir[None, :]), 0.0) * jnp.sqrt(frequency / 0.04) * energy
    mean_energy = lax.optimization_barrier(jnp.mean(energy, axis=0, keepdims=True))
    decay = 0.3 * (frequency / jnp.max(frequency)) ** 2 * mean_energy * mean_energy * energy
    return wind_in + nonlinear - decay

def reference(spectrum, sea_depth, current, depth_slope, wind_forcing, wind_angle, land_sea, quad_table, coupling):
    wet_mask = land_sea.astype(jnp.float32)
    frequency = 0.04 * jnp.power(1.1, jnp.arange(NFREQ).astype(jnp.float32))
    angular_all = 2.0 * jnp.pi * frequency
    heading = 2.0 * jnp.pi / NDIR * jnp.arange(NDIR).astype(jnp.float32)

    def transport(packed):
        slab, angular = packed
        energy = slab[None] * wet_mask
        velocity = speeds(angular.reshape(1, 1, 1, 1), heading.reshape(1, NDIR, 1, 1), sea_depth, current[0], current[1], depth_slope[0], depth_slope[1])
        zeros_row = jnp.zeros((1, NDIR, NY), jnp.float32)
        change = divergence(fluxes(energy, velocity), zeros_row, zeros_row)
        return (energy - change)[0]
    moved = lax.map(transport, (spectrum, angular_all))
    bin_freq = jnp.repeat(frequency, NDIR)[:, None]
    bin_heading = jnp.tile(heading, NFREQ)[:, None]

    def update(block_id, current_moved):
        offset = (block_id * RPS).astype(jnp.int32)
        wet_rows = lax.dynamic_slice_in_dim(wet_mask, offset, RPS, 0)
        energy = lax.dynamic_slice_in_dim(spectrum, offset, RPS, 2) * wet_rows
        forcing = lax.dynamic_slice_in_dim(wind_forcing, offset, RPS, 0).reshape(-1)
        wind_dir = lax.dynamic_slice_in_dim(wind_angle, offset, RPS, 0).reshape(-1)
        sources = source_terms(energy.reshape(NBINS, RPS * NY), bin_freq, bin_heading, quad_table, coupling, forcing, wind_dir)
        block = lax.dynamic_slice_in_dim(current_moved, offset, RPS, 2)
        result = wet_rows * (block + sources.reshape(NFREQ, NDIR, RPS, NY))
        return lax.dynamic_update_slice_in_dim(current_moved, result, offset, 2)
    return lax.fori_loop(0, NX // RPS, update, moved)
```

```python
import functools
import math

import jax
import jax.numpy as jnp
import numpy as np
from jax import lax
from jax.experimental import pallas as pl
from jax.experimental.pallas import tpu as pltpu
from jax.sharding import PartitionSpec as P

NFREQ, NDIR, ROWS, COLS = 32, 36, 64, 128
NY_DEV = 4
PACKED = 32
PAD = 4
WIDE = NDIR + 2 * PAD
F32 = jnp.float32
VMEM = pl.BlockSpec(memory_space=pltpu.VMEM)
SMEM = pl.BlockSpec(memory_space=pltpu.SMEM)
ROW_SIGN = (1, -1, 1, -1)
ROW_DIRS = ((1, 2), (-3, -4), (-1, -2), (3, 4))


def iota(shape, axis):
    return lax.broadcasted_iota(jnp.int32, shape, axis)


def sea_positions(land):
    wet = land.astype(jnp.bfloat16)
    before = (iota((COLS, COLS), 0) < iota((COLS, COLS), 1)).astype(F32).astype(jnp.bfloat16)
    rank = jnp.dot(wet, before, preferred_element_type=F32)
    count = jnp.dot(wet, jnp.ones((COLS, COLS), jnp.bfloat16), preferred_element_type=F32)
    above = (iota((ROWS, ROWS), 0) > iota((ROWS, ROWS), 1)).astype(F32).astype(jnp.bfloat16)
    start = jnp.dot(above, count.astype(jnp.bfloat16), preferred_element_type=F32)
    return start.astype(jnp.int32), rank.astype(jnp.int32), count.astype(jnp.int32)


def packing(land_ref, lane_ref, row_ref, ends_ref):
    land = land_ref[...]
    start, rank, count = sea_positions(land)
    lanes = iota((ROWS, COLS), 1)
    code = jnp.where(land > 0, lanes | ((lanes - rank) << 8), 0)
    for bit in range(7):
        moved = pltpu.roll(code, COLS - (1 << bit), 1)
        comes = ((moved >> (8 + bit)) & 1) == 1
        stays = ((code >> (8 + bit)) & 1) == 0
        code = jnp.where(comes, moved, jnp.where(stays, code, 0))
    lane_ref[...] = jnp.take_along_axis(code & 127, (lanes - start) & 127, axis=1)
    ends_ref[...] = start + count
    slots = iota((PACKED, COLS), 0) * COLS + iota((PACKED, COLS), 1)

    def count_row(r, total):
        return total + (ends_ref[pl.ds(r, 1), :] <= slots).astype(jnp.int32)

    row_ref[...] = lax.fori_loop(0, ROWS, count_row, jnp.zeros((PACKED, COLS), jnp.int32), unroll=8)


def pack(spectrum_ref, lane_ref, row_ref, packed_ref):
    def one(d, carry):
        staged = []
        for v in range(8):
            rows = slice(8 * v, 8 * v + 8)
            staged.append(jnp.take_along_axis(spectrum_ref[d, rows, :], lane_ref[rows, :], axis=1))
        for q in range(4):
            rows = slice(8 * q, 8 * q + 8)
            source = row_ref[rows, :]
            within, block = source & 7, source >> 3
            out = jnp.zeros((8, COLS), F32)
            for v in range(q, 8):
                out = jnp.where(block == v, jnp.take_along_axis(staged[v], within, axis=0), out)
            packed_ref[d, rows, :] = out
        return carry

    lax.fori_loop(0, NDIR, one, 0)


def unpacking(land_ref, slot_row_ref, slot_lane_ref):
    start, rank, _ = sea_positions(land_ref[...])
    lanes = iota((ROWS, COLS), 1)
    slot_row_ref[...] = (start + ((lanes - start) & 127)) >> 7
    slot_lane_ref[...] = (start + rank) & 127


def unpack_block(load, slot_row, slot_lane, v):
    within, block = slot_row & 7, slot_row >> 3
    staged = jnp.take_along_axis(load(0), within, axis=0)
    for q in range(1, min(v, 3) + 1):
        staged = jnp.where(block == q, jnp.take_along_axis(load(q), within, axis=0), staged)
    return jnp.take_along_axis(staged, slot_lane, axis=1)


def transport_fields(angular, root, depth_ref, current_ref, slope_ref, forcing_ref, angle_ref, fields):
    tanh_term = jnp.tanh(angular * angular / 9.81 * depth_ref[...])
    fields[0] = (0.025 * (9.81 / 2.0)) / angular * tanh_term
    fields[1] = 0.025 * current_ref[0]
    fields[2] = 0.025 * current_ref[1]
    turning = 0.2 * (1.0 - tanh_term)
    fields[3] = turning * slope_ref[0]
    fields[4] = turning * slope_ref[1]
    wind = 0.05 * root * forcing_ref[...]
    fields[5] = wind * jnp.cos(angle_ref[...])
    fields[6] = wind * jnp.sin(angle_ref[...])


def transport(trig_ref, spectrum_ref, land_ref, fields, base, ahead, behind, edges, lo, hi):
    rows, lanes = iota((ROWS, COLS), 0), iota((ROWS, COLS), 1)

    def one(j, carry):
        cosine, sine = trig_ref[j], trig_ref[NDIR + j]
        energy = jnp.where(land_ref[...] > 0, spectrum_ref[j], 0.0)
        group = fields[0]
        along = group * cosine + fields[1]
        fx, bx = jnp.maximum(along, 0.0) * energy, jnp.minimum(along, 0.0) * energy
        across = group * sine + fields[2]
        fy, by = jnp.maximum(across, 0.0) * energy, jnp.minimum(across, 0.0) * energy
        turn = sine * fields[3] - cosine * fields[4]
        ft, bt = jnp.maximum(turn, 0.0) * energy, jnp.minimum(turn, 0.0) * energy
        edges[0, pl.ds(j, 1), :] = fx[ROWS - 1 :, :]
        edges[1, pl.ds(j, 1), :] = bx[:1, :]
        prev_x = jnp.where(rows == 0, 0.0, pltpu.roll(fx, 1, 0))
        next_x = jnp.where(rows == ROWS - 1, 0.0, pltpu.roll(bx, ROWS - 1, 0))
        prev_y = jnp.where(lanes == 0, 0.0, pltpu.roll(fy, 1, 1))
        next_y = jnp.where(lanes == COLS - 1, 0.0, pltpu.roll(by, COLS - 1, 1))
        change = (fx + next_x - (prev_x + bx)) + (fy + next_y - (prev_y + by)) + (ft - bt)
        wind = jnp.maximum(cosine * fields[5] + sine * fields[6], 0.0) * energy
        base[j] = energy - change + wind
        ahead[j + 1] = ft
        behind[j] = bt
        return carry

    lax.fori_loop(lo, hi, one, 0)


def quadruplets(table_ref, coupling_ref, decay_ref, x, square, q_one, q_two, n):
    def one(j, carry):
        for f in range(NY_DEV):
            k = f * NDIR + j
            energy = x[(3 + f) * NDIR + j]
            a, b = x[table_ref[k]], x[table_ref[144 + k]]
            c, d = x[table_ref[288 + k]], x[table_ref[432 + k]]
            scaled = coupling_ref[k] * energy
            first = scaled * (energy * (a + b) - 2.0 * a * b)
            second = scaled * (energy * (c + d) - 2.0 * c * d)
            q_one[f, PAD + j] = first
            q_two[f, PAD + j] = second
            n[3 + f, j] = -2.0 * (first + second) - (decay_ref[f] * square) * energy
        return carry

    lax.fori_loop(0, NDIR, one, 0)
    for f in range(NY_DEV):
        for q in (q_one, q_two):
            for i in range(PAD):
                q[f, i] = q[f, NDIR + i]
                q[f, PAD + NDIR + i] = q[f, PAD + i]


def scatter_target(mask_ref, q_one, q_two, t, j, total):
    for row in range(4):
        q = q_one if row < 2 else q_two
        for step in range(2):
            f = t - 3 - ROW_SIGN[row] * (2 + step)
            if not 0 <= f < NY_DEV:
                continue
            for which in range(2):
                source = j - ROW_DIRS[row][which] + PAD
                at = (((row * 2 + step) * 2 + which) * NY_DEV + f) * WIDE
                term = mask_ref[at + source] * q[f, source]
                total = term if total is None else total + term
    return total


def pack_kernel(spectrum_ref, land_ref, packed_ref, lane_ref, row_ref, ends_ref):
    packing(land_ref, lane_ref, row_ref, ends_ref)
    pack(spectrum_ref, lane_ref, row_ref, packed_ref)


def quad_kernel(table_ref, mask_ref, coupling_ref, decay_ref, x_ref, square_ref, n_ref, q_one, q_two):
    quadruplets(table_ref, coupling_ref, decay_ref, x_ref, square_ref[...], q_one, q_two, n_ref)

    def one(j, carry):
        for t in range(10):
            own = n_ref[t, j] if 3 <= t < 7 else None
            n_ref[t, j] = scatter_target(mask_ref, q_one, q_two, t, j, own)
        return carry

    lax.fori_loop(0, NDIR, one, 0)


def final_kernel(
    scalars_ref, trig_ref, spectrum_ref, depth_ref, current_ref, slope_ref, forcing_ref, angle_ref, land_ref,
    preceding_ref, following_ref, source_ref, out_ref, fields, base, ahead, behind, edges, slot_row, slot_lane,
):
    transport_fields(scalars_ref[0], scalars_ref[1], depth_ref, current_ref, slope_ref, forcing_ref, angle_ref, fields)
    transport(trig_ref, spectrum_ref, land_ref, fields, base, ahead, behind, edges, 0, NDIR)
    ahead[0] = ahead[NDIR]
    behind[NDIR] = behind[0]
    unpacking(land_ref, slot_row, slot_lane)

    def one(j, carry):
        base[j, 0:1, :] += preceding_ref[pl.ds(j, 1), :]
        base[j, ROWS - 1 :, :] -= following_ref[pl.ds(j, 1), :]
        for v in range(8):
            rows = slice(8 * v, 8 * v + 8)
            source = unpack_block(
                lambda q: source_ref[j, 8 * q : 8 * q + 8, :], slot_row[rows, :], slot_lane[rows, :], v
            )
            moved = base[j, rows, :] + ahead[j, rows, :] - behind[j + 1, rows, :]
            out_ref[j, rows, :] = jnp.where(land_ref[rows, :] > 0, moved + source, 0.0)
        return carry

    lax.fori_loop(0, NDIR, one, 0)


def edge_kernel(scalars_ref, trig_ref, spectrum_ref, depth_ref, current_ref, land_ref, edges_ref):
    for side, row in ((0, ROWS - 1), (1, 0)):
        at = slice(row, row + 1)
        angular = scalars_ref[0]
        group = (0.025 * (9.81 / 2.0)) / angular * jnp.tanh(angular * angular / 9.81 * depth_ref[at, :])
        flow = 0.025 * current_ref[0, at, :]
        wet = land_ref[at, :] > 0

        def one(j, carry):
            energy = jnp.where(wet, spectrum_ref[j, at, :], 0.0)
            along = group * trig_ref[j] + flow
            edge = jnp.maximum(along, 0.0) if side == 0 else jnp.minimum(along, 0.0)
            edges_ref[side, pl.ds(j, 1), :] = edge * energy
            return carry

        lax.fori_loop(0, NDIR, one, 0)


def quad_masks(block, z):
    table = block.reshape(4, NY_DEV, NDIR)
    table = jnp.concatenate([table[..., -PAD:], table, table[..., :PAD]], axis=-1)
    freq = z * NY_DEV + jnp.arange(NY_DEV)
    direction = (jnp.arange(WIDE) - PAD) % NDIR
    masks = []
    for row in range(4):
        near = jnp.clip(freq + 2 * ROW_SIGN[row], 0, NFREQ - 1)
        far = jnp.clip(freq + 3 * ROW_SIGN[row], 0, NFREQ - 1)
        for target in (near, jnp.where(far == near, -NFREQ, far)):
            for turn in ROW_DIRS[row]:
                bins = target[:, None] * NDIR + ((direction + turn) % NDIR)[None, :]
                masks.append(table[row] == bins)
    return jnp.stack(masks).astype(F32).reshape(-1)


def on_device(spectrum, sea_depth, current, depth_slope, wind_forcing, wind_angle, land_sea, quad_table, coupling):
    spectrum = spectrum.reshape(NDIR, ROWS, COLS)
    index = lax.axis_index("spec")
    z, y = index // NY_DEV, index % NY_DEV
    planes = NFREQ // NY_DEV
    heading = np.float32(2.0 * np.pi / NDIR) * np.arange(NDIR, dtype=np.float32)
    trig = jnp.asarray(np.concatenate([np.cos(heading), np.sin(heading)]).astype(np.float32))
    growth = jnp.power(1.1, index.astype(F32))
    scalars = jnp.stack([2.0 * jnp.pi * 0.04 * growth, jnp.sqrt(growth)])
    own = z * NY_DEV + jnp.arange(NY_DEV)
    decay = 0.3 * jnp.power(1.1, (own - (NFREQ - 1)).astype(F32)) ** 2

    packed = pl.pallas_call(
        pack_kernel,
        out_shape=jax.ShapeDtypeStruct((NDIR, PACKED, COLS), F32),
        in_specs=[VMEM, VMEM],
        out_specs=VMEM,
        scratch_shapes=[
            pltpu.VMEM((ROWS, COLS), jnp.int32),
            pltpu.VMEM((PACKED, COLS), jnp.int32),
            pltpu.VMEM((ROWS, COLS), jnp.int32),
        ],
        compiler_params=pltpu.CompilerParams(vmem_limit_bytes=32 << 20),
    )(spectrum, land_sea)

    edges = pl.pallas_call(
        edge_kernel,
        out_shape=jax.ShapeDtypeStruct((2, NDIR, COLS), F32),
        in_specs=[SMEM, SMEM] + [VMEM] * 4,
        out_specs=VMEM,
    )(scalars, trig, spectrum, sea_depth, current, land_sea)
    spaces = lax.axis_size("space")
    preceding = lax.ppermute(edges[0], "space", [(i, i + 1) for i in range(spaces - 1)])
    following = lax.ppermute(edges[1], "space", [(i + 1, i) for i in range(spaces - 1)])

    groups = [[a * NY_DEV + b for b in range(NY_DEV)] for a in range(planes)]
    columns = [[a * NY_DEV + b for a in range(planes)] for b in range(NY_DEV)]
    quarter = packed.reshape(NDIR, NY_DEV, 8, COLS).swapaxes(0, 1)
    plane = lax.all_to_all(quarter, "spec", 0, 0, axis_index_groups=groups, tiled=True)
    up = [(i, i + NY_DEV) for i in range(NFREQ - NY_DEV)]
    down = [(i + NY_DEV, i) for i in range(NFREQ - NY_DEV)]
    below = lax.ppermute(plane[1:], "spec", up)
    above = lax.ppermute(plane[:-1], "spec", down)
    total = lax.psum(plane.sum(axis=(0, 1)), "spec", axis_index_groups=columns)
    mean = total / (NFREQ * NDIR)
    x = jnp.concatenate([below, plane, above], axis=0).reshape(10 * NDIR, 8, COLS)
    block = lax.dynamic_slice(quad_table, (0, z * 144), (4, 144))
    table = (block - (z * NY_DEV - 3) * NDIR).reshape(-1)
    n = pl.pallas_call(
        quad_kernel,
        out_shape=jax.ShapeDtypeStruct((10, NDIR, 8, COLS), F32),
        in_specs=[SMEM] * 4 + [VMEM] * 2,
        out_specs=VMEM,
        scratch_shapes=[pltpu.VMEM((NY_DEV, WIDE, 8, COLS), F32)] * 2,
        compiler_params=pltpu.CompilerParams(vmem_limit_bytes=32 << 20),
    )(table, quad_masks(block, z), lax.dynamic_slice(coupling, (z * 144,), (144,)), decay, x, mean * mean)
    from_below = lax.ppermute(n[7:], "spec", up)
    from_above = lax.ppermute(n[:3], "spec", down)
    first = jnp.where(z == 0, n[:3].sum(axis=0), 0.0)
    last = jnp.where(z == planes - 1, n[7:].sum(axis=0), 0.0)
    source = n[3:7] + jnp.concatenate([from_below, last[None]]) + jnp.concatenate([first[None], from_above])
    source = lax.all_to_all(source, "spec", 0, 0, axis_index_groups=groups, tiled=True)
    source = source.swapaxes(0, 1).reshape(NDIR, PACKED, COLS)

    big = pltpu.VMEM((NDIR, ROWS, COLS), F32)
    longer = pltpu.VMEM((NDIR + 1, ROWS, COLS), F32)
    tile = pltpu.VMEM((ROWS, COLS), jnp.int32)
    out = pl.pallas_call(
        final_kernel,
        out_shape=jax.ShapeDtypeStruct((NDIR, ROWS, COLS), F32),
        in_specs=[SMEM, SMEM] + [VMEM] * 10,
        out_specs=VMEM,
        scratch_shapes=[
            pltpu.VMEM((7, ROWS, COLS), F32), big, longer, longer, pltpu.VMEM((2, NDIR, COLS), F32), tile, tile
        ],
        compiler_params=pltpu.CompilerParams(vmem_limit_bytes=40 << 20),
    )(scalars, trig, spectrum, sea_depth, current, depth_slope, wind_forcing, wind_angle, land_sea, preceding, following, source)
    return out.reshape(1, NDIR, ROWS, COLS)


def solution(mesh):
    return jax.shard_map(
        on_device,
        mesh=mesh,
        in_specs=(
            P("spec", None, "space", None),
            P("space", None),
            P(None, "space", None),
            P(None, "space", None),
            P("space", None),
            P("space", None),
            P("space", None),
            P(),
            P(),
        ),
        out_specs=P("spec", None, "space", None),
        check_vma=False,
    )
```

```python
import jax
import jax.numpy as jnp
import numpy as np
from jax import lax
from jax.experimental import pallas as pl
from jax.experimental.pallas import tpu as pltpu
from jax.sharding import PartitionSpec as P

NFREQ, NDIR, ROWS, COLS = 32, 36, 64, 128
NY_DEV = 4
PACKED = 32
PLANES = NFREQ // NY_DEV
HALO = 3
NCH = 3
PART = NDIR // NCH
PLANE_BINS = NY_DEV * NDIR
F32 = jnp.float32
VMEM = pl.BlockSpec(memory_space=pltpu.VMEM)
SMEM = pl.BlockSpec(memory_space=pltpu.SMEM)
ROW_SIGN = (1, -1, 1, -1)
ROW_DIRS = ((1, 2), (-3, -4), (-1, -2), (3, 4))


def iota(shape, axis):
    return lax.broadcasted_iota(jnp.int32, shape, axis)


def sea_positions(land):
    wet = land.astype(jnp.bfloat16)
    before = (iota((COLS, COLS), 0) < iota((COLS, COLS), 1)).astype(F32).astype(jnp.bfloat16)
    rank = jnp.dot(wet, before, preferred_element_type=F32)
    count = jnp.dot(wet, jnp.ones((COLS, COLS), jnp.bfloat16), preferred_element_type=F32)
    above = (iota((ROWS, ROWS), 0) > iota((ROWS, ROWS), 1)).astype(F32).astype(jnp.bfloat16)
    start = jnp.dot(above, count.astype(jnp.bfloat16), preferred_element_type=F32)
    return start.astype(jnp.int32), rank.astype(jnp.int32), count.astype(jnp.int32)


def packing(land_ref, lane_ref, row_ref, ends_ref):
    land = land_ref[...]
    start, rank, count = sea_positions(land)
    lanes = iota((ROWS, COLS), 1)
    code = jnp.where(land > 0, lanes | ((lanes - rank) << 8), 0)
    for bit in range(7):
        moved = pltpu.roll(code, COLS - (1 << bit), 1)
        comes = ((moved >> (8 + bit)) & 1) == 1
        stays = ((code >> (8 + bit)) & 1) == 0
        code = jnp.where(comes, moved, jnp.where(stays, code, 0))
    lane_ref[...] = jnp.take_along_axis(code & 127, (lanes - start) & 127, axis=1)
    ends_ref[...] = start + count
    slots = iota((PACKED, COLS), 0) * COLS + iota((PACKED, COLS), 1)

    def count_row(r, total):
        return total + (ends_ref[pl.ds(r, 1), :] <= slots).astype(jnp.int32)

    row_ref[...] = lax.fori_loop(0, ROWS, count_row, jnp.zeros((PACKED, COLS), jnp.int32), unroll=8)


def pack(spectrum_ref, lane_ref, row_ref, packed_ref, lo, hi):
    def one(d, carry):
        staged = []
        for v in range(8):
            rows = slice(8 * v, 8 * v + 8)
            staged.append(jnp.take_along_axis(spectrum_ref[d, rows, :], lane_ref[rows, :], axis=1))
        for q in range(4):
            rows = slice(8 * q, 8 * q + 8)
            source = row_ref[rows, :]
            within, block = source & 7, source >> 3
            out = jnp.zeros((8, COLS), F32)
            for v in range(q, 8):
                out = jnp.where(block == v, jnp.take_along_axis(staged[v], within, axis=0), out)
            packed_ref[d, rows, :] = out
        return carry

    lax.fori_loop(lo, hi, one, 0)


def unpacking(land_ref, slot_row_ref, slot_lane_ref):
    start, rank, _ = sea_positions(land_ref[...])
    lanes = iota((ROWS, COLS), 1)
    slot_row_ref[...] = (start + ((lanes - start) & 127)) >> 7
    slot_lane_ref[...] = (start + rank) & 127


def unpack_block(load, slot_row, slot_lane, v):
    within, block = slot_row & 7, slot_row >> 3
    staged = jnp.take_along_axis(load(0), within, axis=0)
    for q in range(1, min(v, 3) + 1):
        staged = jnp.where(block == q, jnp.take_along_axis(load(q), within, axis=0), staged)
    return jnp.take_along_axis(staged, slot_lane, axis=1)


def transport_fields(angular, root, depth_ref, current_ref, slope_ref, forcing_ref, angle_ref, fields):
    tanh_term = jnp.tanh(angular * angular / 9.81 * depth_ref[...])
    fields[0] = (0.025 * (9.81 / 2.0)) / angular * tanh_term
    fields[1] = 0.025 * current_ref[0]
    fields[2] = 0.025 * current_ref[1]
    turning = 0.2 * (1.0 - tanh_term)
    fields[3] = turning * slope_ref[0]
    fields[4] = turning * slope_ref[1]
    wind = 0.05 * root * forcing_ref[...]
    fields[5] = wind * jnp.cos(angle_ref[...])
    fields[6] = wind * jnp.sin(angle_ref[...])


def transport(trig_ref, spectrum_ref, land_ref, fields, base, ahead, behind, edges, lo, hi, beside):
    rows, lanes = iota((ROWS, COLS), 0), iota((ROWS, COLS), 1)

    def one(j, carry):
        cosine, sine = trig_ref[j], trig_ref[NDIR + j]
        energy = jnp.where(land_ref[...] > 0, spectrum_ref[j], 0.0)
        group = fields[0]
        along = group * cosine + fields[1]
        fx, bx = jnp.maximum(along, 0.0) * energy, jnp.minimum(along, 0.0) * energy
        across = group * sine + fields[2]
        fy, by = jnp.maximum(across, 0.0) * energy, jnp.minimum(across, 0.0) * energy
        turn = sine * fields[3] - cosine * fields[4]
        ft, bt = jnp.maximum(turn, 0.0) * energy, jnp.minimum(turn, 0.0) * energy
        edges[0, pl.ds(j, 1), :] = fx[ROWS - 1 :, :]
        edges[1, pl.ds(j, 1), :] = bx[:1, :]
        prev_x = jnp.where(rows == 0, 0.0, pltpu.roll(fx, 1, 0))
        next_x = jnp.where(rows == ROWS - 1, 0.0, pltpu.roll(bx, ROWS - 1, 0))
        prev_y = jnp.where(lanes == 0, 0.0, pltpu.roll(fy, 1, 1))
        next_y = jnp.where(lanes == COLS - 1, 0.0, pltpu.roll(by, COLS - 1, 1))
        change = (fx + next_x - (prev_x + bx)) + (fy + next_y - (prev_y + by)) + (ft - bt)
        wind = jnp.maximum(cosine * fields[5] + sine * fields[6], 0.0) * energy
        base[j] = energy - change + wind
        ahead[j + 1] = ft
        behind[j] = bt
        beside(j)
        return carry

    lax.fori_loop(lo, hi, one, 0)


def quad_masks(table_ref, mask_ref, z, j):
    def wrapped(turn):
        at = j + turn
        return jnp.where(at < 0, at + NDIR, jnp.where(at >= NDIR, at - NDIR, at))

    for row in range(4):
        turns = [wrapped(turn) for turn in ROW_DIRS[row]]
        for f in range(NY_DEV):
            freq = z * NY_DEV + f
            near = jnp.clip(freq + 2 * ROW_SIGN[row], 0, NFREQ - 1)
            far = jnp.clip(freq + 3 * ROW_SIGN[row], 0, NFREQ - 1)
            far = jnp.where(far == near, -NFREQ, far)
            bins = table_ref[row, z * PLANE_BINS + f * NDIR + j]
            for step, target in enumerate((near, far)):
                for which in range(2):
                    at = ((row * 2 + step) * 2 + which) * PLANE_BINS + f * NDIR
                    mask_ref[at + j] = jnp.where(bins == target * NDIR + turns[which], 1.0, 0.0).astype(F32)


def quadruplets(table_ref, coupling_ref, decay, x, square, q_one, q_two, n, z):
    def one(j, carry):
        for f in range(NY_DEV):
            k = z * PLANE_BINS + f * NDIR + j
            energy = x[k]
            a, b = x[table_ref[0, k]], x[table_ref[1, k]]
            c, d = x[table_ref[2, k]], x[table_ref[3, k]]
            scaled = coupling_ref[k] * energy
            first = scaled * (energy * (a + b) - 2.0 * a * b)
            second = scaled * (energy * (c + d) - 2.0 * c * d)
            q_one[f * NDIR + j] = first
            q_two[f * NDIR + j] = second
            n[(HALO + f) * NDIR + j] = -2.0 * (first + second) - (decay[f] * square) * energy
        return carry

    lax.fori_loop(0, NDIR, one, 0)


def scatter(mask_ref, q_one, q_two, n, targets):
    def one(j, carry):
        source = {}
        for turns in ROW_DIRS:
            for turn in turns:
                at = j - turn
                source[turn] = jnp.where(at < 0, at + NDIR, jnp.where(at >= NDIR, at - NDIR, at))
        for t in targets:
            total = n[t * NDIR + j] if HALO <= t < HALO + NY_DEV else None
            for row in range(4):
                q = q_one if row < 2 else q_two
                for step in range(2):
                    f = t - HALO - ROW_SIGN[row] * (2 + step)
                    if not 0 <= f < NY_DEV:
                        continue
                    for which in range(2):
                        at = ((row * 2 + step) * 2 + which) * PLANE_BINS + f * NDIR
                        s = source[ROW_DIRS[row][which]]
                        term = mask_ref[at + s] * q[f * NDIR + s]
                        total = term if total is None else total + term
            n[t * NDIR + j] = total
        return carry

    lax.fori_loop(0, NDIR, one, 0)


def step_kernel(
    const_ref, table_ref, coupling_ref,
    spectrum_ref, depth_ref, current_ref, slope_ref, forcing_ref, angle_ref, land_ref,
    out_ref,
    fields, base, ahead, behind, edges, edge_in, slot_row, slot_lane, lane_ref, row_ref, ends_ref,
    packed, x, n, q_one, q_two, up_in, down_in, source, sums, mask_ref,
    own_sem, send_y, recv_y, send_up, recv_up, send_down, recv_down, send_mean, recv_mean, send_edge, recv_edge,
    send_cup, recv_cup, send_cdown, recv_cdown, send_back, recv_back,
):
    space, spec = lax.axis_index("space"), lax.axis_index("spec")
    z, y = spec // NY_DEV, spec % NY_DEV
    has_up, has_down = z < PLANES - 1, z > 0
    not_first, not_last = space > 0, space < 7

    def to(plane, row):
        return {"spec": plane * NY_DEV + row}

    def remote(src, dst, send, recv, device):
        return pltpu.make_async_remote_copy(
            src_ref=src, dst_ref=dst, send_sem=send, recv_sem=recv, device_id=device, device_id_type=pl.DeviceIdType.MESH
        )

    def signal(device):
        pl.semaphore_signal(barrier, inc=1, device_id=device, device_id_type=pl.DeviceIdType.MESH)

    barrier = pltpu.get_barrier_semaphore()
    for d in range(1, NY_DEV):
        signal(to(z, (y + d) % NY_DEV))
    for d in range(1, PLANES):
        signal(to((z + d) % PLANES, y))

    @pl.when(not_first)
    def _():
        signal({"space": space - 1})

    @pl.when(not_last)
    def _():
        signal({"space": space + 1})

    def bins(freq, c):
        return pl.ds(freq * NDIR + c * PART, PART)

    def eight(row):
        return pl.ds(pl.multiple_of(row * 8, 8), 8)

    def at(f, c):
        return x.at[bins(z * NY_DEV + f, c)]

    def along_y(d, c):
        row = (y + d) % NY_DEV
        src = packed.at[pl.ds(c * PART, PART), eight(row), :]
        return remote(src, at(y, c), send_y.at[d, c], recv_y.at[y, c], to(z, row))

    def from_y(d, c):
        f = (y + d) % NY_DEV
        return remote(at(f, c), at(f, c), send_y.at[d, c], recv_y.at[f, c], to(z, f))

    def up(f, c, src=None):
        src = at(f, c) if src is None else src
        return remote(src, at(f, c), send_up.at[f - 1, c], recv_up.at[f - 1, c], to(z + 1, y))

    def down(f, c, src=None):
        src = at(f, c) if src is None else src
        return remote(src, at(f, c), send_down.at[f, c], recv_down.at[f, c], to(z - 1, y))

    def forward(f, c, src=None):
        @pl.when(has_up & (f >= 1))
        def _():
            up(f, c, src).start()

        @pl.when(has_down & (f < HALO))
        def _():
            down(f, c, src).start()

    def own(c):
        return pltpu.make_async_copy(packed.at[pl.ds(c * PART, PART), eight(y), :], at(y, c), own_sem.at[c])

    packing(land_ref, lane_ref, row_ref, ends_ref)
    for c in range(NCH):
        pack(spectrum_ref, lane_ref, row_ref, packed, c * PART, (c + 1) * PART)
        if c == 0:
            pl.semaphore_wait(barrier, 2 + PLANES + not_first.astype(jnp.int32) + not_last.astype(jnp.int32))
        forward(y, c, packed.at[pl.ds(c * PART, PART), eight(y), :])
        for d in (1, 3, 2):
            along_y(d, c).start()
        own(c).start()

    transport_fields(
        const_ref[2 * NDIR + spec], const_ref[2 * NDIR + NFREQ + spec],
        depth_ref, current_ref, slope_ref, forcing_ref, angle_ref, fields,
    )
    for c in range(NCH):
        for d in (1, 3, 2):
            from_y(d, c).wait_recv()
            forward((y + d) % NY_DEV, c)
        transport(const_ref, spectrum_ref, land_ref, fields, base, ahead, behind, edges, c * PART, (c + 1) * PART,
                  lambda j: quad_masks(table_ref, mask_ref, z, j))
        own(c).wait()

    def edge(side):
        return remote(edges.at[side], edge_in.at[side], send_edge.at[side], recv_edge.at[side],
                      {"space": space + 1 if side == 0 else space - 1})

    @pl.when(not_last)
    def _():
        edge(0).start()

    @pl.when(not_first)
    def _():
        edge(1).start()

    def add_up(k, total):
        return total + x[z * PLANE_BINS + k]

    sums[z] = lax.fori_loop(0, PLANE_BINS, add_up, jnp.zeros((8, COLS), F32), unroll=8)

    def mean(d):
        return remote(sums.at[z], sums.at[z], send_mean.at[d], recv_mean.at[z], to((z + d) % PLANES, y))

    for d in range(1, PLANES):
        mean(d).start()
    ahead[0] = ahead[NDIR]
    behind[NDIR] = behind[0]
    unpacking(land_ref, slot_row, slot_lane)
    for d in range(1, PLANES):
        other = (z + d) % PLANES
        remote(sums.at[other], sums.at[other], send_mean.at[d], recv_mean.at[other], to(other, y)).wait_recv()
    square = jnp.sum(sums[...], axis=0) * (1.0 / (NFREQ * NDIR))
    square = square * square

    @pl.when(has_down)
    def _():
        for c in range(NCH):
            for f in range(1, NY_DEV):
                remote(at(f - NY_DEV, c), at(f - NY_DEV, c), send_up.at[f - 1, c], recv_up.at[f - 1, c], to(z - 1, y)).wait_recv()

    @pl.when(has_up)
    def _():
        for c in range(NCH):
            for f in range(HALO):
                remote(at(NY_DEV + f, c), at(NY_DEV + f, c), send_down.at[f, c], recv_down.at[f, c], to(z + 1, y)).wait_recv()

    decay = [const_ref[2 * NDIR + 2 * NFREQ + z * NY_DEV + f] for f in range(NY_DEV)]
    quadruplets(table_ref, coupling_ref, decay, x, square, q_one, q_two, n, z)
    scatter(mask_ref, q_one, q_two, n, (0, 1, 2, 7, 8, 9))

    def whole(freq):
        return pl.ds(freq * NDIR, NDIR)

    def give_up(f):
        return remote(n.at[whole(HALO + NY_DEV + f)], up_in.at[f], send_cup.at[f], recv_cup.at[f], to(z + 1, y))

    def give_down(f):
        return remote(n.at[whole(f - 1)], down_in.at[f - 1], send_cdown.at[f - 1], recv_cdown.at[f - 1], to(z - 1, y))

    for d in (2, 1, 3, 0):
        f = (y + d) % NY_DEV

        @pl.when(has_up & (f < HALO))
        def _():
            give_up(f).start()

        @pl.when(has_down & (f >= 1))
        def _():
            give_down(f).start()

    scatter(mask_ref, q_one, q_two, n, (3, 4, 5, 6))

    @pl.when(z == 0)
    def _():
        def fold(j, carry):
            n[HALO * NDIR + j] += n[j] + n[NDIR + j] + n[2 * NDIR + j]
            return carry

        lax.fori_loop(0, NDIR, fold, 0)

    @pl.when(z == PLANES - 1)
    def _():
        def fold(j, carry):
            n[6 * NDIR + j] += n[7 * NDIR + j] + n[8 * NDIR + j] + n[9 * NDIR + j]
            return carry

        lax.fori_loop(0, NDIR, fold, 0)

    def back(d):
        f = (y + d) % NY_DEV
        return remote(n.at[whole(HALO + f)], source.at[:, eight(y), :], send_back.at[d], recv_back.at[y], to(z, f))

    for d in (2, 1, 3, 0):
        f = (y + d) % NY_DEV

        @pl.when(has_down & (f < HALO))
        def _():
            remote(n.at[whole(HALO + NY_DEV + f)], up_in.at[f], send_cup.at[f], recv_cup.at[f], to(z - 1, y)).wait_recv()

            def add(j, carry):
                n[(HALO + f) * NDIR + j] += up_in[f, j]
                return carry

            lax.fori_loop(0, NDIR, add, 0, unroll=4)

        @pl.when(has_up & (f >= 1))
        def _():
            remote(n.at[whole(f - 1)], down_in.at[f - 1], send_cdown.at[f - 1], recv_cdown.at[f - 1], to(z + 1, y)).wait_recv()

            def add(j, carry):
                n[(HALO + f) * NDIR + j] += down_in[f - 1, j]
                return carry

            lax.fori_loop(0, NDIR, add, 0, unroll=4)

        if d:
            back(d).start()
        else:
            def keep(j, carry):
                source[j, eight(y), :] = n[(HALO + f) * NDIR + j]
                return carry

            lax.fori_loop(0, NDIR, keep, 0, unroll=4)

    for side, there in ((0, not_first), (1, not_last)):
        @pl.when(there)
        def _():
            remote(edges.at[side], edge_in.at[side], send_edge.at[side], recv_edge.at[side],
                   {"space": space - 1 if side == 0 else space + 1}).wait_recv()

        @pl.when(jnp.logical_not(there))
        def _():
            edge_in[side] = jnp.zeros((NDIR, COLS), F32)

    for d in (2, 1, 3):
        f = (y + d) % NY_DEV
        remote(n.at[whole(HALO)], source.at[:, eight(f), :], send_back.at[d], recv_back.at[f], to(z, f)).wait_recv()

    def finish(j, carry):
        base[j, 0:1, :] += edge_in[0, pl.ds(j, 1), :]
        base[j, ROWS - 1 :, :] -= edge_in[1, pl.ds(j, 1), :]
        for v in range(8):
            rows = slice(8 * v, 8 * v + 8)
            added = unpack_block(lambda q: source[j, 8 * q : 8 * q + 8, :], slot_row[rows, :], slot_lane[rows, :], v)
            moved = base[j, rows, :] + ahead[j, rows, :] - behind[j + 1, rows, :]
            out_ref[j, rows, :] = jnp.where(land_ref[rows, :] > 0, moved + added, 0.0)
        return carry

    lax.fori_loop(0, NDIR, finish, 0)

    for c in range(NCH):
        for d in range(1, NY_DEV):
            along_y(d, c).wait_send()

    @pl.when(has_up)
    def _():
        for c in range(NCH):
            for f in range(1, NY_DEV):
                up(f, c).wait_send()
        for f in range(HALO):
            give_up(f).wait_send()

    @pl.when(has_down)
    def _():
        for c in range(NCH):
            for f in range(HALO):
                down(f, c).wait_send()
        for f in range(1, NY_DEV):
            give_down(f).wait_send()

    for d in range(1, PLANES):
        mean(d).wait_send()
    for d in range(1, NY_DEV):
        back(d).wait_send()

    @pl.when(not_last)
    def _():
        edge(0).wait_send()

    @pl.when(not_first)
    def _():
        edge(1).wait_send()


def constants():
    heading = np.float32(2.0 * np.pi / NDIR) * np.arange(NDIR, dtype=np.float32)
    growth = 1.1 ** np.arange(NFREQ)
    parts = [np.cos(heading), np.sin(heading), 2.0 * np.pi * 0.04 * growth, np.sqrt(growth), 0.3 * (growth / growth[-1]) ** 2]
    return np.concatenate(parts).astype(np.float32)


def on_device(spectrum, sea_depth, current, depth_slope, wind_forcing, wind_angle, land_sea, quad_table, coupling):
    spectrum = spectrum.reshape(NDIR, ROWS, COLS)
    dma = pltpu.SemaphoreType.DMA
    tile = pltpu.VMEM((ROWS, COLS), jnp.int32)
    longer = pltpu.VMEM((NDIR + 1, ROWS, COLS), F32)
    edges = pltpu.VMEM((2, NDIR, COLS), F32)
    own_bins = pltpu.VMEM((PLANE_BINS, 8, COLS), F32)
    all_bins = pltpu.VMEM(((NY_DEV + 2 * HALO) * NDIR, 8, COLS), F32)
    halo = pltpu.VMEM((HALO, NDIR, 8, COLS), F32)
    packed = pltpu.VMEM((NDIR, PACKED, COLS), F32)
    out = pl.pallas_call(
        step_kernel,
        out_shape=jax.ShapeDtypeStruct((NDIR, ROWS, COLS), F32),
        in_specs=[SMEM] * 3 + [VMEM] * 7,
        out_specs=VMEM,
        scratch_shapes=[
            pltpu.VMEM((7, ROWS, COLS), F32), pltpu.VMEM((NDIR, ROWS, COLS), F32), longer, longer, edges, edges,
            tile, tile, tile, pltpu.VMEM((PACKED, COLS), jnp.int32), tile,
            packed, pltpu.VMEM((NFREQ * NDIR, 8, COLS), F32), all_bins, own_bins, own_bins, halo, halo, packed,
            pltpu.VMEM((PLANES, 8, COLS), F32), pltpu.SMEM((16 * PLANE_BINS,), F32),
            dma((NCH,)), dma((NY_DEV, NCH)), dma((NY_DEV, NCH)),
            dma((HALO, NCH)), dma((HALO, NCH)), dma((HALO, NCH)), dma((HALO, NCH)),
            dma((PLANES,)), dma((PLANES,)), dma((2,)), dma((2,)),
            dma((HALO,)), dma((HALO,)), dma((HALO,)), dma((HALO,)), dma((NY_DEV,)), dma((NY_DEV,)),
        ],
        compiler_params=pltpu.CompilerParams(vmem_limit_bytes=40 << 20, collective_id=0, has_side_effects=True),
    )(jnp.asarray(constants()), quad_table, coupling, spectrum, sea_depth, current, depth_slope, wind_forcing, wind_angle, land_sea)
    return out.reshape(1, NDIR, ROWS, COLS)


def solution(mesh):
    return jax.shard_map(
        on_device,
        mesh=mesh,
        in_specs=(
            P("spec", None, "space", None),
            P("space", None),
            P(None, "space", None),
            P(None, "space", None),
            P("space", None),
            P("space", None),
            P("space", None),
            P(),
            P(),
        ),
        out_specs=P("spec", None, "space", None),
        check_vma=False,
    )
```

```python
import jax
import jax.numpy as jnp
import numpy as np
from jax import lax
from jax.experimental import pallas as pl
from jax.experimental.pallas import tpu as pltpu
from jax.sharding import PartitionSpec as P

NFREQ, NDIR, ROWS, COLS = 32, 36, 64, 128
NY_DEV = 4
PACKED = 32
PLANES = NFREQ // NY_DEV
HALO = 3
NCH = 3
PART = NDIR // NCH
PLANE_BINS = NY_DEV * NDIR
F32 = jnp.float32
VMEM = pl.BlockSpec(memory_space=pltpu.VMEM)
SMEM = pl.BlockSpec(memory_space=pltpu.SMEM)
ROW_SIGN = (1, -1, 1, -1)
ROW_DIRS = ((1, 2), (-3, -4), (-1, -2), (3, 4))


def iota(shape, axis):
    return lax.broadcasted_iota(jnp.int32, shape, axis)


def sea_positions(land):
    wet = land.astype(jnp.bfloat16)
    before = (iota((COLS, COLS), 0) < iota((COLS, COLS), 1)).astype(F32).astype(jnp.bfloat16)
    rank = jnp.dot(wet, before, preferred_element_type=F32)
    count = jnp.dot(wet, jnp.ones((COLS, COLS), jnp.bfloat16), preferred_element_type=F32)
    above = (iota((ROWS, ROWS), 0) > iota((ROWS, ROWS), 1)).astype(F32).astype(jnp.bfloat16)
    start = jnp.dot(above, count.astype(jnp.bfloat16), preferred_element_type=F32)
    return start.astype(jnp.int32), rank.astype(jnp.int32), count.astype(jnp.int32)


def packing(land_ref, lane_ref, row_ref, ends_ref):
    land = land_ref[...]
    start, rank, count = sea_positions(land)
    lanes = iota((ROWS, COLS), 1)
    code = jnp.where(land > 0, lanes | ((lanes - rank) << 8), 0)
    for bit in range(7):
        moved = pltpu.roll(code, COLS - (1 << bit), 1)
        comes = ((moved >> (8 + bit)) & 1) == 1
        stays = ((code >> (8 + bit)) & 1) == 0
        code = jnp.where(comes, moved, jnp.where(stays, code, 0))
    lane_ref[...] = jnp.take_along_axis(code & 127, (lanes - start) & 127, axis=1)
    ends_ref[...] = start + count
    slots = iota((PACKED, COLS), 0) * COLS + iota((PACKED, COLS), 1)

    def count_row(r, total):
        return total + (ends_ref[pl.ds(r, 1), :] <= slots).astype(jnp.int32)

    row_ref[...] = lax.fori_loop(0, ROWS, count_row, jnp.zeros((PACKED, COLS), jnp.int32), unroll=8)


def pack(spectrum_ref, lane_ref, row_ref, packed_ref, lo, hi):
    def one(d, carry):
        staged = []
        for v in range(8):
            rows = slice(8 * v, 8 * v + 8)
            staged.append(jnp.take_along_axis(spectrum_ref[d, rows, :], lane_ref[rows, :], axis=1))
        for q in range(4):
            rows = slice(8 * q, 8 * q + 8)
            source = row_ref[rows, :]
            within, block = source & 7, source >> 3
            out = jnp.zeros((8, COLS), F32)
            for v in range(q, 8):
                out = jnp.where(block == v, jnp.take_along_axis(staged[v], within, axis=0), out)
            packed_ref[d, rows, :] = out
        return carry

    lax.fori_loop(lo, hi, one, 0)


def unpacking(land_ref, slot_row_ref, slot_lane_ref):
    start, rank, _ = sea_positions(land_ref[...])
    lanes = iota((ROWS, COLS), 1)
    slot_row_ref[...] = (start + ((lanes - start) & 127)) >> 7
    slot_lane_ref[...] = (start + rank) & 127


def unpack_block(load, slot_row, slot_lane, v):
    within, block = slot_row & 7, slot_row >> 3
    staged = jnp.take_along_axis(load(0), within, axis=0)
    for q in range(1, min(v, 3) + 1):
        staged = jnp.where(block == q, jnp.take_along_axis(load(q), within, axis=0), staged)
    return jnp.take_along_axis(staged, slot_lane, axis=1)


def transport_fields(angular, root, depth_ref, current_ref, slope_ref, forcing_ref, angle_ref, fields):
    tanh_term = jnp.tanh(angular * angular / 9.81 * depth_ref[...])
    fields[0] = (0.025 * (9.81 / 2.0)) / angular * tanh_term
    fields[1] = 0.025 * current_ref[0]
    fields[2] = 0.025 * current_ref[1]
    turning = 0.2 * (1.0 - tanh_term)
    fields[3] = turning * slope_ref[0]
    fields[4] = turning * slope_ref[1]
    wind = 0.05 * root * forcing_ref[...]
    fields[5] = wind * jnp.cos(angle_ref[...])
    fields[6] = wind * jnp.sin(angle_ref[...])


def transport(trig_ref, spectrum_ref, land_ref, fields, base, ahead, behind, edges, lo, hi, beside):
    rows, lanes = iota((ROWS, COLS), 0), iota((ROWS, COLS), 1)

    def one(j, carry):
        cosine, sine = trig_ref[j], trig_ref[NDIR + j]
        energy = jnp.where(land_ref[...] > 0, spectrum_ref[j], 0.0)
        group = fields[0]
        along = group * cosine + fields[1]
        fx, bx = jnp.maximum(along, 0.0) * energy, jnp.minimum(along, 0.0) * energy
        across = group * sine + fields[2]
        fy, by = jnp.maximum(across, 0.0) * energy, jnp.minimum(across, 0.0) * energy
        turn = sine * fields[3] - cosine * fields[4]
        ft, bt = jnp.maximum(turn, 0.0) * energy, jnp.minimum(turn, 0.0) * energy
        edges[0, pl.ds(j, 1), :] = fx[ROWS - 1 :, :]
        edges[1, pl.ds(j, 1), :] = bx[:1, :]
        prev_x = jnp.where(rows == 0, 0.0, pltpu.roll(fx, 1, 0))
        next_x = jnp.where(rows == ROWS - 1, 0.0, pltpu.roll(bx, ROWS - 1, 0))
        prev_y = jnp.where(lanes == 0, 0.0, pltpu.roll(fy, 1, 1))
        next_y = jnp.where(lanes == COLS - 1, 0.0, pltpu.roll(by, COLS - 1, 1))
        change = (fx + next_x - (prev_x + bx)) + (fy + next_y - (prev_y + by)) + (ft - bt)
        wind = jnp.maximum(cosine * fields[5] + sine * fields[6], 0.0) * energy
        base[j] = energy - change + wind
        ahead[j + 1] = ft
        behind[j] = bt
        beside(j)
        return carry

    lax.fori_loop(lo, hi, one, 0)


def quad_masks(table_ref, mask_ref, z, j):
    def wrapped(turn):
        at = j + turn
        return jnp.where(at < 0, at + NDIR, jnp.where(at >= NDIR, at - NDIR, at))

    for row in range(4):
        turns = [wrapped(turn) for turn in ROW_DIRS[row]]
        for f in range(NY_DEV):
            freq = z * NY_DEV + f
            near = jnp.clip(freq + 2 * ROW_SIGN[row], 0, NFREQ - 1)
            far = jnp.clip(freq + 3 * ROW_SIGN[row], 0, NFREQ - 1)
            far = jnp.where(far == near, -NFREQ, far)
            bins = table_ref[row, z * PLANE_BINS + f * NDIR + j]
            for step, target in enumerate((near, far)):
                for which in range(2):
                    at = ((row * 2 + step) * 2 + which) * PLANE_BINS + f * NDIR
                    mask_ref[at + j] = jnp.where(bins == target * NDIR + turns[which], 1.0, 0.0).astype(F32)


def quadruplets(table_ref, coupling_ref, x, q_one, q_two, n, z):
    def one(j, carry):
        for f in range(NY_DEV):
            k = z * PLANE_BINS + f * NDIR + j
            energy = x[k]
            a, b = x[table_ref[0, k]], x[table_ref[1, k]]
            c, d = x[table_ref[2, k]], x[table_ref[3, k]]
            scaled = coupling_ref[k] * energy
            first = scaled * (energy * (a + b) - 2.0 * a * b)
            second = scaled * (energy * (c + d) - 2.0 * c * d)
            q_one[f * NDIR + j] = first
            q_two[f * NDIR + j] = second
            n[(HALO + f) * NDIR + j] = -2.0 * (first + second)
        return carry

    lax.fori_loop(0, NDIR, one, 0)


def decline(decay, square, x, n, z):
    def one(j, carry):
        for f in range(NY_DEV):
            n[(HALO + f) * NDIR + j] -= (decay[f] * square) * x[z * PLANE_BINS + f * NDIR + j]
        return carry

    lax.fori_loop(0, NDIR, one, 0)


def scatter(mask_ref, q_one, q_two, n, targets, lo, hi):
    def one(j, carry):
        source = {}
        for turns in ROW_DIRS:
            for turn in turns:
                at = j - turn
                source[turn] = jnp.where(at < 0, at + NDIR, jnp.where(at >= NDIR, at - NDIR, at))
        for t in targets:
            total = n[t * NDIR + j] if HALO <= t < HALO + NY_DEV else None
            for row in range(4):
                q = q_one if row < 2 else q_two
                for step in range(2):
                    f = t - HALO - ROW_SIGN[row] * (2 + step)
                    if not 0 <= f < NY_DEV:
                        continue
                    for which in range(2):
                        at = ((row * 2 + step) * 2 + which) * PLANE_BINS + f * NDIR
                        s = source[ROW_DIRS[row][which]]
                        term = mask_ref[at + s] * q[f * NDIR + s]
                        total = term if total is None else total + term
            n[t * NDIR + j] = total
        return carry

    lax.fori_loop(lo, hi, one, 0)


def step_kernel(
    const_hbm, table_hbm, coupling_hbm,
    spectrum_hbm, depth_hbm, current_hbm, slope_hbm, forcing_hbm, angle_hbm, land_hbm,
    out_ref,
    const_ref, table_ref, coupling_ref,
    spectrum_ref, depth_ref, current_ref, slope_ref, forcing_ref, angle_ref, land_ref,
    fields, base, ahead, behind, edges, edge_in, slot_row, slot_lane, lane_ref, row_ref, ends_ref,
    packed, x, n, q_one, q_two, up_in, down_in, source, sums, sums_in, mask_ref,
    load_sem, part_sem,
    own_sem, send_y, recv_y, send_up, recv_up, send_down, recv_down, send_mean, recv_mean, send_edge, recv_edge,
    send_cup, recv_cup, send_cdown, recv_cdown, send_back, recv_back,
):
    space, spec = lax.axis_index("space"), lax.axis_index("spec")
    z, y = spec // NY_DEV, spec % NY_DEV
    has_up, has_down = z < PLANES - 1, z > 0
    not_first, not_last = space > 0, space < 7

    def to(plane, row):
        return {"spec": plane * NY_DEV + row}

    def remote(src, dst, send, recv, device):
        return pltpu.make_async_remote_copy(
            src_ref=src, dst_ref=dst, send_sem=send, recv_sem=recv, device_id=device, device_id_type=pl.DeviceIdType.MESH
        )

    def signal(device):
        pl.semaphore_signal(barrier, inc=1, device_id=device, device_id_type=pl.DeviceIdType.MESH)

    def spectrum_load(c):
        part = pl.ds(c * PART, PART)
        return pltpu.make_async_copy(spectrum_hbm.at[part], spectrum_ref.at[part], part_sem.at[c])

    pairs = (
        (land_hbm, land_ref), (const_hbm, const_ref), (depth_hbm, depth_ref), (current_hbm, current_ref),
        (slope_hbm, slope_ref), (forcing_hbm, forcing_ref), (angle_hbm, angle_ref), (table_hbm, table_ref),
        (coupling_hbm, coupling_ref),
    )
    loads = [pltpu.make_async_copy(src, dst, load_sem.at[i]) for i, (src, dst) in enumerate(pairs)]
    loads[0].start()
    for c in range(NCH):
        spectrum_load(c).start()
    for load in loads[1:]:
        load.start()

    barrier = pltpu.get_barrier_semaphore()
    even = space % 2 == 0
    in_spec = NY_DEV - 1 + has_up.astype(jnp.int32) + has_down.astype(jnp.int32)
    in_space = not_first.astype(jnp.int32) + not_last.astype(jnp.int32)
    for d in range(1, NY_DEV):
        signal(to(z, (y + d) % NY_DEV))

    @pl.when(has_up)
    def _():
        signal(to(z + 1, y))

    @pl.when(has_down)
    def _():
        signal(to(z - 1, y))

    def greet():
        pl.semaphore_wait(barrier, in_spec + jnp.where(even, 0, in_space))

        @pl.when(not_first)
        def _():
            signal({"space": space - 1})

        @pl.when(not_last)
        def _():
            signal({"space": space + 1})

    def bins(freq, c):
        return pl.ds(freq * NDIR + c * PART, PART)

    def eight(row):
        return pl.ds(pl.multiple_of(row * 8, 8), 8)

    def at(f, c):
        return x.at[bins(z * NY_DEV + f, c)]

    def along_y(d, c):
        row = (y + d) % NY_DEV
        src = packed.at[pl.ds(c * PART, PART), eight(row), :]
        return remote(src, at(y, c), send_y.at[d, c], recv_y.at[y, c], to(z, row))

    def from_y(d, c):
        f = (y + d) % NY_DEV
        return remote(at(f, c), at(f, c), send_y.at[d, c], recv_y.at[f, c], to(z, f))

    def up(f, c, src=None):
        src = at(f, c) if src is None else src
        return remote(src, at(f, c), send_up.at[f - 1, c], recv_up.at[f - 1, c], to(z + 1, y))

    def down(f, c, src=None):
        src = at(f, c) if src is None else src
        return remote(src, at(f, c), send_down.at[f, c], recv_down.at[f, c], to(z - 1, y))

    def forward(f, c, src=None):
        @pl.when(has_up & (f >= 1))
        def _():
            up(f, c, src).start()

        @pl.when(has_down & (f < HALO))
        def _():
            down(f, c, src).start()

    def own(c):
        return pltpu.make_async_copy(packed.at[pl.ds(c * PART, PART), eight(y), :], at(y, c), own_sem.at[c])

    loads[0].wait()
    packing(land_ref, lane_ref, row_ref, ends_ref)
    for c in range(NCH):
        spectrum_load(c).wait()
        pack(spectrum_ref, lane_ref, row_ref, packed, c * PART, (c + 1) * PART)
        if c == 0:
            greet()
        forward(y, c, packed.at[pl.ds(c * PART, PART), eight(y), :])
        for d in (1, 3, 2):
            along_y(d, c).start()
        own(c).start()

    for load in loads[1:]:
        load.wait()
    transport_fields(
        const_ref[2 * NDIR + spec], const_ref[2 * NDIR + NFREQ + spec],
        depth_ref, current_ref, slope_ref, forcing_ref, angle_ref, fields,
    )
    for c in range(NCH):
        for d in (1, 3, 2):
            from_y(d, c).wait_recv()
            forward((y + d) % NY_DEV, c)
        transport(const_ref, spectrum_ref, land_ref, fields, base, ahead, behind, edges, c * PART, (c + 1) * PART,
                  lambda j: quad_masks(table_ref, mask_ref, z, j))
        own(c).wait()

    def edge(side):
        return remote(edges.at[side], edge_in.at[side], send_edge.at[side], recv_edge.at[side],
                      {"space": space + 1 if side == 0 else space - 1})

    @pl.when(even)
    def _():
        pl.semaphore_wait(barrier, in_space)

    @pl.when(not_last)
    def _():
        edge(0).start()

    @pl.when(not_first)
    def _():
        edge(1).start()

    def add_up(k, total):
        return total + x[z * PLANE_BINS + k]

    total = lax.fori_loop(0, PLANE_BINS, add_up, jnp.zeros((8, COLS), F32), unroll=8)
    sums[0, 0] = total
    sums[1, 0] = total

    def across(stage, way):
        step = 1 << stage
        other = z + step if way == 0 else z - step
        there = (other < PLANES) if way == 0 else (other >= 0)
        comes = (z >= step) if way == 0 else (z + step < PLANES)
        copy = remote(
            sums.at[way, stage], sums_in.at[way, stage], send_mean.at[way, stage], recv_mean.at[way, stage], to(other, y)
        )
        return there, comes, copy

    def sums_out(stage):
        for way in range(2):
            there, _, copy = across(stage, way)

            @pl.when(there)
            def _():
                copy.start()

    def sums_come(stage):
        for way in range(2):
            _, comes, copy = across(stage, way)

            @pl.when(comes)
            def _():
                copy.wait_recv()
                sums[way, stage + 1] = sums[way, stage] + sums_in[way, stage]

            @pl.when(jnp.logical_not(comes))
            def _():
                sums[way, stage + 1] = sums[way, stage]

    sums_out(0)
    ahead[0] = ahead[NDIR]
    behind[NDIR] = behind[0]
    unpacking(land_ref, slot_row, slot_lane)
    sums_come(0)
    sums_out(1)

    @pl.when(has_down)
    def _():
        for c in range(NCH):
            for f in range(1, NY_DEV):
                remote(at(f - NY_DEV, c), at(f - NY_DEV, c), send_up.at[f - 1, c], recv_up.at[f - 1, c], to(z - 1, y)).wait_recv()

    @pl.when(has_up)
    def _():
        for c in range(NCH):
            for f in range(HALO):
                remote(at(NY_DEV + f, c), at(NY_DEV + f, c), send_down.at[f, c], recv_down.at[f, c], to(z + 1, y)).wait_recv()

    sums_come(1)
    sums_out(2)
    quadruplets(table_ref, coupling_ref, x, q_one, q_two, n, z)

    def give_up(f, c):
        return remote(n.at[bins(HALO + NY_DEV + f, c)], up_in.at[bins(f, c)], send_cup.at[f, c], recv_cup.at[f, c], to(z + 1, y))

    def give_down(f, c):
        return remote(n.at[bins(f - 1, c)], down_in.at[bins(f - 1, c)], send_cdown.at[f - 1, c], recv_cdown.at[f - 1, c], to(z - 1, y))

    for c in range(NCH):
        scatter(mask_ref, q_one, q_two, n, (0, 1, 2, 7, 8, 9), c * PART, (c + 1) * PART)

        @pl.when(has_up)
        def _():
            for f in range(HALO):
                give_up(f, c).start()

        @pl.when(has_down)
        def _():
            for f in range(1, NY_DEV):
                give_down(f, c).start()

    scatter(mask_ref, q_one, q_two, n, (3, 4, 5, 6), 0, NDIR)

    @pl.when(z == 0)
    def _():
        def fold(j, carry):
            n[HALO * NDIR + j] += n[j] + n[NDIR + j] + n[2 * NDIR + j]
            return carry

        lax.fori_loop(0, NDIR, fold, 0)

    @pl.when(z == PLANES - 1)
    def _():
        def fold(j, carry):
            n[6 * NDIR + j] += n[7 * NDIR + j] + n[8 * NDIR + j] + n[9 * NDIR + j]
            return carry

        lax.fori_loop(0, NDIR, fold, 0)

    sums_come(2)
    square = (sums[0, 3] + sums[1, 3] - sums[0, 0]) * (1.0 / (NFREQ * NDIR))
    square = square * square
    decline([const_ref[2 * NDIR + 2 * NFREQ + z * NY_DEV + f] for f in range(NY_DEV)], square, x, n, z)

    for side, there in ((0, not_first), (1, not_last)):
        @pl.when(there)
        def _():
            remote(edges.at[side], edge_in.at[side], send_edge.at[side], recv_edge.at[side],
                   {"space": space - 1 if side == 0 else space + 1}).wait_recv()

        @pl.when(jnp.logical_not(there))
        def _():
            edge_in[side] = jnp.zeros((NDIR, COLS), F32)

    def back(d, c):
        f = (y + d) % NY_DEV
        return remote(n.at[bins(HALO + f, c)], source.at[pl.ds(c * PART, PART), eight(y), :], send_back.at[d, c], recv_back.at[y, c], to(z, f))

    def finish(j, carry):
        base[j, 0:1, :] += edge_in[0, pl.ds(j, 1), :]
        base[j, ROWS - 1 :, :] -= edge_in[1, pl.ds(j, 1), :]
        for v in range(8):
            rows = slice(8 * v, 8 * v + 8)
            added = unpack_block(lambda q: source[j, 8 * q : 8 * q + 8, :], slot_row[rows, :], slot_lane[rows, :], v)
            moved = base[j, rows, :] + ahead[j, rows, :] - behind[j + 1, rows, :]
            out_ref[j, rows, :] = jnp.where(land_ref[rows, :] > 0, moved + added, 0.0)
        return carry

    def complete(c):
        @pl.when(has_down)
        def _():
            for f in range(HALO):
                at_n = n.at[bins(HALO + NY_DEV + f, c)]
                remote(at_n, up_in.at[bins(f, c)], send_cup.at[f, c], recv_cup.at[f, c], to(z - 1, y)).wait_recv()

            def add(j, carry):
                for f in range(HALO):
                    n[(HALO + f) * NDIR + j] += up_in[f * NDIR + j]
                return carry

            lax.fori_loop(c * PART, (c + 1) * PART, add, 0)

        @pl.when(has_up)
        def _():
            for f in range(1, NY_DEV):
                at_n = n.at[bins(f - 1, c)]
                remote(at_n, down_in.at[bins(f - 1, c)], send_cdown.at[f - 1, c], recv_cdown.at[f - 1, c], to(z + 1, y)).wait_recv()

            def add(j, carry):
                for f in range(1, NY_DEV):
                    n[(HALO + f) * NDIR + j] += down_in[(f - 1) * NDIR + j]
                return carry

            lax.fori_loop(c * PART, (c + 1) * PART, add, 0)

        for d in (2, 1, 3):
            back(d, c).start()

        def keep(j, carry):
            source[j, eight(y), :] = n[(HALO + y) * NDIR + j]
            return carry

        lax.fori_loop(c * PART, (c + 1) * PART, keep, 0)

    def conclude(c):
        for d in (1, 3, 2):
            f = (y + d) % NY_DEV
            at_source = source.at[pl.ds(c * PART, PART), eight(f), :]
            remote(n.at[bins(HALO, c)], at_source, send_back.at[d, c], recv_back.at[f, c], to(z, f)).wait_recv()
        lax.fori_loop(c * PART, (c + 1) * PART, finish, 0)

    for c in range(NCH):
        complete(c)
        if c:
            conclude(c - 1)
    conclude(NCH - 1)

    for c in range(NCH):
        for d in range(1, NY_DEV):
            along_y(d, c).wait_send()

    @pl.when(has_up)
    def _():
        for c in range(NCH):
            for f in range(1, NY_DEV):
                up(f, c).wait_send()
            for f in range(HALO):
                give_up(f, c).wait_send()

    @pl.when(has_down)
    def _():
        for c in range(NCH):
            for f in range(HALO):
                down(f, c).wait_send()
            for f in range(1, NY_DEV):
                give_down(f, c).wait_send()

    for stage in range(3):
        for way in range(2):
            there, _, copy = across(stage, way)

            @pl.when(there)
            def _():
                copy.wait_send()

    for c in range(NCH):
        for d in range(1, NY_DEV):
            back(d, c).wait_send()

    @pl.when(not_last)
    def _():
        edge(0).wait_send()

    @pl.when(not_first)
    def _():
        edge(1).wait_send()


def constants():
    heading = np.float32(2.0 * np.pi / NDIR) * np.arange(NDIR, dtype=np.float32)
    growth = 1.1 ** np.arange(NFREQ)
    parts = [np.cos(heading), np.sin(heading), 2.0 * np.pi * 0.04 * growth, np.sqrt(growth), 0.3 * (growth / growth[-1]) ** 2]
    return np.concatenate(parts).astype(np.float32)


def on_device(spectrum, sea_depth, current, depth_slope, wind_forcing, wind_angle, land_sea, quad_table, coupling):
    spectrum = spectrum.reshape(NDIR, ROWS, COLS)
    dma = pltpu.SemaphoreType.DMA
    tile, field, two = pltpu.VMEM((ROWS, COLS), jnp.int32), pltpu.VMEM((ROWS, COLS), F32), pltpu.VMEM((2, ROWS, COLS), F32)
    longer = pltpu.VMEM((NDIR + 1, ROWS, COLS), F32)
    edges = pltpu.VMEM((2, NDIR, COLS), F32)
    own_bins = pltpu.VMEM((PLANE_BINS, 8, COLS), F32)
    all_bins = pltpu.VMEM(((NY_DEV + 2 * HALO) * NDIR, 8, COLS), F32)
    halo = pltpu.VMEM((HALO * NDIR, 8, COLS), F32)
    packed = pltpu.VMEM((NDIR, PACKED, COLS), F32)
    out = pl.pallas_call(
        step_kernel,
        out_shape=jax.ShapeDtypeStruct((NDIR, ROWS, COLS), F32),
        in_specs=[pl.BlockSpec(memory_space=pltpu.HBM)] * 10,
        out_specs=VMEM,
        scratch_shapes=[
            pltpu.SMEM((2 * NDIR + 3 * NFREQ,), F32), pltpu.SMEM((4, NFREQ * NDIR), jnp.int32), pltpu.SMEM((NFREQ * NDIR,), F32),
            pltpu.VMEM((NDIR, ROWS, COLS), F32), field, two, two, field, field, tile,
            pltpu.VMEM((7, ROWS, COLS), F32), pltpu.VMEM((NDIR, ROWS, COLS), F32), longer, longer, edges, edges,
            tile, tile, tile, pltpu.VMEM((PACKED, COLS), jnp.int32), tile,
            packed, pltpu.VMEM((NFREQ * NDIR, 8, COLS), F32), all_bins, own_bins, own_bins, halo, halo, packed,
            pltpu.VMEM((2, 4, 8, COLS), F32), pltpu.VMEM((2, 3, 8, COLS), F32), pltpu.SMEM((16 * PLANE_BINS,), F32),
            dma((9,)), dma((NCH,)),
            dma((NCH,)), dma((NY_DEV, NCH)), dma((NY_DEV, NCH)),
            dma((HALO, NCH)), dma((HALO, NCH)), dma((HALO, NCH)), dma((HALO, NCH)),
            dma((2, 3)), dma((2, 3)), dma((2,)), dma((2,)),
            dma((HALO, NCH)), dma((HALO, NCH)), dma((HALO, NCH)), dma((HALO, NCH)), dma((NY_DEV, NCH)), dma((NY_DEV, NCH)),
        ],
        compiler_params=pltpu.CompilerParams(vmem_limit_bytes=40 << 20, collective_id=0, has_side_effects=True),
    )(jnp.asarray(constants()), quad_table, coupling, spectrum, sea_depth, current, depth_slope, wind_forcing, wind_angle, land_sea)
    return out.reshape(1, NDIR, ROWS, COLS)


def solution(mesh):
    return jax.shard_map(
        on_device,
        mesh=mesh,
        in_specs=(
            P("spec", None, "space", None),
            P("space", None),
            P(None, "space", None),
            P(None, "space", None),
            P("space", None),
            P("space", None),
            P("space", None),
            P(),
            P(),
        ),
        out_specs=P("spec", None, "space", None),
        check_vma=False,
    )
```

```python
import jax
import jax.numpy as jnp
import numpy as np
from jax import lax
from jax.experimental import pallas as pl
from jax.experimental.pallas import tpu as pltpu
from jax.sharding import PartitionSpec as P

NFREQ, NDIR, ROWS, COLS = 32, 36, 64, 128
NY_DEV = 4
PACKED = 32
PLANES = NFREQ // NY_DEV
HALO = 3
IN_PARTS = ((0, 6), (6, 12), (18, 18))
OUT_PARTS = ((0, 16), (16, 14), (30, 6))
PLANE_BINS = NY_DEV * NDIR
F32 = jnp.float32
VMEM = pl.BlockSpec(memory_space=pltpu.VMEM)
SMEM = pl.BlockSpec(memory_space=pltpu.SMEM)
ROW_SIGN = (1, -1, 1, -1)
ROW_DIRS = ((1, 2), (-3, -4), (-1, -2), (3, 4))


def iota(shape, axis):
    return lax.broadcasted_iota(jnp.int32, shape, axis)


def sea_positions(land):
    wet = land.astype(jnp.bfloat16)
    before = (iota((COLS, COLS), 0) < iota((COLS, COLS), 1)).astype(F32).astype(jnp.bfloat16)
    rank = jnp.dot(wet, before, preferred_element_type=F32)
    count = jnp.dot(wet, jnp.ones((COLS, COLS), jnp.bfloat16), preferred_element_type=F32)
    above = (iota((ROWS, ROWS), 0) > iota((ROWS, ROWS), 1)).astype(F32).astype(jnp.bfloat16)
    start = jnp.dot(above, count.astype(jnp.bfloat16), preferred_element_type=F32)
    return start.astype(jnp.int32), rank.astype(jnp.int32), count.astype(jnp.int32)


def packing(land_ref, lane_ref, row_ref, ends_ref):
    land = land_ref[...]
    start, rank, count = sea_positions(land)
    lanes = iota((ROWS, COLS), 1)
    code = jnp.where(land > 0, lanes | ((lanes - rank) << 8), 0)
    for bit in range(7):
        moved = pltpu.roll(code, COLS - (1 << bit), 1)
        comes = ((moved >> (8 + bit)) & 1) == 1
        stays = ((code >> (8 + bit)) & 1) == 0
        code = jnp.where(comes, moved, jnp.where(stays, code, 0))
    lane_ref[...] = jnp.take_along_axis(code & 127, (lanes - start) & 127, axis=1)
    ends_ref[...] = start + count
    slots = iota((PACKED, COLS), 0) * COLS + iota((PACKED, COLS), 1)

    def count_row(r, total):
        return total + (ends_ref[pl.ds(r, 1), :] <= slots).astype(jnp.int32)

    row_ref[...] = lax.fori_loop(0, ROWS, count_row, jnp.zeros((PACKED, COLS), jnp.int32), unroll=8)


def pack(spectrum_ref, lane_ref, row_ref, packed_ref, lo, hi, sums):
    def one(d, carry):
        carry, staged = list(carry), []
        for v in range(8):
            rows = slice(8 * v, 8 * v + 8)
            staged.append(jnp.take_along_axis(spectrum_ref[d, rows, :], lane_ref[rows, :], axis=1))
        for q in range(4):
            rows = slice(8 * q, 8 * q + 8)
            source = row_ref[rows, :]
            within, block = source & 7, source >> 3
            out = jnp.zeros((8, COLS), F32)
            for v in range(q, 8):
                out = jnp.where(block == v, jnp.take_along_axis(staged[v], within, axis=0), out)
            packed_ref[d, rows, :] = out
            carry[q] = carry[q] + out
        return tuple(carry)

    return lax.fori_loop(lo, hi, one, tuple(sums))


def unpacking(land_ref, slot_row_ref, slot_lane_ref):
    start, rank, _ = sea_positions(land_ref[...])
    lanes = iota((ROWS, COLS), 1)
    slot_row_ref[...] = (start + ((lanes - start) & 127)) >> 7
    slot_lane_ref[...] = (start + rank) & 127


def unpack_block(load, slot_row, slot_lane, v):
    within, block = slot_row & 7, slot_row >> 3
    staged = jnp.take_along_axis(load(0), within, axis=0)
    for q in range(1, min(v, 3) + 1):
        staged = jnp.where(block == q, jnp.take_along_axis(load(q), within, axis=0), staged)
    return jnp.take_along_axis(staged, slot_lane, axis=1)


def transport_fields(angular, root, depth_ref, current_ref, slope_ref, forcing_ref, angle_ref, fields):
    tanh_term = jnp.tanh(angular * angular / 9.81 * depth_ref[...])
    fields[0] = (0.025 * (9.81 / 2.0)) / angular * tanh_term
    fields[1] = 0.025 * current_ref[0]
    fields[2] = 0.025 * current_ref[1]
    turning = 0.2 * (1.0 - tanh_term)
    fields[3] = turning * slope_ref[0]
    fields[4] = turning * slope_ref[1]
    wind = 0.05 * root * forcing_ref[...]
    fields[5] = wind * jnp.cos(angle_ref[...])
    fields[6] = wind * jnp.sin(angle_ref[...])


def transport(trig_ref, spectrum_ref, land_ref, fields, base, ahead, behind, edges, lo, hi):
    rows, lanes = iota((ROWS, COLS), 0), iota((ROWS, COLS), 1)

    def one(j, carry):
        cosine, sine = trig_ref[j], trig_ref[NDIR + j]
        energy = jnp.where(land_ref[...] > 0, spectrum_ref[j], 0.0)
        group = fields[0]
        along = group * cosine + fields[1]
        fx, bx = jnp.maximum(along, 0.0) * energy, jnp.minimum(along, 0.0) * energy
        across = group * sine + fields[2]
        fy, by = jnp.maximum(across, 0.0) * energy, jnp.minimum(across, 0.0) * energy
        turn = sine * fields[3] - cosine * fields[4]
        ft, bt = jnp.maximum(turn, 0.0) * energy, jnp.minimum(turn, 0.0) * energy
        edges[0, pl.ds(j, 1), :] = fx[ROWS - 1 :, :]
        edges[1, pl.ds(j, 1), :] = bx[:1, :]
        prev_x = jnp.where(rows == 0, 0.0, pltpu.roll(fx, 1, 0))
        next_x = jnp.where(rows == ROWS - 1, 0.0, pltpu.roll(bx, ROWS - 1, 0))
        prev_y = jnp.where(lanes == 0, 0.0, pltpu.roll(fy, 1, 1))
        next_y = jnp.where(lanes == COLS - 1, 0.0, pltpu.roll(by, COLS - 1, 1))
        change = (fx + next_x - (prev_x + bx)) + (fy + next_y - (prev_y + by)) + (ft - bt)
        wind = jnp.maximum(cosine * fields[5] + sine * fields[6], 0.0) * energy
        base[j] = energy - change + wind
        ahead[j + 1] = ft
        behind[j] = bt
        return carry

    lax.fori_loop(lo, hi, one, 0)


def quad_masks(table_ref, mask_ref, z, j):
    def wrapped(turn):
        at = j + turn
        return jnp.where(at < 0, at + NDIR, jnp.where(at >= NDIR, at - NDIR, at))

    for row in range(4):
        turns = [wrapped(turn) for turn in ROW_DIRS[row]]
        for f in range(NY_DEV):
            freq = z * NY_DEV + f
            near = jnp.clip(freq + 2 * ROW_SIGN[row], 0, NFREQ - 1)
            far = jnp.clip(freq + 3 * ROW_SIGN[row], 0, NFREQ - 1)
            far = jnp.where(far == near, -NFREQ, far)
            bins = table_ref[row, z * PLANE_BINS + f * NDIR + j]
            for step, target in enumerate((near, far)):
                for which in range(2):
                    at = ((row * 2 + step) * 2 + which) * PLANE_BINS + f * NDIR
                    mask_ref[at + j] = jnp.where(bins == target * NDIR + turns[which], 1.0, 0.0).astype(F32)


def quadruplets(table_ref, coupling_ref, x, q_one, q_two, n, z):
    def one(j, carry):
        for f in range(NY_DEV):
            k = z * PLANE_BINS + f * NDIR + j
            energy = x[k]
            a, b = x[table_ref[0, k]], x[table_ref[1, k]]
            c, d = x[table_ref[2, k]], x[table_ref[3, k]]
            scaled = coupling_ref[k] * energy
            first = scaled * (energy * (a + b) - 2.0 * a * b)
            second = scaled * (energy * (c + d) - 2.0 * c * d)
            q_one[f * NDIR + j] = first
            q_two[f * NDIR + j] = second
            n[HALO + f, j] = -2.0 * (first + second)
        return carry

    lax.fori_loop(0, NDIR, one, 0)


def scatter(mask_ref, q_one, q_two, n, targets, lo, hi):
    def one(j, carry):
        source = {}
        for turns in ROW_DIRS:
            for turn in turns:
                at = j - turn
                source[turn] = jnp.where(at < 0, at + NDIR, jnp.where(at >= NDIR, at - NDIR, at))
        for t in targets:
            total = n[t, j] if HALO <= t < HALO + NY_DEV else None
            for row in range(4):
                q = q_one if row < 2 else q_two
                for step in range(2):
                    f = t - HALO - ROW_SIGN[row] * (2 + step)
                    if not 0 <= f < NY_DEV:
                        continue
                    for which in range(2):
                        at = ((row * 2 + step) * 2 + which) * PLANE_BINS + f * NDIR
                        s = source[ROW_DIRS[row][which]]
                        term = mask_ref[at + s] * q[f * NDIR + s]
                        total = term if total is None else total + term
            n[t, j] = total
        return carry

    lax.fori_loop(lo, hi, one, 0)


def step_kernel(
    const_hbm, table_hbm, coupling_hbm,
    spectrum_hbm, depth_hbm, current_hbm, slope_hbm, forcing_hbm, angle_hbm, land_hbm,
    out_ref,
    const_ref, table_ref, coupling_ref,
    spectrum_ref, depth_ref, current_ref, slope_ref, forcing_ref, angle_ref, land_ref,
    fields, base, ahead, behind, edges, edge_in, slot_row, slot_lane, lane_ref, row_ref, ends_ref,
    packed, x, n, q_one, q_two, up_in, down_in, source, sums, sums_in, column, decay, mask_ref,
    load_sem, part_sem,
    own_sem, send_y, recv_y, send_up, recv_up, send_down, recv_down, send_mean, recv_mean, send_edge, recv_edge,
    send_cup, recv_cup, send_cdown, recv_cdown, send_back, recv_back, send_col, recv_col,
):
    space, spec = lax.axis_index("space"), lax.axis_index("spec")
    z, y = spec // NY_DEV, spec % NY_DEV
    has_up, has_down = z < PLANES - 1, z > 0
    not_first, not_last = space > 0, space < 7

    def to(plane, row):
        return {"spec": plane * NY_DEV + row}

    def remote(src, dst, send, recv, device):
        return pltpu.make_async_remote_copy(
            src_ref=src, dst_ref=dst, send_sem=send, recv_sem=recv, device_id=device, device_id_type=pl.DeviceIdType.MESH
        )

    def signal(device):
        pl.semaphore_signal(barrier, inc=1, device_id=device, device_id_type=pl.DeviceIdType.MESH)

    def spectrum_load(c):
        part = pl.ds(*IN_PARTS[c])
        return pltpu.make_async_copy(spectrum_hbm.at[part], spectrum_ref.at[part], part_sem.at[c])

    pairs = (
        (land_hbm, land_ref), (const_hbm, const_ref), (depth_hbm, depth_ref), (current_hbm, current_ref),
        (slope_hbm, slope_ref), (forcing_hbm, forcing_ref), (angle_hbm, angle_ref), (table_hbm, table_ref),
        (coupling_hbm, coupling_ref),
    )
    loads = [pltpu.make_async_copy(src, dst, load_sem.at[i]) for i, (src, dst) in enumerate(pairs)]
    loads[0].start()
    for c in range(len(IN_PARTS)):
        spectrum_load(c).start()
    for load in loads[1:]:
        load.start()

    barrier = pltpu.get_barrier_semaphore()
    even = space % 2 == 0
    in_spec = NY_DEV - 1 + has_up.astype(jnp.int32) + has_down.astype(jnp.int32)
    in_space = not_first.astype(jnp.int32) + not_last.astype(jnp.int32)
    for d in range(1, NY_DEV):
        signal(to(z, (y + d) % NY_DEV))

    @pl.when(has_up)
    def _():
        signal(to(z + 1, y))

    @pl.when(has_down)
    def _():
        signal(to(z - 1, y))

    def greet():
        pl.semaphore_wait(barrier, in_spec + jnp.where(even, 0, in_space))

        @pl.when(not_first)
        def _():
            signal({"space": space - 1})

        @pl.when(not_last)
        def _():
            signal({"space": space + 1})

    def bins(freq, c):
        return pl.ds(freq * NDIR + IN_PARTS[c][0], IN_PARTS[c][1])

    def eight(row):
        return pl.ds(pl.multiple_of(row * 8, 8), 8)

    def at(f, c):
        return x.at[bins(z * NY_DEV + f, c)]

    def along_y(d, c):
        row = (y + d) % NY_DEV
        src = packed.at[pl.ds(*IN_PARTS[c]), eight(row), :]
        return remote(src, at(y, c), send_y.at[d, c], recv_y.at[y, c], to(z, row))

    def from_y(d, c):
        f = (y + d) % NY_DEV
        return remote(at(f, c), at(f, c), send_y.at[d, c], recv_y.at[f, c], to(z, f))

    def up(f, c, src=None):
        src = at(f, c) if src is None else src
        return remote(src, at(f, c), send_up.at[f - 1, c], recv_up.at[f - 1, c], to(z + 1, y))

    def down(f, c, src=None):
        src = at(f, c) if src is None else src
        return remote(src, at(f, c), send_down.at[f, c], recv_down.at[f, c], to(z - 1, y))

    def forward(f, c, src=None):
        @pl.when(has_up & (f >= 1))
        def _():
            up(f, c, src).start()

        @pl.when(has_down & (f < HALO))
        def _():
            down(f, c, src).start()

    def own(c):
        return pltpu.make_async_copy(packed.at[pl.ds(*IN_PARTS[c]), eight(y), :], at(y, c), own_sem.at[c])

    loads[0].wait()
    packing(land_ref, lane_ref, row_ref, ends_ref)
    mine = [jnp.zeros((8, COLS), F32)] * 4
    for c, (first, number) in enumerate(IN_PARTS):
        spectrum_load(c).wait()
        mine = pack(spectrum_ref, lane_ref, row_ref, packed, first, first + number, mine)
        if c == 0:
            greet()
        forward(y, c, packed.at[pl.ds(*IN_PARTS[c]), eight(y), :])
        for d in (1, 3, 2):
            along_y(d, c).start()
        own(c).start()

    def across(stage, way):
        step = 1 << stage
        other = z + step if way == 0 else z - step
        there = (other < PLANES) if way == 0 else (other >= 0)
        comes = (z >= step) if way == 0 else (z + step < PLANES)
        copy = remote(
            sums.at[way, stage], sums_in.at[way, stage], send_mean.at[way, stage], recv_mean.at[way, stage], to(other, y)
        )
        return there, comes, copy

    def sums_out(stage):
        for way in range(2):
            there, _, copy = across(stage, way)

            @pl.when(there)
            def _():
                copy.start()

    def sums_come(stage):
        for way in range(2):
            _, comes, copy = across(stage, way)

            @pl.when(comes)
            def _():
                copy.wait_recv()
                sums[way, stage + 1] = sums[way, stage] + sums_in[way, stage]

            @pl.when(jnp.logical_not(comes))
            def _():
                sums[way, stage + 1] = sums[way, stage]

    for way in range(2):
        for q in range(4):
            sums[way, 0, 8 * q : 8 * q + 8, :] = mine[q]
    sums_out(0)
    for load in loads[1:]:
        load.wait()
    transport_fields(
        const_ref[2 * NDIR + spec], const_ref[2 * NDIR + NFREQ + spec],
        depth_ref, current_ref, slope_ref, forcing_ref, angle_ref, fields,
    )
    for c, (first, number) in enumerate(IN_PARTS):
        for d in (1, 3, 2):
            from_y(d, c).wait_recv()
            forward((y + d) % NY_DEV, c)
        own(c).wait()
        if c == len(IN_PARTS) - 1:
            sums_come(0)
            sums_out(1)
        transport(const_ref, spectrum_ref, land_ref, fields, base, ahead, behind, edges, first, first + number)

    def edge(side):
        return remote(edges.at[side], edge_in.at[side], send_edge.at[side], recv_edge.at[side],
                      {"space": space + 1 if side == 0 else space - 1})

    @pl.when(even)
    def _():
        pl.semaphore_wait(barrier, in_space)

    @pl.when(not_last)
    def _():
        edge(0).start()

    @pl.when(not_first)
    def _():
        edge(1).start()

    ahead[0] = ahead[NDIR]
    behind[NDIR] = behind[0]

    def masks(lo, hi):
        def one(j, carry):
            quad_masks(table_ref, mask_ref, z, j)
            return carry

        lax.fori_loop(lo, hi, one, 0)

    masks(0, NDIR // 2)
    sums_come(1)
    sums_out(2)
    masks(NDIR // 2, NDIR)
    unpacking(land_ref, slot_row, slot_lane)

    @pl.when(has_down)
    def _():
        for c in range(len(IN_PARTS)):
            for f in range(1, NY_DEV):
                remote(at(f - NY_DEV, c), at(f - NY_DEV, c), send_up.at[f - 1, c], recv_up.at[f - 1, c], to(z - 1, y)).wait_recv()

    @pl.when(has_up)
    def _():
        for c in range(len(IN_PARTS)):
            for f in range(HALO):
                remote(at(NY_DEV + f, c), at(NY_DEV + f, c), send_down.at[f, c], recv_down.at[f, c], to(z + 1, y)).wait_recv()

    quadruplets(table_ref, coupling_ref, x, q_one, q_two, n, z)

    def give_up(c):
        part = pl.ds(*OUT_PARTS[c])
        return remote(n.at[pl.ds(HALO + NY_DEV, HALO), part], up_in.at[:, part], send_cup.at[c], recv_cup.at[c], to(z + 1, y))

    def give_down(c):
        part = pl.ds(*OUT_PARTS[c])
        return remote(n.at[pl.ds(0, HALO), part], down_in.at[:, part], send_cdown.at[c], recv_cdown.at[c], to(z - 1, y))

    for c, (first, number) in enumerate(OUT_PARTS):
        scatter(mask_ref, q_one, q_two, n, (0, 1, 2, 7, 8, 9), first, first + number)

        @pl.when(has_up)
        def _():
            give_up(c).start()

        @pl.when(has_down)
        def _():
            give_down(c).start()

    scatter(mask_ref, q_one, q_two, n, (3, 4, 5, 6), 0, NDIR)

    @pl.when(z == 0)
    def _():
        def fold(j, carry):
            n[HALO, j] += n[0, j] + n[1, j] + n[2, j]
            return carry

        lax.fori_loop(0, NDIR, fold, 0)

    @pl.when(z == PLANES - 1)
    def _():
        def fold(j, carry):
            n[6, j] += n[7, j] + n[8, j] + n[9, j]
            return carry

        lax.fori_loop(0, NDIR, fold, 0)

    sums_come(2)
    column[y] = sums[0, 3] + sums[1, 3] - sums[0, 0]

    def to_columns(d):
        return remote(column.at[y], column.at[y], send_col.at[d], recv_col.at[y], to(z, (y + d) % NY_DEV))

    for d in (2, 1, 3):
        to_columns(d).start()

    for side, there in ((0, not_first), (1, not_last)):
        @pl.when(there)
        def _():
            remote(edges.at[side], edge_in.at[side], send_edge.at[side], recv_edge.at[side],
                   {"space": space - 1 if side == 0 else space + 1}).wait_recv()

        @pl.when(jnp.logical_not(there))
        def _():
            edge_in[side] = jnp.zeros((NDIR, COLS), F32)

    def back(d, c):
        f = (y + d) % NY_DEV
        part = pl.ds(*OUT_PARTS[c])
        return remote(n.at[HALO + f, part], source.at[part, eight(y), :], send_back.at[d, c], recv_back.at[y, c], to(z, f))

    def finish(j, carry):
        base[j, 0:1, :] += edge_in[0, pl.ds(j, 1), :]
        base[j, ROWS - 1 :, :] -= edge_in[1, pl.ds(j, 1), :]
        for v in range(8):
            rows = slice(8 * v, 8 * v + 8)
            added = unpack_block(lambda q: source[j, 8 * q : 8 * q + 8, :], slot_row[rows, :], slot_lane[rows, :], v)
            moved = base[j, rows, :] + ahead[j, rows, :] - behind[j + 1, rows, :]
            moved = moved - decay[rows, :] * spectrum_ref[j, rows, :]
            out_ref[j, rows, :] = jnp.where(land_ref[rows, :] > 0, moved + added, 0.0)
        return carry

    def complete(c):
        first, number = OUT_PARTS[c]
        part = pl.ds(first, number)

        @pl.when(has_down)
        def _():
            remote(n.at[pl.ds(HALO + NY_DEV, HALO), part], up_in.at[:, part], send_cup.at[c], recv_cup.at[c], to(z - 1, y)).wait_recv()

            def add(j, carry):
                for f in range(HALO):
                    n[HALO + f, j] += up_in[f, j]
                return carry

            lax.fori_loop(first, first + number, add, 0)

        @pl.when(has_up)
        def _():
            remote(n.at[pl.ds(0, HALO), part], down_in.at[:, part], send_cdown.at[c], recv_cdown.at[c], to(z + 1, y)).wait_recv()

            def add(j, carry):
                for f in range(1, NY_DEV):
                    n[HALO + f, j] += down_in[f - 1, j]
                return carry

            lax.fori_loop(first, first + number, add, 0)

        for d in (2, 1, 3):
            back(d, c).start()

        def keep(j, carry):
            source[j, eight(y), :] = n[HALO + y, j]
            return carry

        lax.fori_loop(first, first + number, keep, 0)

    def conclude(c):
        first, number = OUT_PARTS[c]
        for d in (1, 3, 2):
            f = (y + d) % NY_DEV
            at_source = source.at[pl.ds(first, number), eight(f), :]
            remote(n.at[HALO, pl.ds(first, number)], at_source, send_back.at[d, c], recv_back.at[f, c], to(z, f)).wait_recv()
        lax.fori_loop(first, first + number, finish, 0)

    complete(0)
    for d in (1, 3, 2):
        f = (y + d) % NY_DEV
        remote(column.at[f], column.at[f], send_col.at[d], recv_col.at[f], to(z, f)).wait_recv()
    mean = (column[0] + column[1] + column[2] + column[3]) * (1.0 / (NFREQ * NDIR))
    sums[0, 3] = mean * mean
    rate = const_ref[2 * NDIR + 2 * NFREQ + spec]
    for v in range(8):
        rows = slice(8 * v, 8 * v + 8)
        square = unpack_block(lambda q: sums[0, 3, 8 * q : 8 * q + 8, :], slot_row[rows, :], slot_lane[rows, :], v)
        decay[rows, :] = rate * square
    for c in range(1, len(OUT_PARTS)):
        complete(c)
        conclude(c - 1)
    conclude(len(OUT_PARTS) - 1)

    for c in range(len(IN_PARTS)):
        for d in range(1, NY_DEV):
            along_y(d, c).wait_send()

    @pl.when(has_up)
    def _():
        for c in range(len(IN_PARTS)):
            for f in range(1, NY_DEV):
                up(f, c).wait_send()
        for c in range(len(OUT_PARTS)):
            give_up(c).wait_send()

    @pl.when(has_down)
    def _():
        for c in range(len(IN_PARTS)):
            for f in range(HALO):
                down(f, c).wait_send()
        for c in range(len(OUT_PARTS)):
            give_down(c).wait_send()

    for stage in range(3):
        for way in range(2):
            there, _, copy = across(stage, way)

            @pl.when(there)
            def _():
                copy.wait_send()

    for d in range(1, NY_DEV):
        to_columns(d).wait_send()
        for c in range(len(OUT_PARTS)):
            back(d, c).wait_send()

    @pl.when(not_last)
    def _():
        edge(0).wait_send()

    @pl.when(not_first)
    def _():
        edge(1).wait_send()


def constants():
    heading = np.float32(2.0 * np.pi / NDIR) * np.arange(NDIR, dtype=np.float32)
    growth = 1.1 ** np.arange(NFREQ)
    parts = [np.cos(heading), np.sin(heading), 2.0 * np.pi * 0.04 * growth, np.sqrt(growth), 0.3 * (growth / growth[-1]) ** 2]
    return np.concatenate(parts).astype(np.float32)


def on_device(spectrum, sea_depth, current, depth_slope, wind_forcing, wind_angle, land_sea, quad_table, coupling):
    spectrum = spectrum.reshape(NDIR, ROWS, COLS)
    dma, parts, backs = pltpu.SemaphoreType.DMA, len(IN_PARTS), len(OUT_PARTS)
    tile, field, two = pltpu.VMEM((ROWS, COLS), jnp.int32), pltpu.VMEM((ROWS, COLS), F32), pltpu.VMEM((2, ROWS, COLS), F32)
    longer = pltpu.VMEM((NDIR + 1, ROWS, COLS), F32)
    edges = pltpu.VMEM((2, NDIR, COLS), F32)
    own_bins = pltpu.VMEM((PLANE_BINS, 8, COLS), F32)
    all_bins = pltpu.VMEM((NY_DEV + 2 * HALO, NDIR, 8, COLS), F32)
    halo = pltpu.VMEM((HALO, NDIR, 8, COLS), F32)
    packed = pltpu.VMEM((NDIR, PACKED, COLS), F32)
    out = pl.pallas_call(
        step_kernel,
        out_shape=jax.ShapeDtypeStruct((NDIR, ROWS, COLS), F32),
        in_specs=[pl.BlockSpec(memory_space=pltpu.HBM)] * 10,
        out_specs=VMEM,
        scratch_shapes=[
            pltpu.SMEM((2 * NDIR + 3 * NFREQ,), F32), pltpu.SMEM((4, NFREQ * NDIR), jnp.int32), pltpu.SMEM((NFREQ * NDIR,), F32),
            pltpu.VMEM((NDIR, ROWS, COLS), F32), field, two, two, field, field, tile,
            pltpu.VMEM((7, ROWS, COLS), F32), pltpu.VMEM((NDIR, ROWS, COLS), F32), longer, longer, edges, edges,
            tile, tile, tile, pltpu.VMEM((PACKED, COLS), jnp.int32), tile,
            packed, pltpu.VMEM((NFREQ * NDIR, 8, COLS), F32), all_bins, own_bins, own_bins, halo, halo, packed,
            pltpu.VMEM((2, 4, PACKED, COLS), F32), pltpu.VMEM((2, 3, PACKED, COLS), F32),
            pltpu.VMEM((NY_DEV, PACKED, COLS), F32), field, pltpu.SMEM((16 * PLANE_BINS,), F32),
            dma((9,)), dma((parts,)),
            dma((parts,)), dma((NY_DEV, parts)), dma((NY_DEV, parts)),
            dma((HALO, parts)), dma((HALO, parts)), dma((HALO, parts)), dma((HALO, parts)),
            dma((2, 3)), dma((2, 3)), dma((2,)), dma((2,)),
            dma((backs,)), dma((backs,)), dma((backs,)), dma((backs,)), dma((NY_DEV, backs)), dma((NY_DEV, backs)),
            dma((NY_DEV,)), dma((NY_DEV,)),
        ],
        compiler_params=pltpu.CompilerParams(vmem_limit_bytes=60 << 20, collective_id=0, has_side_effects=True),
    )(jnp.asarray(constants()), quad_table, coupling, spectrum, sea_depth, current, depth_slope, wind_forcing, wind_angle, land_sea)
    return out.reshape(1, NDIR, ROWS, COLS)


def solution(mesh):
    return jax.shard_map(
        on_device,
        mesh=mesh,
        in_specs=(
            P("spec", None, "space", None),
            P("space", None),
            P(None, "space", None),
            P(None, "space", None),
            P("space", None),
            P("space", None),
            P("space", None),
            P(),
            P(),
        ),
        out_specs=P("spec", None, "space", None),
        check_vma=False,
    )
```

```python
import jax
import jax.numpy as jnp
import numpy as np
from jax import lax
from jax.experimental import pallas as pl
from jax.experimental.pallas import tpu as pltpu
from jax.sharding import PartitionSpec as P

NFREQ, NDIR, ROWS, COLS = 32, 36, 64, 128
NY_DEV = 4
PACKED = 32
PLANES = NFREQ // NY_DEV
HALO = 3
IN_PARTS = ((0, 6), (6, 12), (18, 18))
OUT_PARTS = ((0, 16), (16, 14), (30, 6))
PLANE_BINS = NY_DEV * NDIR
F32 = jnp.float32
VMEM = pl.BlockSpec(memory_space=pltpu.VMEM)
SMEM = pl.BlockSpec(memory_space=pltpu.SMEM)
ROW_SIGN = (1, -1, 1, -1)
ROW_DIRS = ((1, 2), (-3, -4), (-1, -2), (3, 4))


def iota(shape, axis):
    return lax.broadcasted_iota(jnp.int32, shape, axis)


def sea_positions(land):
    wet = land.astype(jnp.bfloat16)
    before = (iota((COLS, COLS), 0) < iota((COLS, COLS), 1)).astype(F32).astype(jnp.bfloat16)
    rank = jnp.dot(wet, before, preferred_element_type=F32)
    count = jnp.dot(wet, jnp.ones((COLS, COLS), jnp.bfloat16), preferred_element_type=F32)
    above = (iota((ROWS, ROWS), 0) > iota((ROWS, ROWS), 1)).astype(F32).astype(jnp.bfloat16)
    start = jnp.dot(above, count.astype(jnp.bfloat16), preferred_element_type=F32)
    return start.astype(jnp.int32), rank.astype(jnp.int32), count.astype(jnp.int32)


def packing(land_ref, lane_ref, row_ref, ends_ref):
    land = land_ref[...]
    start, rank, count = sea_positions(land)
    lanes = iota((ROWS, COLS), 1)
    code = jnp.where(land > 0, lanes | ((lanes - rank) << 8), 0)
    for bit in range(7):
        moved = pltpu.roll(code, COLS - (1 << bit), 1)
        comes = ((moved >> (8 + bit)) & 1) == 1
        stays = ((code >> (8 + bit)) & 1) == 0
        code = jnp.where(comes, moved, jnp.where(stays, code, 0))
    lane_ref[...] = jnp.take_along_axis(code & 127, (lanes - start) & 127, axis=1)
    ends_ref[...] = start + count
    slots = iota((PACKED, COLS), 0) * COLS + iota((PACKED, COLS), 1)

    def count_row(r, total):
        return total + (ends_ref[pl.ds(r, 1), :] <= slots).astype(jnp.int32)

    row_ref[...] = lax.fori_loop(0, ROWS, count_row, jnp.zeros((PACKED, COLS), jnp.int32), unroll=8)


def pack(spectrum_ref, lane_ref, row_ref, packed_ref, lo, hi, sums):
    def one(d, carry):
        carry, staged = list(carry), []
        for v in range(8):
            rows = slice(8 * v, 8 * v + 8)
            staged.append(jnp.take_along_axis(spectrum_ref[d, rows, :], lane_ref[rows, :], axis=1))
        for q in range(4):
            rows = slice(8 * q, 8 * q + 8)
            source = row_ref[rows, :]
            within, block = source & 7, source >> 3
            out = jnp.zeros((8, COLS), F32)
            for v in range(q, 8):
                out = jnp.where(block == v, jnp.take_along_axis(staged[v], within, axis=0), out)
            packed_ref[d, rows, :] = out
            carry[q] = carry[q] + out
        return tuple(carry)

    return lax.fori_loop(lo, hi, one, tuple(sums))


def unpacking(land_ref, slot_row_ref, slot_lane_ref):
    start, rank, _ = sea_positions(land_ref[...])
    lanes = iota((ROWS, COLS), 1)
    slot_row_ref[...] = (start + ((lanes - start) & 127)) >> 7
    slot_lane_ref[...] = (start + rank) & 127


def unpack_block(load, slot_row, slot_lane, v):
    within, block = slot_row & 7, slot_row >> 3
    staged = jnp.take_along_axis(load(0), within, axis=0)
    for q in range(1, min(v, 3) + 1):
        staged = jnp.where(block == q, jnp.take_along_axis(load(q), within, axis=0), staged)
    return jnp.take_along_axis(staged, slot_lane, axis=1)


def transport_fields(angular, root, depth_ref, current_ref, slope_ref, forcing_ref, angle_ref, fields):
    tanh_term = jnp.tanh(angular * angular / 9.81 * depth_ref[...])
    fields[0] = (0.025 * (9.81 / 2.0)) / angular * tanh_term
    fields[1] = 0.025 * current_ref[0]
    fields[2] = 0.025 * current_ref[1]
    turning = 0.2 * (1.0 - tanh_term)
    fields[3] = turning * slope_ref[0]
    fields[4] = turning * slope_ref[1]
    wind = 0.05 * root * forcing_ref[...]
    fields[5] = wind * jnp.cos(angle_ref[...])
    fields[6] = wind * jnp.sin(angle_ref[...])


def transport(trig_ref, spectrum_ref, land_ref, fields, base, ahead, behind, edges, lo, hi):
    rows, lanes = iota((ROWS, COLS), 0), iota((ROWS, COLS), 1)

    def one(j, carry):
        cosine, sine = trig_ref[j], trig_ref[NDIR + j]
        energy = jnp.where(land_ref[...] > 0, spectrum_ref[j], 0.0)
        group = fields[0]
        along = group * cosine + fields[1]
        fx, bx = jnp.maximum(along, 0.0) * energy, jnp.minimum(along, 0.0) * energy
        across = group * sine + fields[2]
        fy, by = jnp.maximum(across, 0.0) * energy, jnp.minimum(across, 0.0) * energy
        turn = sine * fields[3] - cosine * fields[4]
        ft, bt = jnp.maximum(turn, 0.0) * energy, jnp.minimum(turn, 0.0) * energy
        edges[0, pl.ds(j, 1), :] = fx[ROWS - 1 :, :]
        edges[1, pl.ds(j, 1), :] = bx[:1, :]
        prev_x = jnp.where(rows == 0, 0.0, pltpu.roll(fx, 1, 0))
        next_x = jnp.where(rows == ROWS - 1, 0.0, pltpu.roll(bx, ROWS - 1, 0))
        prev_y = jnp.where(lanes == 0, 0.0, pltpu.roll(fy, 1, 1))
        next_y = jnp.where(lanes == COLS - 1, 0.0, pltpu.roll(by, COLS - 1, 1))
        change = (fx + next_x - (prev_x + bx)) + (fy + next_y - (prev_y + by)) + (ft - bt)
        wind = jnp.maximum(cosine * fields[5] + sine * fields[6], 0.0) * energy
        base[j] = energy - change + wind
        ahead[j + 1] = ft
        behind[j] = bt
        return carry

    lax.fori_loop(lo, hi, one, 0)


def quad_masks(table, mask_out):
    shape = (4, NFREQ * NDIR)
    row, k = iota(shape, 0), iota(shape, 1)
    freq = (k * 1821) >> 16
    direction = k - freq * NDIR
    sign = 1 - 2 * (row & 1)
    near = jnp.clip(freq + 2 * sign, 0, NFREQ - 1)
    far = jnp.clip(freq + 3 * sign, 0, NFREQ - 1)
    far = jnp.where(far == near, -NFREQ, far)
    for which in range(2):
        turn = jnp.where(row == 0, ROW_DIRS[0][which], ROW_DIRS[1][which])
        turn = jnp.where(row == 2, ROW_DIRS[2][which], jnp.where(row == 3, ROW_DIRS[3][which], turn))
        there = direction + turn
        there = jnp.where(there < 0, there + NDIR, jnp.where(there >= NDIR, there - NDIR, there))
        for step, target in enumerate((near, far)):
            mask_out[step * 2 + which] = jnp.where(table == target * NDIR + there, 1.0, 0.0).astype(F32)


def quadruplets(table_ref, coupling_ref, x, q_one, q_two, n, z):
    def one(j, carry):
        for f in range(NY_DEV):
            k = z * PLANE_BINS + f * NDIR + j
            energy = x[k]
            a, b = x[table_ref[0, k]], x[table_ref[1, k]]
            c, d = x[table_ref[2, k]], x[table_ref[3, k]]
            scaled = coupling_ref[k] * energy
            first = scaled * (energy * (a + b) - 2.0 * a * b)
            second = scaled * (energy * (c + d) - 2.0 * c * d)
            q_one[f * NDIR + j] = first
            q_two[f * NDIR + j] = second
            n[HALO + f, j] = -2.0 * (first + second)
        return carry

    lax.fori_loop(0, NDIR, one, 0)


def scatter(mask_ref, shift, q_one, q_two, n, targets, lo, hi):
    def one(j, carry):
        source = {}
        for turns in ROW_DIRS:
            for turn in turns:
                at = j - turn
                source[turn] = jnp.where(at < 0, at + NDIR, jnp.where(at >= NDIR, at - NDIR, at))
        for t in targets:
            total = n[t, j] if HALO <= t < HALO + NY_DEV else None
            for row in range(4):
                q = q_one if row < 2 else q_two
                for step in range(2):
                    f = t - HALO - ROW_SIGN[row] * (2 + step)
                    if not 0 <= f < NY_DEV:
                        continue
                    for which in range(2):
                        s = source[ROW_DIRS[row][which]]
                        term = mask_ref[step * 2 + which, row, shift + f * NDIR + s] * q[f * NDIR + s]
                        total = term if total is None else total + term
            n[t, j] = total
        return carry

    lax.fori_loop(lo, hi, one, 0)


def step_kernel(
    const_hbm, table_hbm, coupling_hbm,
    spectrum_hbm, depth_hbm, current_hbm, slope_hbm, forcing_hbm, angle_hbm, land_hbm,
    out_hbm,
    const_ref, table_ref, coupling_ref,
    spectrum_ref, depth_ref, current_ref, slope_ref, forcing_ref, angle_ref, land_ref,
    fields, base, ahead, behind, edges, edge_in, slot_row, slot_lane, lane_ref, row_ref, ends_ref,
    packed, x, n, q_one, q_two, up_in, down_in, source, sums, sums_in, column, decay, table_v, mask_v, mask_ref,
    load_sem, part_sem, mask_sem, out_sem,
    own_sem, send_y, recv_y, send_up, recv_up, send_down, recv_down, send_mean, recv_mean, send_edge, recv_edge,
    send_cup, recv_cup, send_cdown, recv_cdown, send_back, recv_back, send_col, recv_col,
):
    space, spec = lax.axis_index("space"), lax.axis_index("spec")
    z, y = spec // NY_DEV, spec % NY_DEV
    has_up, has_down = z < PLANES - 1, z > 0
    not_first, not_last = space > 0, space < 7

    def to(plane, row):
        return {"spec": plane * NY_DEV + row}

    def remote(src, dst, send, recv, device):
        return pltpu.make_async_remote_copy(
            src_ref=src, dst_ref=dst, send_sem=send, recv_sem=recv, device_id=device, device_id_type=pl.DeviceIdType.MESH
        )

    def signal(device):
        pl.semaphore_signal(barrier, inc=1, device_id=device, device_id_type=pl.DeviceIdType.MESH)

    def spectrum_load(c):
        part = pl.ds(*IN_PARTS[c])
        return pltpu.make_async_copy(spectrum_hbm.at[part], spectrum_ref.at[part], part_sem.at[c])

    pairs = (
        (land_hbm, land_ref), (const_hbm, const_ref), (depth_hbm, depth_ref), (current_hbm, current_ref),
        (slope_hbm, slope_ref), (forcing_hbm, forcing_ref), (angle_hbm, angle_ref), (table_hbm, table_ref),
        (coupling_hbm, coupling_ref), (table_hbm, table_v),
    )
    loads = [pltpu.make_async_copy(src, dst, load_sem.at[i]) for i, (src, dst) in enumerate(pairs)]
    loads[0].start()
    for c in range(len(IN_PARTS)):
        spectrum_load(c).start()
    for load in loads[1:]:
        load.start()

    barrier = pltpu.get_barrier_semaphore()
    even = space % 2 == 0
    in_spec = NY_DEV - 1 + has_up.astype(jnp.int32) + has_down.astype(jnp.int32)
    in_space = not_first.astype(jnp.int32) + not_last.astype(jnp.int32)
    for d in range(1, NY_DEV):
        signal(to(z, (y + d) % NY_DEV))

    @pl.when(has_up)
    def _():
        signal(to(z + 1, y))

    @pl.when(has_down)
    def _():
        signal(to(z - 1, y))

    def greet():
        pl.semaphore_wait(barrier, in_spec + jnp.where(even, 0, in_space))

        @pl.when(not_first)
        def _():
            signal({"space": space - 1})

        @pl.when(not_last)
        def _():
            signal({"space": space + 1})

    def bins(freq, c):
        return pl.ds(freq * NDIR + IN_PARTS[c][0], IN_PARTS[c][1])

    def eight(row):
        return pl.ds(pl.multiple_of(row * 8, 8), 8)

    def at(f, c):
        return x.at[bins(z * NY_DEV + f, c)]

    def along_y(d, c):
        row = (y + d) % NY_DEV
        src = packed.at[pl.ds(*IN_PARTS[c]), eight(row), :]
        return remote(src, at(y, c), send_y.at[d, c], recv_y.at[y, c], to(z, row))

    def from_y(d, c):
        f = (y + d) % NY_DEV
        return remote(at(f, c), at(f, c), send_y.at[d, c], recv_y.at[f, c], to(z, f))

    def up(f, c, src=None):
        src = at(f, c) if src is None else src
        return remote(src, at(f, c), send_up.at[f - 1, c], recv_up.at[f - 1, c], to(z + 1, y))

    def down(f, c, src=None):
        src = at(f, c) if src is None else src
        return remote(src, at(f, c), send_down.at[f, c], recv_down.at[f, c], to(z - 1, y))

    def forward(f, c, src=None):
        @pl.when(has_up & (f >= 1))
        def _():
            up(f, c, src).start()

        @pl.when(has_down & (f < HALO))
        def _():
            down(f, c, src).start()

    def own(c):
        return pltpu.make_async_copy(packed.at[pl.ds(*IN_PARTS[c]), eight(y), :], at(y, c), own_sem.at[c])

    loads[0].wait()
    packing(land_ref, lane_ref, row_ref, ends_ref)
    for c in range(len(IN_PARTS)):
        spectrum_load(c).wait()
    for load in loads[1:]:
        load.wait()
    odd = jnp.logical_not(even)

    def send(c):
        forward(y, c, packed.at[pl.ds(*IN_PARTS[c]), eight(y), :])
        for d in (1, 3, 2):
            along_y(d, c).start()
        own(c).start()

    mine = [jnp.zeros((8, COLS), F32)] * 4
    for c, (first, number) in enumerate(IN_PARTS):
        mine = pack(spectrum_ref, lane_ref, row_ref, packed, first, first + number, mine)
        if c == 0:
            greet()

        @pl.when(even)
        def _():
            send(c)

    def across(stage, way):
        step = 1 << stage
        other = z + step if way == 0 else z - step
        there = (other < PLANES) if way == 0 else (other >= 0)
        comes = (z >= step) if way == 0 else (z + step < PLANES)
        copy = remote(
            sums.at[way, stage], sums_in.at[way, stage], send_mean.at[way, stage], recv_mean.at[way, stage], to(other, y)
        )
        return there, comes, copy

    def sums_out(stage):
        for way in range(2):
            there, _, copy = across(stage, way)

            @pl.when(there)
            def _():
                copy.start()

    def sums_come(stage):
        for way in range(2):
            _, comes, copy = across(stage, way)

            @pl.when(comes)
            def _():
                copy.wait_recv()
                sums[way, stage + 1] = sums[way, stage] + sums_in[way, stage]

            @pl.when(jnp.logical_not(comes))
            def _():
                sums[way, stage + 1] = sums[way, stage]

    for way in range(2):
        for q in range(4):
            sums[way, 0, 8 * q : 8 * q + 8, :] = mine[q]
    sums_out(0)
    def move():
        transport_fields(
            const_ref[2 * NDIR + spec], const_ref[2 * NDIR + NFREQ + spec],
            depth_ref, current_ref, slope_ref, forcing_ref, angle_ref, fields,
        )
        transport(const_ref, spectrum_ref, land_ref, fields, base, ahead, behind, edges, 0, NDIR)
        ahead[0] = ahead[NDIR]
        behind[NDIR] = behind[0]

    @pl.when(odd)
    def _():
        move()
        sums_come(0)
        sums_out(1)
        for c in range(len(IN_PARTS)):
            send(c)

    for c in range(len(IN_PARTS)):
        for d in (1, 3, 2):
            from_y(d, c).wait_recv()
            forward((y + d) % NY_DEV, c)
        own(c).wait()

    @pl.when(even)
    def _():
        sums_come(0)
        sums_out(1)

    @pl.when(odd)
    def _():
        sums_come(1)
        sums_out(2)

    quad_masks(table_v[...], mask_v)
    shift = z * (PLANE_BINS - COLS)
    masks = pltpu.make_async_copy(mask_v.at[:, :, pl.ds(pl.multiple_of(z * COLS, COLS), 2 * COLS)], mask_ref, mask_sem)
    masks.start()
    unpacking(land_ref, slot_row, slot_lane)

    @pl.when(has_down)
    def _():
        for c in range(len(IN_PARTS)):
            for f in range(1, NY_DEV):
                remote(at(f - NY_DEV, c), at(f - NY_DEV, c), send_up.at[f - 1, c], recv_up.at[f - 1, c], to(z - 1, y)).wait_recv()

    @pl.when(has_up)
    def _():
        for c in range(len(IN_PARTS)):
            for f in range(HALO):
                remote(at(NY_DEV + f, c), at(NY_DEV + f, c), send_down.at[f, c], recv_down.at[f, c], to(z + 1, y)).wait_recv()

    quadruplets(table_ref, coupling_ref, x, q_one, q_two, n, z)
    masks.wait()

    @pl.when(even)
    def _():
        sums_come(1)
        sums_out(2)

    def give_up(c):
        part = pl.ds(*OUT_PARTS[c])
        return remote(n.at[pl.ds(HALO + NY_DEV, HALO), part], up_in.at[:, part], send_cup.at[c], recv_cup.at[c], to(z + 1, y))

    def give_down(c):
        part = pl.ds(*OUT_PARTS[c])
        return remote(n.at[pl.ds(0, HALO), part], down_in.at[:, part], send_cdown.at[c], recv_cdown.at[c], to(z - 1, y))

    for c, (first, number) in enumerate(OUT_PARTS):
        scatter(mask_ref, shift, q_one, q_two, n, (0, 1, 2, 7, 8, 9), first, first + number)

        @pl.when(has_up)
        def _():
            give_up(c).start()

        @pl.when(has_down)
        def _():
            give_down(c).start()

    @pl.when(even)
    def _():
        move()

    def edge(side):
        return remote(edges.at[side], edge_in.at[side], send_edge.at[side], recv_edge.at[side],
                      {"space": space + 1 if side == 0 else space - 1})

    @pl.when(even)
    def _():
        pl.semaphore_wait(barrier, in_space)

    @pl.when(not_last)
    def _():
        edge(0).start()

    @pl.when(not_first)
    def _():
        edge(1).start()

    scatter(mask_ref, shift, q_one, q_two, n, (3, 4, 5, 6), 0, NDIR)

    @pl.when(z == 0)
    def _():
        def fold(j, carry):
            n[HALO, j] += n[0, j] + n[1, j] + n[2, j]
            return carry

        lax.fori_loop(0, NDIR, fold, 0)

    @pl.when(z == PLANES - 1)
    def _():
        def fold(j, carry):
            n[6, j] += n[7, j] + n[8, j] + n[9, j]
            return carry

        lax.fori_loop(0, NDIR, fold, 0)

    for side, there in ((0, not_first), (1, not_last)):
        @pl.when(there)
        def _():
            remote(edges.at[side], edge_in.at[side], send_edge.at[side], recv_edge.at[side],
                   {"space": space - 1 if side == 0 else space + 1}).wait_recv()

        @pl.when(jnp.logical_not(there))
        def _():
            edge_in[side] = jnp.zeros((NDIR, COLS), F32)

    def back(d, c):
        f = (y + d) % NY_DEV
        part = pl.ds(*OUT_PARTS[c])
        return remote(n.at[HALO + f, part], source.at[part, eight(y), :], send_back.at[d, c], recv_back.at[y, c], to(z, f))

    def finish(j, carry):
        base[j, 0:1, :] += edge_in[0, pl.ds(j, 1), :]
        base[j, ROWS - 1 :, :] -= edge_in[1, pl.ds(j, 1), :]
        for v in range(8):
            rows = slice(8 * v, 8 * v + 8)
            added = unpack_block(lambda q: source[j, 8 * q : 8 * q + 8, :], slot_row[rows, :], slot_lane[rows, :], v)
            moved = base[j, rows, :] + ahead[j, rows, :] - behind[j + 1, rows, :]
            moved = moved - decay[rows, :] * spectrum_ref[j, rows, :]
            base[j, rows, :] = jnp.where(land_ref[rows, :] > 0, moved + added, 0.0)
        return carry

    def complete(c):
        first, number = OUT_PARTS[c]
        part = pl.ds(first, number)

        @pl.when(has_down)
        def _():
            remote(n.at[pl.ds(HALO + NY_DEV, HALO), part], up_in.at[:, part], send_cup.at[c], recv_cup.at[c], to(z - 1, y)).wait_recv()

            def add(j, carry):
                for f in range(HALO):
                    n[HALO + f, j] += up_in[f, j]
                return carry

            lax.fori_loop(first, first + number, add, 0)

        @pl.when(has_up)
        def _():
            remote(n.at[pl.ds(0, HALO), part], down_in.at[:, part], send_cdown.at[c], recv_cdown.at[c], to(z + 1, y)).wait_recv()

            def add(j, carry):
                for f in range(1, NY_DEV):
                    n[HALO + f, j] += down_in[f - 1, j]
                return carry

            lax.fori_loop(first, first + number, add, 0)

        for d in (2, 1, 3):
            back(d, c).start()

        def keep(j, carry):
            source[j, eight(y), :] = n[HALO + y, j]
            return carry

        lax.fori_loop(first, first + number, keep, 0)

    def result(c):
        part = pl.ds(*OUT_PARTS[c])
        return pltpu.make_async_copy(base.at[part], out_hbm.at[part], out_sem.at[c])

    def conclude(c):
        first, number = OUT_PARTS[c]
        for d in (1, 3, 2):
            f = (y + d) % NY_DEV
            at_source = source.at[pl.ds(first, number), eight(f), :]
            remote(n.at[HALO, pl.ds(first, number)], at_source, send_back.at[d, c], recv_back.at[f, c], to(z, f)).wait_recv()
        lax.fori_loop(first, first + number, finish, 0)
        result(c).start()

    complete(0)
    sums_come(2)
    column[y] = sums[0, 3] + sums[1, 3] - sums[0, 0]

    def to_columns(d):
        return remote(column.at[y], column.at[y], send_col.at[d], recv_col.at[y], to(z, (y + d) % NY_DEV))

    for d in (2, 1, 3):
        to_columns(d).start()

    complete(1)
    for d in (1, 3, 2):
        f = (y + d) % NY_DEV
        remote(column.at[f], column.at[f], send_col.at[d], recv_col.at[f], to(z, f)).wait_recv()
    mean = (column[0] + column[1] + column[2] + column[3]) * (1.0 / (NFREQ * NDIR))
    sums[0, 3] = mean * mean
    rate = const_ref[2 * NDIR + 2 * NFREQ + spec]
    for v in range(8):
        rows = slice(8 * v, 8 * v + 8)
        square = unpack_block(lambda q: sums[0, 3, 8 * q : 8 * q + 8, :], slot_row[rows, :], slot_lane[rows, :], v)
        decay[rows, :] = rate * square
    conclude(0)
    for c in range(2, len(OUT_PARTS)):
        complete(c)
        conclude(c - 1)
    conclude(len(OUT_PARTS) - 1)

    for c in range(len(IN_PARTS)):
        for d in range(1, NY_DEV):
            along_y(d, c).wait_send()

    @pl.when(has_up)
    def _():
        for c in range(len(IN_PARTS)):
            for f in range(1, NY_DEV):
                up(f, c).wait_send()
        for c in range(len(OUT_PARTS)):
            give_up(c).wait_send()

    @pl.when(has_down)
    def _():
        for c in range(len(IN_PARTS)):
            for f in range(HALO):
                down(f, c).wait_send()
        for c in range(len(OUT_PARTS)):
            give_down(c).wait_send()

    for stage in range(3):
        for way in range(2):
            there, _, copy = across(stage, way)

            @pl.when(there)
            def _():
                copy.wait_send()

    for d in range(1, NY_DEV):
        to_columns(d).wait_send()
        for c in range(len(OUT_PARTS)):
            back(d, c).wait_send()
    for c in range(len(OUT_PARTS)):
        result(c).wait()

    @pl.when(not_last)
    def _():
        edge(0).wait_send()

    @pl.when(not_first)
    def _():
        edge(1).wait_send()


def constants():
    heading = np.float32(2.0 * np.pi / NDIR) * np.arange(NDIR, dtype=np.float32)
    growth = 1.1 ** np.arange(NFREQ)
    parts = [np.cos(heading), np.sin(heading), 2.0 * np.pi * 0.04 * growth, np.sqrt(growth), 0.3 * (growth / growth[-1]) ** 2]
    return np.concatenate(parts).astype(np.float32)


def on_device(spectrum, sea_depth, current, depth_slope, wind_forcing, wind_angle, land_sea, quad_table, coupling):
    spectrum = spectrum.reshape(NDIR, ROWS, COLS)
    dma, parts, backs = pltpu.SemaphoreType.DMA, len(IN_PARTS), len(OUT_PARTS)
    tile, field, two = pltpu.VMEM((ROWS, COLS), jnp.int32), pltpu.VMEM((ROWS, COLS), F32), pltpu.VMEM((2, ROWS, COLS), F32)
    longer = pltpu.VMEM((NDIR + 1, ROWS, COLS), F32)
    edges = pltpu.VMEM((2, NDIR, COLS), F32)
    own_bins = pltpu.VMEM((PLANE_BINS, 8, COLS), F32)
    all_bins = pltpu.VMEM((NY_DEV + 2 * HALO, NDIR, 8, COLS), F32)
    halo = pltpu.VMEM((HALO, NDIR, 8, COLS), F32)
    packed = pltpu.VMEM((NDIR, PACKED, COLS), F32)
    out = pl.pallas_call(
        step_kernel,
        out_shape=jax.ShapeDtypeStruct((NDIR, ROWS, COLS), F32),
        in_specs=[pl.BlockSpec(memory_space=pltpu.HBM)] * 10,
        out_specs=pl.BlockSpec(memory_space=pltpu.HBM),
        scratch_shapes=[
            pltpu.SMEM((2 * NDIR + 3 * NFREQ,), F32), pltpu.SMEM((4, NFREQ * NDIR), jnp.int32), pltpu.SMEM((NFREQ * NDIR,), F32),
            pltpu.VMEM((NDIR, ROWS, COLS), F32), field, two, two, field, field, tile,
            pltpu.VMEM((7, ROWS, COLS), F32), pltpu.VMEM((NDIR, ROWS, COLS), F32), longer, longer, edges, edges,
            tile, tile, tile, pltpu.VMEM((PACKED, COLS), jnp.int32), tile,
            packed, pltpu.VMEM((NFREQ * NDIR, 8, COLS), F32), all_bins, own_bins, own_bins, halo, halo, packed,
            pltpu.VMEM((2, 4, PACKED, COLS), F32), pltpu.VMEM((2, 3, PACKED, COLS), F32),
            pltpu.VMEM((NY_DEV, PACKED, COLS), F32), field,
            pltpu.VMEM((4, NFREQ * NDIR), jnp.int32), pltpu.VMEM((4, 4, NFREQ * NDIR), F32), pltpu.SMEM((4, 4, 2 * COLS), F32),
            dma((10,)), dma((parts,)), dma, dma((backs,)),
            dma((parts,)), dma((NY_DEV, parts)), dma((NY_DEV, parts)),
            dma((HALO, parts)), dma((HALO, parts)), dma((HALO, parts)), dma((HALO, parts)),
            dma((2, 3)), dma((2, 3)), dma((2,)), dma((2,)),
            dma((backs,)), dma((backs,)), dma((backs,)), dma((backs,)), dma((NY_DEV, backs)), dma((NY_DEV, backs)),
            dma((NY_DEV,)), dma((NY_DEV,)),
        ],
        compiler_params=pltpu.CompilerParams(vmem_limit_bytes=60 << 20, collective_id=0, has_side_effects=True),
    )(jnp.asarray(constants()), quad_table, coupling, spectrum, sea_depth, current, depth_slope, wind_forcing, wind_angle, land_sea)
    return out.reshape(1, NDIR, ROWS, COLS)


def solution(mesh):
    return jax.shard_map(
        on_device,
        mesh=mesh,
        in_specs=(
            P("spec", None, "space", None),
            P("space", None),
            P(None, "space", None),
            P(None, "space", None),
            P("space", None),
            P("space", None),
            P("space", None),
            P(),
            P(),
        ),
        out_specs=P("spec", None, "space", None),
        check_vma=False,
    )
```

```python
import jax
import jax.numpy as jnp
import numpy as np
from jax import lax
from jax.experimental import pallas as pl
from jax.experimental.pallas import tpu as pltpu
from jax.sharding import PartitionSpec as P

NFREQ, NDIR, ROWS, COLS = 32, 36, 64, 128
NY_DEV = 4
PACKED = 32
PLANES = NFREQ // NY_DEV
HALO = 3
IN_PARTS = ((0, 12), (12, 12), (24, 12))
OUT_PARTS = ((0, 18), (18, 18))
PLANE_BINS = NY_DEV * NDIR
F32 = jnp.float32
VMEM = pl.BlockSpec(memory_space=pltpu.VMEM)
SMEM = pl.BlockSpec(memory_space=pltpu.SMEM)
ROW_SIGN = (1, -1, 1, -1)
ROW_DIRS = ((1, 2), (-3, -4), (-1, -2), (3, 4))


def iota(shape, axis):
    return lax.broadcasted_iota(jnp.int32, shape, axis)


def sea_positions(land):
    wet = land.astype(jnp.bfloat16)
    before = (iota((COLS, COLS), 0) < iota((COLS, COLS), 1)).astype(F32).astype(jnp.bfloat16)
    rank = jnp.dot(wet, before, preferred_element_type=F32)
    count = jnp.dot(wet, jnp.ones((COLS, COLS), jnp.bfloat16), preferred_element_type=F32)
    above = (iota((ROWS, ROWS), 0) > iota((ROWS, ROWS), 1)).astype(F32).astype(jnp.bfloat16)
    start = jnp.dot(above, count.astype(jnp.bfloat16), preferred_element_type=F32)
    return start.astype(jnp.int32), rank.astype(jnp.int32), count.astype(jnp.int32)


def packing(land_ref, lane_ref, row_ref, ends_ref):
    land = land_ref[...]
    start, rank, count = sea_positions(land)
    lanes = iota((ROWS, COLS), 1)
    code = jnp.where(land > 0, lanes | ((lanes - rank) << 8), 0)
    for bit in range(7):
        moved = pltpu.roll(code, COLS - (1 << bit), 1)
        comes = ((moved >> (8 + bit)) & 1) == 1
        stays = ((code >> (8 + bit)) & 1) == 0
        code = jnp.where(comes, moved, jnp.where(stays, code, 0))
    lane_ref[...] = jnp.take_along_axis(code & 127, (lanes - start) & 127, axis=1)
    ends_ref[...] = start + count
    slots = iota((PACKED, COLS), 0) * COLS + iota((PACKED, COLS), 1)

    def count_row(r, total):
        return total + (ends_ref[pl.ds(r, 1), :] <= slots).astype(jnp.int32)

    row_ref[...] = lax.fori_loop(0, ROWS, count_row, jnp.zeros((PACKED, COLS), jnp.int32), unroll=8)


def pack(spectrum_ref, lane_ref, row_ref, packed_ref, lo, hi, sums):
    def one(d, carry):
        carry, staged = list(carry), []
        for v in range(8):
            rows = slice(8 * v, 8 * v + 8)
            staged.append(jnp.take_along_axis(spectrum_ref[d, rows, :], lane_ref[rows, :], axis=1))
        for q in range(4):
            rows = slice(8 * q, 8 * q + 8)
            source = row_ref[rows, :]
            within, block = source & 7, source >> 3
            out = jnp.zeros((8, COLS), F32)
            for v in range(q, 8):
                out = jnp.where(block == v, jnp.take_along_axis(staged[v], within, axis=0), out)
            packed_ref[d, rows, :] = out
            carry[q] = carry[q] + out
        return tuple(carry)

    return lax.fori_loop(lo, hi, one, tuple(sums), unroll=6)


def unpacking(land_ref, slot_row_ref, slot_lane_ref):
    start, rank, _ = sea_positions(land_ref[...])
    lanes = iota((ROWS, COLS), 1)
    slot_row_ref[...] = (start + ((lanes - start) & 127)) >> 7
    slot_lane_ref[...] = (start + rank) & 127


def unpack_block(load, slot_row, slot_lane, v):
    within, block = slot_row & 7, slot_row >> 3
    staged = jnp.take_along_axis(load(0), within, axis=0)
    for q in range(1, min(v, 3) + 1):
        staged = jnp.where(block == q, jnp.take_along_axis(load(q), within, axis=0), staged)
    return jnp.take_along_axis(staged, slot_lane, axis=1)


def transport_fields(angular, root, depth_ref, current_ref, slope_ref, forcing_ref, angle_ref, fields):
    tanh_term = jnp.tanh(angular * angular / 9.81 * depth_ref[...])
    fields[0] = (0.025 * (9.81 / 2.0)) / angular * tanh_term
    fields[1] = 0.025 * current_ref[0]
    fields[2] = 0.025 * current_ref[1]
    turning = 0.2 * (1.0 - tanh_term)
    fields[3] = turning * slope_ref[0]
    fields[4] = turning * slope_ref[1]
    wind = 0.05 * root * forcing_ref[...]
    fields[5] = wind * jnp.cos(angle_ref[...])
    fields[6] = wind * jnp.sin(angle_ref[...])


def transport(trig_ref, spectrum_ref, land_ref, fields, base, ahead, behind, edges, lo, hi):
    rows, lanes = iota((ROWS, COLS), 0), iota((ROWS, COLS), 1)

    def one(j, carry):
        cosine, sine = trig_ref[j], trig_ref[NDIR + j]
        energy = jnp.where(land_ref[...] > 0, spectrum_ref[j], 0.0)
        group = fields[0]
        along = group * cosine + fields[1]
        fx, bx = jnp.maximum(along, 0.0) * energy, jnp.minimum(along, 0.0) * energy
        across = group * sine + fields[2]
        fy, by = jnp.maximum(across, 0.0) * energy, jnp.minimum(across, 0.0) * energy
        turn = sine * fields[3] - cosine * fields[4]
        ft, bt = jnp.maximum(turn, 0.0) * energy, jnp.minimum(turn, 0.0) * energy
        edges[0, pl.ds(j, 1), :] = fx[ROWS - 1 :, :]
        edges[1, pl.ds(j, 1), :] = bx[:1, :]
        prev_x = jnp.where(rows == 0, 0.0, pltpu.roll(fx, 1, 0))
        next_x = jnp.where(rows == ROWS - 1, 0.0, pltpu.roll(bx, ROWS - 1, 0))
        prev_y = jnp.where(lanes == 0, 0.0, pltpu.roll(fy, 1, 1))
        next_y = jnp.where(lanes == COLS - 1, 0.0, pltpu.roll(by, COLS - 1, 1))
        change = (fx + next_x - (prev_x + bx)) + (fy + next_y - (prev_y + by)) + (ft - bt)
        wind = jnp.maximum(cosine * fields[5] + sine * fields[6], 0.0) * energy
        base[j] = energy - change + wind
        ahead[j + 1] = ft
        behind[j] = bt
        return carry

    lax.fori_loop(lo, hi, one, 0, unroll=4)


def quad_masks(table, mask_out):
    shape = (4, NFREQ * NDIR)
    row, k = iota(shape, 0), iota(shape, 1)
    freq = (k * 1821) >> 16
    direction = k - freq * NDIR
    sign = 1 - 2 * (row & 1)
    near = jnp.clip(freq + 2 * sign, 0, NFREQ - 1)
    far = jnp.clip(freq + 3 * sign, 0, NFREQ - 1)
    far = jnp.where(far == near, -NFREQ, far)
    for which in range(2):
        turn = jnp.where(row == 0, ROW_DIRS[0][which], ROW_DIRS[1][which])
        turn = jnp.where(row == 2, ROW_DIRS[2][which], jnp.where(row == 3, ROW_DIRS[3][which], turn))
        there = direction + turn
        there = jnp.where(there < 0, there + NDIR, jnp.where(there >= NDIR, there - NDIR, there))
        for step, target in enumerate((near, far)):
            mask_out[step * 2 + which] = jnp.where(table == target * NDIR + there, 1.0, 0.0).astype(F32)


def quadruplets(table_ref, coupling_ref, x, q_one, q_two, n, z):
    def one(j, carry):
        for f in range(NY_DEV):
            k = z * PLANE_BINS + f * NDIR + j
            energy = x[k]
            a, b = x[table_ref[0, k]], x[table_ref[1, k]]
            c, d = x[table_ref[2, k]], x[table_ref[3, k]]
            scaled = coupling_ref[k] * energy
            first = scaled * (energy * (a + b) - 2.0 * a * b)
            second = scaled * (energy * (c + d) - 2.0 * c * d)
            q_one[f * NDIR + j] = first
            q_two[f * NDIR + j] = second
            n[HALO + f, j] = -2.0 * (first + second)
        return carry

    lax.fori_loop(0, NDIR, one, 0, unroll=4)


def scatter(mask_ref, shift, q_one, q_two, n, targets, lo, hi):
    def one(j, carry):
        source = {}
        for turns in ROW_DIRS:
            for turn in turns:
                at = j - turn
                source[turn] = jnp.where(at < 0, at + NDIR, jnp.where(at >= NDIR, at - NDIR, at))
        for t in targets:
            total = n[t, j] if HALO <= t < HALO + NY_DEV else None
            for row in range(4):
                q = q_one if row < 2 else q_two
                for step in range(2):
                    f = t - HALO - ROW_SIGN[row] * (2 + step)
                    if not 0 <= f < NY_DEV:
                        continue
                    for which in range(2):
                        s = source[ROW_DIRS[row][which]]
                        term = mask_ref[step * 2 + which, row, shift + f * NDIR + s] * q[f * NDIR + s]
                        total = term if total is None else total + term
            n[t, j] = total
        return carry

    lax.fori_loop(lo, hi, one, 0, unroll=3)


def step_kernel(
    const_hbm, table_hbm, coupling_hbm,
    spectrum_hbm, depth_hbm, current_hbm, slope_hbm, forcing_hbm, angle_hbm, land_hbm,
    out_hbm,
    const_ref, table_ref, coupling_ref,
    spectrum_ref, depth_ref, current_ref, slope_ref, forcing_ref, angle_ref, land_ref,
    fields, base, ahead, behind, edges, edge_in, slot_row, slot_lane, lane_ref, row_ref, ends_ref,
    packed, x, n, q_one, q_two, up_in, down_in, source, sums, sums_in, column, decay, table_v, mask_v, mask_ref,
    load_sem, part_sem, mask_sem, out_sem,
    own_sem, send_y, recv_y, send_up, recv_up, send_down, recv_down, send_mean, recv_mean, send_edge, recv_edge,
    send_cup, recv_cup, send_cdown, recv_cdown, send_back, recv_back, send_col, recv_col,
):
    space, spec = lax.axis_index("space"), lax.axis_index("spec")
    z, y = spec // NY_DEV, spec % NY_DEV
    has_up, has_down = z < PLANES - 1, z > 0
    not_first, not_last = space > 0, space < 7

    def to(plane, row):
        return {"spec": plane * NY_DEV + row}

    def remote(src, dst, send, recv, device):
        return pltpu.make_async_remote_copy(
            src_ref=src, dst_ref=dst, send_sem=send, recv_sem=recv, device_id=device, device_id_type=pl.DeviceIdType.MESH
        )

    def signal(device):
        pl.semaphore_signal(barrier, inc=1, device_id=device, device_id_type=pl.DeviceIdType.MESH)

    def spectrum_load(c):
        part = pl.ds(*IN_PARTS[c])
        return pltpu.make_async_copy(spectrum_hbm.at[part], spectrum_ref.at[part], part_sem.at[c])

    pairs = (
        (land_hbm, land_ref), (const_hbm, const_ref), (depth_hbm, depth_ref), (current_hbm, current_ref),
        (slope_hbm, slope_ref), (forcing_hbm, forcing_ref), (angle_hbm, angle_ref), (table_hbm, table_ref),
        (coupling_hbm, coupling_ref), (table_hbm, table_v),
    )
    loads = [pltpu.make_async_copy(src, dst, load_sem.at[i]) for i, (src, dst) in enumerate(pairs)]
    loads[0].start()
    for c in range(len(IN_PARTS)):
        spectrum_load(c).start()
    for load in loads[1:]:
        load.start()

    barrier = pltpu.get_barrier_semaphore()
    leads = space % 2 == 1
    follows = jnp.logical_not(leads)
    in_spec = NY_DEV - 1 + has_up.astype(jnp.int32) + has_down.astype(jnp.int32)
    in_space = not_first.astype(jnp.int32) + not_last.astype(jnp.int32)
    for d in range(1, NY_DEV):
        signal(to(z, (y + d) % NY_DEV))

    @pl.when(has_up)
    def _():
        signal(to(z + 1, y))

    @pl.when(has_down)
    def _():
        signal(to(z - 1, y))

    def greet():
        pl.semaphore_wait(barrier, in_spec + jnp.where(leads, 0, in_space))

        @pl.when(not_first)
        def _():
            signal({"space": space - 1})

        @pl.when(not_last)
        def _():
            signal({"space": space + 1})

    def bins(freq, c):
        return pl.ds(freq * NDIR + IN_PARTS[c][0], IN_PARTS[c][1])

    def eight(row):
        return pl.ds(pl.multiple_of(row * 8, 8), 8)

    def at(f, c):
        return x.at[bins(z * NY_DEV + f, c)]

    def along_y(d, c):
        row = (y + d) % NY_DEV
        src = packed.at[pl.ds(*IN_PARTS[c]), eight(row), :]
        return remote(src, at(y, c), send_y.at[d, c], recv_y.at[y, c], to(z, row))

    def from_y(d, c):
        f = (y + d) % NY_DEV
        return remote(at(f, c), at(f, c), send_y.at[d, c], recv_y.at[f, c], to(z, f))

    def up(f, c, src=None):
        src = at(f, c) if src is None else src
        return remote(src, at(f, c), send_up.at[f - 1, c], recv_up.at[f - 1, c], to(z + 1, y))

    def down(f, c, src=None):
        src = at(f, c) if src is None else src
        return remote(src, at(f, c), send_down.at[f, c], recv_down.at[f, c], to(z - 1, y))

    def forward(f, c, src=None):
        @pl.when(has_up & (f >= 1))
        def _():
            up(f, c, src).start()

        @pl.when(has_down & (f < HALO))
        def _():
            down(f, c, src).start()

    def own(c):
        return pltpu.make_async_copy(packed.at[pl.ds(*IN_PARTS[c]), eight(y), :], at(y, c), own_sem.at[c])

    loads[0].wait()
    packing(land_ref, lane_ref, row_ref, ends_ref)
    for c in range(len(IN_PARTS)):
        spectrum_load(c).wait()
    for load in loads[1:]:
        load.wait()

    def send(c):
        forward(y, c, packed.at[pl.ds(*IN_PARTS[c]), eight(y), :])
        for d in (1, 3, 2):
            along_y(d, c).start()
        own(c).start()

    mine = [jnp.zeros((8, COLS), F32)] * 4
    for c, (first, number) in enumerate(IN_PARTS):
        mine = pack(spectrum_ref, lane_ref, row_ref, packed, first, first + number, mine)
        if c == 0:
            greet()

        @pl.when(leads)
        def _():
            send(c)

    def across(stage, way):
        step = 1 << stage
        other = z + step if way == 0 else z - step
        there = (other < PLANES) if way == 0 else (other >= 0)
        comes = (z >= step) if way == 0 else (z + step < PLANES)
        copy = remote(
            sums.at[way, stage], sums_in.at[way, stage], send_mean.at[way, stage], recv_mean.at[way, stage], to(other, y)
        )
        return there, comes, copy

    def sums_out(stage):
        for way in range(2):
            there, _, copy = across(stage, way)

            @pl.when(there)
            def _():
                copy.start()

    def sums_come(stage):
        for way in range(2):
            _, comes, copy = across(stage, way)

            @pl.when(comes)
            def _():
                copy.wait_recv()
                sums[way, stage + 1] = sums[way, stage] + sums_in[way, stage]

            @pl.when(jnp.logical_not(comes))
            def _():
                sums[way, stage + 1] = sums[way, stage]

    for way in range(2):
        for q in range(4):
            sums[way, 0, 8 * q : 8 * q + 8, :] = mine[q]
    sums_out(0)
    def move():
        transport_fields(
            const_ref[2 * NDIR + spec], const_ref[2 * NDIR + NFREQ + spec],
            depth_ref, current_ref, slope_ref, forcing_ref, angle_ref, fields,
        )
        transport(const_ref, spectrum_ref, land_ref, fields, base, ahead, behind, edges, 0, NDIR)
        ahead[0] = ahead[NDIR]
        behind[NDIR] = behind[0]

    @pl.when(follows)
    def _():
        move()
        sums_come(0)
        sums_out(1)
        for c in range(len(IN_PARTS)):
            send(c)

    for c in range(len(IN_PARTS)):
        for d in (1, 3, 2):
            from_y(d, c).wait_recv()
            forward((y + d) % NY_DEV, c)
        own(c).wait()

    @pl.when(leads)
    def _():
        sums_come(0)
        sums_out(1)

    @pl.when(follows)
    def _():
        sums_come(1)
        sums_out(2)

    quad_masks(table_v[...], mask_v)
    shift = z * (PLANE_BINS - COLS)
    masks = pltpu.make_async_copy(mask_v.at[:, :, pl.ds(pl.multiple_of(z * COLS, COLS), 2 * COLS)], mask_ref, mask_sem)
    masks.start()
    unpacking(land_ref, slot_row, slot_lane)

    @pl.when(has_down)
    def _():
        for c in range(len(IN_PARTS)):
            for f in range(1, NY_DEV):
                remote(at(f - NY_DEV, c), at(f - NY_DEV, c), send_up.at[f - 1, c], recv_up.at[f - 1, c], to(z - 1, y)).wait_recv()

    @pl.when(has_up)
    def _():
        for c in range(len(IN_PARTS)):
            for f in range(HALO):
                remote(at(NY_DEV + f, c), at(NY_DEV + f, c), send_down.at[f, c], recv_down.at[f, c], to(z + 1, y)).wait_recv()

    quadruplets(table_ref, coupling_ref, x, q_one, q_two, n, z)
    masks.wait()

    @pl.when(leads)
    def _():
        sums_come(1)
        sums_out(2)

    def give_up(c):
        part = pl.ds(*OUT_PARTS[c])
        return remote(n.at[pl.ds(HALO + NY_DEV, HALO), part], up_in.at[:, part], send_cup.at[c], recv_cup.at[c], to(z + 1, y))

    def give_down(c):
        part = pl.ds(*OUT_PARTS[c])
        return remote(n.at[pl.ds(0, HALO), part], down_in.at[:, part], send_cdown.at[c], recv_cdown.at[c], to(z - 1, y))

    for c, (first, number) in enumerate(OUT_PARTS):
        scatter(mask_ref, shift, q_one, q_two, n, (0, 1, 2, 7, 8, 9), first, first + number)

        @pl.when(has_up)
        def _():
            give_up(c).start()

        @pl.when(has_down)
        def _():
            give_down(c).start()

    @pl.when(leads)
    def _():
        move()

    def edge(side):
        return remote(edges.at[side], edge_in.at[side], send_edge.at[side], recv_edge.at[side],
                      {"space": space + 1 if side == 0 else space - 1})

    @pl.when(leads)
    def _():
        pl.semaphore_wait(barrier, in_space)

    @pl.when(not_last)
    def _():
        edge(0).start()

    @pl.when(not_first)
    def _():
        edge(1).start()

    scatter(mask_ref, shift, q_one, q_two, n, (3, 4, 5, 6), 0, NDIR)

    @pl.when(z == 0)
    def _():
        def fold(j, carry):
            n[HALO, j] += n[0, j] + n[1, j] + n[2, j]
            return carry

        lax.fori_loop(0, NDIR, fold, 0)

    @pl.when(z == PLANES - 1)
    def _():
        def fold(j, carry):
            n[6, j] += n[7, j] + n[8, j] + n[9, j]
            return carry

        lax.fori_loop(0, NDIR, fold, 0)

    for side, there in ((0, not_first), (1, not_last)):
        @pl.when(there)
        def _():
            remote(edges.at[side], edge_in.at[side], send_edge.at[side], recv_edge.at[side],
                   {"space": space - 1 if side == 0 else space + 1}).wait_recv()

        @pl.when(jnp.logical_not(there))
        def _():
            edge_in[side] = jnp.zeros((NDIR, COLS), F32)

    def back(d, c):
        f = (y + d) % NY_DEV
        part = pl.ds(*OUT_PARTS[c])
        return remote(n.at[HALO + f, part], source.at[part, eight(y), :], send_back.at[d, c], recv_back.at[y, c], to(z, f))

    def finish(j, carry):
        base[j, 0:1, :] += edge_in[0, pl.ds(j, 1), :]
        base[j, ROWS - 1 :, :] -= edge_in[1, pl.ds(j, 1), :]
        for v in range(8):
            rows = slice(8 * v, 8 * v + 8)
            added = unpack_block(lambda q: source[j, 8 * q : 8 * q + 8, :], slot_row[rows, :], slot_lane[rows, :], v)
            moved = base[j, rows, :] + ahead[j, rows, :] - behind[j + 1, rows, :]
            moved = moved - decay[rows, :] * spectrum_ref[j, rows, :]
            base[j, rows, :] = jnp.where(land_ref[rows, :] > 0, moved + added, 0.0)
        return carry

    def complete(c):
        first, number = OUT_PARTS[c]
        part = pl.ds(first, number)

        @pl.when(has_down)
        def _():
            remote(n.at[pl.ds(HALO + NY_DEV, HALO), part], up_in.at[:, part], send_cup.at[c], recv_cup.at[c], to(z - 1, y)).wait_recv()

            def add(j, carry):
                for f in range(HALO):
                    n[HALO + f, j] += up_in[f, j]
                return carry

            lax.fori_loop(first, first + number, add, 0, unroll=2)

        @pl.when(has_up)
        def _():
            remote(n.at[pl.ds(0, HALO), part], down_in.at[:, part], send_cdown.at[c], recv_cdown.at[c], to(z + 1, y)).wait_recv()

            def add(j, carry):
                for f in range(1, NY_DEV):
                    n[HALO + f, j] += down_in[f - 1, j]
                return carry

            lax.fori_loop(first, first + number, add, 0, unroll=2)

        for d in (2, 1, 3):
            back(d, c).start()

        def keep(j, carry):
            source[j, eight(y), :] = n[HALO + y, j]
            return carry

        lax.fori_loop(first, first + number, keep, 0, unroll=2)

    def result(c):
        part = pl.ds(*OUT_PARTS[c])
        return pltpu.make_async_copy(base.at[part], out_hbm.at[part], out_sem.at[c])

    def conclude(c):
        first, number = OUT_PARTS[c]
        for d in (1, 3, 2):
            f = (y + d) % NY_DEV
            at_source = source.at[pl.ds(first, number), eight(f), :]
            remote(n.at[HALO, pl.ds(first, number)], at_source, send_back.at[d, c], recv_back.at[f, c], to(z, f)).wait_recv()
        lax.fori_loop(first, first + number, finish, 0, unroll=6)
        result(c).start()

    complete(0)
    sums_come(2)
    column[y] = sums[0, 3] + sums[1, 3] - sums[0, 0]

    def to_columns(d):
        return remote(column.at[y], column.at[y], send_col.at[d], recv_col.at[y], to(z, (y + d) % NY_DEV))

    for d in (2, 1, 3):
        to_columns(d).start()

    complete(1)
    for d in (1, 3, 2):
        f = (y + d) % NY_DEV
        remote(column.at[f], column.at[f], send_col.at[d], recv_col.at[f], to(z, f)).wait_recv()
    mean = (column[0] + column[1] + column[2] + column[3]) * (1.0 / (NFREQ * NDIR))
    sums[0, 3] = mean * mean
    rate = const_ref[2 * NDIR + 2 * NFREQ + spec]
    for v in range(8):
        rows = slice(8 * v, 8 * v + 8)
        square = unpack_block(lambda q: sums[0, 3, 8 * q : 8 * q + 8, :], slot_row[rows, :], slot_lane[rows, :], v)
        decay[rows, :] = rate * square
    conclude(0)
    for c in range(2, len(OUT_PARTS)):
        complete(c)
        conclude(c - 1)
    conclude(len(OUT_PARTS) - 1)

    for c in range(len(IN_PARTS)):
        for d in range(1, NY_DEV):
            along_y(d, c).wait_send()

    @pl.when(has_up)
    def _():
        for c in range(len(IN_PARTS)):
            for f in range(1, NY_DEV):
                up(f, c).wait_send()
        for c in range(len(OUT_PARTS)):
            give_up(c).wait_send()

    @pl.when(has_down)
    def _():
        for c in range(len(IN_PARTS)):
            for f in range(HALO):
                down(f, c).wait_send()
        for c in range(len(OUT_PARTS)):
            give_down(c).wait_send()

    for stage in range(3):
        for way in range(2):
            there, _, copy = across(stage, way)

            @pl.when(there)
            def _():
                copy.wait_send()

    for d in range(1, NY_DEV):
        to_columns(d).wait_send()
        for c in range(len(OUT_PARTS)):
            back(d, c).wait_send()
    for c in range(len(OUT_PARTS)):
        result(c).wait()

    @pl.when(not_last)
    def _():
        edge(0).wait_send()

    @pl.when(not_first)
    def _():
        edge(1).wait_send()


def constants():
    heading = np.float32(2.0 * np.pi / NDIR) * np.arange(NDIR, dtype=np.float32)
    growth = 1.1 ** np.arange(NFREQ)
    parts = [np.cos(heading), np.sin(heading), 2.0 * np.pi * 0.04 * growth, np.sqrt(growth), 0.3 * (growth / growth[-1]) ** 2]
    return np.concatenate(parts).astype(np.float32)


def on_device(spectrum, sea_depth, current, depth_slope, wind_forcing, wind_angle, land_sea, quad_table, coupling):
    spectrum = spectrum.reshape(NDIR, ROWS, COLS)
    dma, parts, backs = pltpu.SemaphoreType.DMA, len(IN_PARTS), len(OUT_PARTS)
    tile, field, two = pltpu.VMEM((ROWS, COLS), jnp.int32), pltpu.VMEM((ROWS, COLS), F32), pltpu.VMEM((2, ROWS, COLS), F32)
    longer = pltpu.VMEM((NDIR + 1, ROWS, COLS), F32)
    edges = pltpu.VMEM((2, NDIR, COLS), F32)
    own_bins = pltpu.VMEM((PLANE_BINS, 8, COLS), F32)
    all_bins = pltpu.VMEM((NY_DEV + 2 * HALO, NDIR, 8, COLS), F32)
    halo = pltpu.VMEM((HALO, NDIR, 8, COLS), F32)
    packed = pltpu.VMEM((NDIR, PACKED, COLS), F32)
    out = pl.pallas_call(
        step_kernel,
        out_shape=jax.ShapeDtypeStruct((NDIR, ROWS, COLS), F32),
        in_specs=[pl.BlockSpec(memory_space=pltpu.HBM)] * 10,
        out_specs=pl.BlockSpec(memory_space=pltpu.HBM),
        scratch_shapes=[
            pltpu.SMEM((2 * NDIR + 3 * NFREQ,), F32), pltpu.SMEM((4, NFREQ * NDIR), jnp.int32), pltpu.SMEM((NFREQ * NDIR,), F32),
            pltpu.VMEM((NDIR, ROWS, COLS), F32), field, two, two, field, field, tile,
            pltpu.VMEM((7, ROWS, COLS), F32), pltpu.VMEM((NDIR, ROWS, COLS), F32), longer, longer, edges, edges,
            tile, tile, tile, pltpu.VMEM((PACKED, COLS), jnp.int32), tile,
            packed, pltpu.VMEM((NFREQ * NDIR, 8, COLS), F32), all_bins, own_bins, own_bins, halo, halo, packed,
            pltpu.VMEM((2, 4, PACKED, COLS), F32), pltpu.VMEM((2, 3, PACKED, COLS), F32),
            pltpu.VMEM((NY_DEV, PACKED, COLS), F32), field,
            pltpu.VMEM((4, NFREQ * NDIR), jnp.int32), pltpu.VMEM((4, 4, NFREQ * NDIR), F32), pltpu.SMEM((4, 4, 2 * COLS), F32),
            dma((10,)), dma((parts,)), dma, dma((backs,)),
            dma((parts,)), dma((NY_DEV, parts)), dma((NY_DEV, parts)),
            dma((HALO, parts)), dma((HALO, parts)), dma((HALO, parts)), dma((HALO, parts)),
            dma((2, 3)), dma((2, 3)), dma((2,)), dma((2,)),
            dma((backs,)), dma((backs,)), dma((backs,)), dma((backs,)), dma((NY_DEV, backs)), dma((NY_DEV, backs)),
            dma((NY_DEV,)), dma((NY_DEV,)),
        ],
        compiler_params=pltpu.CompilerParams(vmem_limit_bytes=60 << 20, collective_id=0, has_side_effects=True),
    )(jnp.asarray(constants()), quad_table, coupling, spectrum, sea_depth, current, depth_slope, wind_forcing, wind_angle, land_sea)
    return out.reshape(1, NDIR, ROWS, COLS)


def solution(mesh):
    return jax.shard_map(
        on_device,
        mesh=mesh,
        in_specs=(
            P("spec", None, "space", None),
            P("space", None),
            P(None, "space", None),
            P(None, "space", None),
            P("space", None),
            P("space", None),
            P("space", None),
            P(),
            P(),
        ),
        out_specs=P("spec", None, "space", None),
        check_vma=False,
    )
```

```python
import jax
import jax.numpy as jnp
import numpy as np
from jax import lax
from jax.experimental import pallas as pl
from jax.experimental.pallas import tpu as pltpu
from jax.sharding import PartitionSpec as P

NFREQ, NDIR, ROWS, COLS = 32, 36, 64, 128
NY_DEV = 4
PACKED = 32
PLANES = NFREQ // NY_DEV
HALO = 3
IN_PARTS = ((0, 12), (12, 12), (24, 12))
OUT_PARTS = ((0, 24), (24, 12))
PLANE_BINS = NY_DEV * NDIR
F32 = jnp.float32
VMEM = pl.BlockSpec(memory_space=pltpu.VMEM)
SMEM = pl.BlockSpec(memory_space=pltpu.SMEM)
ROW_SIGN = (1, -1, 1, -1)
ROW_DIRS = ((1, 2), (-3, -4), (-1, -2), (3, 4))


def iota(shape, axis):
    return lax.broadcasted_iota(jnp.int32, shape, axis)


def sea_positions(land):
    wet = land.astype(jnp.bfloat16)
    before = (iota((COLS, COLS), 0) < iota((COLS, COLS), 1)).astype(F32).astype(jnp.bfloat16)
    rank = jnp.dot(wet, before, preferred_element_type=F32)
    count = jnp.dot(wet, jnp.ones((COLS, COLS), jnp.bfloat16), preferred_element_type=F32)
    above = (iota((ROWS, ROWS), 0) > iota((ROWS, ROWS), 1)).astype(F32).astype(jnp.bfloat16)
    start = jnp.dot(above, count.astype(jnp.bfloat16), preferred_element_type=F32)
    return start.astype(jnp.int32), rank.astype(jnp.int32), count.astype(jnp.int32)


def packing(land_ref, lane_ref, row_ref, ends_ref):
    land = land_ref[...]
    start, rank, count = sea_positions(land)
    lanes = iota((ROWS, COLS), 1)
    code = jnp.where(land > 0, lanes | ((lanes - rank) << 8), 0)
    for bit in range(7):
        moved = pltpu.roll(code, COLS - (1 << bit), 1)
        comes = ((moved >> (8 + bit)) & 1) == 1
        stays = ((code >> (8 + bit)) & 1) == 0
        code = jnp.where(comes, moved, jnp.where(stays, code, 0))
    lane_ref[...] = jnp.take_along_axis(code & 127, (lanes - start) & 127, axis=1)
    ends_ref[...] = start + count
    slots = iota((PACKED, COLS), 0) * COLS + iota((PACKED, COLS), 1)

    def count_row(r, total):
        return total + (ends_ref[pl.ds(r, 1), :] <= slots).astype(jnp.int32)

    row_ref[...] = lax.fori_loop(0, ROWS, count_row, jnp.zeros((PACKED, COLS), jnp.int32), unroll=8)


def pack(spectrum_ref, lane_ref, row_ref, packed_ref, lo, hi, sums):
    def one(d, carry):
        carry, staged = list(carry), []
        for v in range(8):
            rows = slice(8 * v, 8 * v + 8)
            staged.append(jnp.take_along_axis(spectrum_ref[d, rows, :], lane_ref[rows, :], axis=1))
        for q in range(4):
            rows = slice(8 * q, 8 * q + 8)
            source = row_ref[rows, :]
            within, block = source & 7, source >> 3
            out = jnp.zeros((8, COLS), F32)
            for v in range(q, 8):
                out = jnp.where(block == v, jnp.take_along_axis(staged[v], within, axis=0), out)
            packed_ref[d, rows, :] = out
            carry[q] = carry[q] + out
        return tuple(carry)

    return lax.fori_loop(lo, hi, one, tuple(sums), unroll=6)


def unpacking(land_ref, slot_row_ref, slot_lane_ref):
    start, rank, _ = sea_positions(land_ref[...])
    lanes = iota((ROWS, COLS), 1)
    slot_row_ref[...] = (start + ((lanes - start) & 127)) >> 7
    slot_lane_ref[...] = (start + rank) & 127


def unpack_block(load, slot_row, slot_lane, v):
    within, block = slot_row & 7, slot_row >> 3
    staged = jnp.take_along_axis(load(0), within, axis=0)
    for q in range(1, min(v, 3) + 1):
        staged = jnp.where(block == q, jnp.take_along_axis(load(q), within, axis=0), staged)
    return jnp.take_along_axis(staged, slot_lane, axis=1)


def transport_fields(angular, root, depth_ref, current_ref, slope_ref, forcing_ref, angle_ref, fields):
    tanh_term = jnp.tanh(angular * angular / 9.81 * depth_ref[...])
    fields[0] = (0.025 * (9.81 / 2.0)) / angular * tanh_term
    fields[1] = 0.025 * current_ref[0]
    fields[2] = 0.025 * current_ref[1]
    turning = 0.2 * (1.0 - tanh_term)
    fields[3] = turning * slope_ref[0]
    fields[4] = turning * slope_ref[1]
    wind = 0.05 * root * forcing_ref[...]
    fields[5] = wind * jnp.cos(angle_ref[...])
    fields[6] = wind * jnp.sin(angle_ref[...])


def transport(trig_ref, spectrum_ref, land_ref, fields, base, ahead, behind, edges, lo, hi):
    rows, lanes = iota((ROWS, COLS), 0), iota((ROWS, COLS), 1)

    def one(j, carry):
        cosine, sine = trig_ref[j], trig_ref[NDIR + j]
        energy = jnp.where(land_ref[...] > 0, spectrum_ref[j], 0.0)
        group = fields[0]
        along = group * cosine + fields[1]
        fx, bx = jnp.maximum(along, 0.0) * energy, jnp.minimum(along, 0.0) * energy
        across = group * sine + fields[2]
        fy, by = jnp.maximum(across, 0.0) * energy, jnp.minimum(across, 0.0) * energy
        turn = sine * fields[3] - cosine * fields[4]
        ft, bt = jnp.maximum(turn, 0.0) * energy, jnp.minimum(turn, 0.0) * energy
        edges[0, pl.ds(j, 1), :] = fx[ROWS - 1 :, :]
        edges[1, pl.ds(j, 1), :] = bx[:1, :]
        prev_x = jnp.where(rows == 0, 0.0, pltpu.roll(fx, 1, 0))
        next_x = jnp.where(rows == ROWS - 1, 0.0, pltpu.roll(bx, ROWS - 1, 0))
        prev_y = jnp.where(lanes == 0, 0.0, pltpu.roll(fy, 1, 1))
        next_y = jnp.where(lanes == COLS - 1, 0.0, pltpu.roll(by, COLS - 1, 1))
        change = (fx + next_x - (prev_x + bx)) + (fy + next_y - (prev_y + by)) + (ft - bt)
        wind = jnp.maximum(cosine * fields[5] + sine * fields[6], 0.0) * energy
        base[j] = energy - change + wind
        ahead[j + 1] = ft
        behind[j] = bt
        return carry

    lax.fori_loop(lo, hi, one, 0, unroll=4)


def quad_masks(table, mask_out):
    shape = (4, NFREQ * NDIR)
    row, k = iota(shape, 0), iota(shape, 1)
    freq = (k * 1821) >> 16
    direction = k - freq * NDIR
    sign = 1 - 2 * (row & 1)
    near = jnp.clip(freq + 2 * sign, 0, NFREQ - 1)
    far = jnp.clip(freq + 3 * sign, 0, NFREQ - 1)
    far = jnp.where(far == near, -NFREQ, far)
    for which in range(2):
        turn = jnp.where(row == 0, ROW_DIRS[0][which], ROW_DIRS[1][which])
        turn = jnp.where(row == 2, ROW_DIRS[2][which], jnp.where(row == 3, ROW_DIRS[3][which], turn))
        there = direction + turn
        there = jnp.where(there < 0, there + NDIR, jnp.where(there >= NDIR, there - NDIR, there))
        for step, target in enumerate((near, far)):
            mask_out[step * 2 + which] = jnp.where(table == target * NDIR + there, 1.0, 0.0).astype(F32)


def quadruplets(table_ref, coupling_ref, x, q_one, q_two, n, z):
    def one(j, carry):
        for f in range(NY_DEV):
            k = z * PLANE_BINS + f * NDIR + j
            energy = x[k]
            a, b = x[table_ref[0, k]], x[table_ref[1, k]]
            c, d = x[table_ref[2, k]], x[table_ref[3, k]]
            scaled = coupling_ref[k] * energy
            first = scaled * (energy * (a + b) - 2.0 * a * b)
            second = scaled * (energy * (c + d) - 2.0 * c * d)
            q_one[f * NDIR + j] = first
            q_two[f * NDIR + j] = second
            n[HALO + f, j] = -2.0 * (first + second)
        return carry

    lax.fori_loop(0, NDIR, one, 0, unroll=4)


def scatter(mask_ref, shift, q_one, q_two, n, targets, lo, hi):
    def one(j, carry):
        source = {}
        for turns in ROW_DIRS:
            for turn in turns:
                at = j - turn
                source[turn] = jnp.where(at < 0, at + NDIR, jnp.where(at >= NDIR, at - NDIR, at))
        for t in targets:
            total = n[t, j] if HALO <= t < HALO + NY_DEV else None
            for row in range(4):
                q = q_one if row < 2 else q_two
                for step in range(2):
                    f = t - HALO - ROW_SIGN[row] * (2 + step)
                    if not 0 <= f < NY_DEV:
                        continue
                    for which in range(2):
                        s = source[ROW_DIRS[row][which]]
                        term = mask_ref[step * 2 + which, row, shift + f * NDIR + s] * q[f * NDIR + s]
                        total = term if total is None else total + term
            n[t, j] = total
        return carry

    lax.fori_loop(lo, hi, one, 0, unroll=3)


def step_kernel(
    const_hbm, table_hbm, coupling_hbm,
    spectrum_hbm, depth_hbm, current_hbm, slope_hbm, forcing_hbm, angle_hbm, land_hbm,
    out_hbm,
    const_ref, table_ref, coupling_ref,
    spectrum_ref, depth_ref, current_ref, slope_ref, forcing_ref, angle_ref, land_ref,
    fields, base, ahead, behind, edges, edge_in, slot_row, slot_lane, lane_ref, row_ref, ends_ref,
    packed, x, n, q_one, q_two, up_in, down_in, source, sums, sums_in, column, decay, table_v, mask_v, mask_ref,
    load_sem, part_sem, mask_sem, out_sem,
    own_sem, send_y, recv_y, send_up, recv_up, send_down, recv_down, send_mean, recv_mean, send_edge, recv_edge,
    send_cup, recv_cup, send_cdown, recv_cdown, send_back, recv_back, send_col, recv_col,
):
    space, spec = lax.axis_index("space"), lax.axis_index("spec")
    z, y = spec // NY_DEV, spec % NY_DEV
    has_up, has_down = z < PLANES - 1, z > 0
    not_first, not_last = space > 0, space < 7

    def to(plane, row):
        return {"spec": plane * NY_DEV + row}

    def remote(src, dst, send, recv, device):
        return pltpu.make_async_remote_copy(
            src_ref=src, dst_ref=dst, send_sem=send, recv_sem=recv, device_id=device, device_id_type=pl.DeviceIdType.MESH
        )

    def signal(device):
        pl.semaphore_signal(barrier, inc=1, device_id=device, device_id_type=pl.DeviceIdType.MESH)

    def spectrum_load(c):
        part = pl.ds(*IN_PARTS[c])
        return pltpu.make_async_copy(spectrum_hbm.at[part], spectrum_ref.at[part], part_sem.at[c])

    pairs = (
        (land_hbm, land_ref), (const_hbm, const_ref), (depth_hbm, depth_ref), (current_hbm, current_ref),
        (slope_hbm, slope_ref), (forcing_hbm, forcing_ref), (angle_hbm, angle_ref), (table_hbm, table_ref),
        (coupling_hbm, coupling_ref), (table_hbm, table_v),
    )
    loads = [pltpu.make_async_copy(src, dst, load_sem.at[i]) for i, (src, dst) in enumerate(pairs)]
    loads[0].start()
    for c in range(len(IN_PARTS)):
        spectrum_load(c).start()
    for load in loads[1:]:
        load.start()

    barrier = pltpu.get_barrier_semaphore()
    leads = space % 2 == 1
    follows = jnp.logical_not(leads)
    in_spec = NY_DEV - 1 + has_up.astype(jnp.int32) + has_down.astype(jnp.int32)
    in_space = not_first.astype(jnp.int32) + not_last.astype(jnp.int32)
    for d in range(1, NY_DEV):
        signal(to(z, (y + d) % NY_DEV))

    @pl.when(has_up)
    def _():
        signal(to(z + 1, y))

    @pl.when(has_down)
    def _():
        signal(to(z - 1, y))

    def greet():
        pl.semaphore_wait(barrier, in_spec + jnp.where(leads, 0, in_space))

        @pl.when(not_first)
        def _():
            signal({"space": space - 1})

        @pl.when(not_last)
        def _():
            signal({"space": space + 1})

    def bins(freq, c):
        return pl.ds(freq * NDIR + IN_PARTS[c][0], IN_PARTS[c][1])

    def eight(row):
        return pl.ds(pl.multiple_of(row * 8, 8), 8)

    def at(f, c):
        return x.at[bins(z * NY_DEV + f, c)]

    def along_y(d, c):
        row = (y + d) % NY_DEV
        src = packed.at[pl.ds(*IN_PARTS[c]), eight(row), :]
        return remote(src, at(y, c), send_y.at[d, c], recv_y.at[y, c], to(z, row))

    def from_y(d, c):
        f = (y + d) % NY_DEV
        return remote(at(f, c), at(f, c), send_y.at[d, c], recv_y.at[f, c], to(z, f))

    def up(f, c, src=None):
        src = at(f, c) if src is None else src
        return remote(src, at(f, c), send_up.at[f - 1, c], recv_up.at[f - 1, c], to(z + 1, y))

    def down(f, c, src=None):
        src = at(f, c) if src is None else src
        return remote(src, at(f, c), send_down.at[f, c], recv_down.at[f, c], to(z - 1, y))

    def forward(f, c, src=None):
        @pl.when(has_up & (f >= 1))
        def _():
            up(f, c, src).start()

        @pl.when(has_down & (f < HALO))
        def _():
            down(f, c, src).start()

    def own(c):
        return pltpu.make_async_copy(packed.at[pl.ds(*IN_PARTS[c]), eight(y), :], at(y, c), own_sem.at[c])

    loads[0].wait()
    packing(land_ref, lane_ref, row_ref, ends_ref)
    for c in range(len(IN_PARTS)):
        spectrum_load(c).wait()
    for load in loads[1:]:
        load.wait()

    def send(c):
        forward(y, c, packed.at[pl.ds(*IN_PARTS[c]), eight(y), :])
        for d in (1, 3, 2):
            along_y(d, c).start()
        own(c).start()

    mine = [jnp.zeros((8, COLS), F32)] * 4
    for c, (first, number) in enumerate(IN_PARTS):
        mine = pack(spectrum_ref, lane_ref, row_ref, packed, first, first + number, mine)
        if c == 0:
            greet()

        @pl.when(leads)
        def _():
            send(c)

    def across(stage, way):
        step = 1 << stage
        other = z + step if way == 0 else z - step
        there = (other < PLANES) if way == 0 else (other >= 0)
        comes = (z >= step) if way == 0 else (z + step < PLANES)
        copy = remote(
            sums.at[way, stage], sums_in.at[way, stage], send_mean.at[way, stage], recv_mean.at[way, stage], to(other, y)
        )
        return there, comes, copy

    def sums_out(stage):
        for way in range(2):
            there, _, copy = across(stage, way)

            @pl.when(there)
            def _():
                copy.start()

    def sums_come(stage):
        for way in range(2):
            _, comes, copy = across(stage, way)

            @pl.when(comes)
            def _():
                copy.wait_recv()
                sums[way, stage + 1] = sums[way, stage] + sums_in[way, stage]

            @pl.when(jnp.logical_not(comes))
            def _():
                sums[way, stage + 1] = sums[way, stage]

    for way in range(2):
        for q in range(4):
            sums[way, 0, 8 * q : 8 * q + 8, :] = mine[q]
    sums_out(0)
    def move():
        transport_fields(
            const_ref[2 * NDIR + spec], const_ref[2 * NDIR + NFREQ + spec],
            depth_ref, current_ref, slope_ref, forcing_ref, angle_ref, fields,
        )
        transport(const_ref, spectrum_ref, land_ref, fields, base, ahead, behind, edges, 0, NDIR)
        ahead[0] = ahead[NDIR]
        behind[NDIR] = behind[0]

    @pl.when(follows)
    def _():
        move()
        for c in range(len(IN_PARTS)):
            send(c)

    for c in range(len(IN_PARTS)):
        for d in (1, 3, 2):
            from_y(d, c).wait_recv()
            forward((y + d) % NY_DEV, c)
        own(c).wait()
        if c == 1:
            sums_come(0)
            sums_out(1)


    quad_masks(table_v[...], mask_v)
    shift = z * (PLANE_BINS - COLS)
    masks = pltpu.make_async_copy(mask_v.at[:, :, pl.ds(pl.multiple_of(z * COLS, COLS), 2 * COLS)], mask_ref, mask_sem)
    masks.start()
    unpacking(land_ref, slot_row, slot_lane)

    @pl.when(has_down)
    def _():
        for c in range(len(IN_PARTS)):
            for f in range(1, NY_DEV):
                remote(at(f - NY_DEV, c), at(f - NY_DEV, c), send_up.at[f - 1, c], recv_up.at[f - 1, c], to(z - 1, y)).wait_recv()

    @pl.when(has_up)
    def _():
        for c in range(len(IN_PARTS)):
            for f in range(HALO):
                remote(at(NY_DEV + f, c), at(NY_DEV + f, c), send_down.at[f, c], recv_down.at[f, c], to(z + 1, y)).wait_recv()

    quadruplets(table_ref, coupling_ref, x, q_one, q_two, n, z)
    masks.wait()
    sums_come(1)
    sums_out(2)

    def give_up(c):
        part = pl.ds(*OUT_PARTS[c])
        return remote(n.at[pl.ds(HALO + NY_DEV, HALO), part], up_in.at[:, part], send_cup.at[c], recv_cup.at[c], to(z + 1, y))

    def give_down(c):
        part = pl.ds(*OUT_PARTS[c])
        return remote(n.at[pl.ds(0, HALO), part], down_in.at[:, part], send_cdown.at[c], recv_cdown.at[c], to(z - 1, y))

    for c, (first, number) in enumerate(OUT_PARTS):
        scatter(mask_ref, shift, q_one, q_two, n, (0, 1, 2, 7, 8, 9), first, first + number)

        @pl.when(has_up)
        def _():
            give_up(c).start()

        @pl.when(has_down)
        def _():
            give_down(c).start()

    @pl.when(leads)
    def _():
        move()

    def edge(side):
        return remote(edges.at[side], edge_in.at[side], send_edge.at[side], recv_edge.at[side],
                      {"space": space + 1 if side == 0 else space - 1})

    @pl.when(leads)
    def _():
        pl.semaphore_wait(barrier, in_space)

    @pl.when(not_last)
    def _():
        edge(0).start()

    @pl.when(not_first)
    def _():
        edge(1).start()

    scatter(mask_ref, shift, q_one, q_two, n, (3, 4, 5, 6), 0, NDIR)

    @pl.when(z == 0)
    def _():
        def fold(j, carry):
            n[HALO, j] += n[0, j] + n[1, j] + n[2, j]
            return carry

        lax.fori_loop(0, NDIR, fold, 0)

    @pl.when(z == PLANES - 1)
    def _():
        def fold(j, carry):
            n[6, j] += n[7, j] + n[8, j] + n[9, j]
            return carry

        lax.fori_loop(0, NDIR, fold, 0)

    for side, there in ((0, not_first), (1, not_last)):
        @pl.when(there)
        def _():
            remote(edges.at[side], edge_in.at[side], send_edge.at[side], recv_edge.at[side],
                   {"space": space - 1 if side == 0 else space + 1}).wait_recv()

        @pl.when(jnp.logical_not(there))
        def _():
            edge_in[side] = jnp.zeros((NDIR, COLS), F32)

    def back(d, c):
        f = (y + d) % NY_DEV
        part = pl.ds(*OUT_PARTS[c])
        return remote(n.at[HALO + f, part], source.at[part, eight(y), :], send_back.at[d, c], recv_back.at[y, c], to(z, f))

    def finish(j, carry):
        base[j, 0:1, :] += edge_in[0, pl.ds(j, 1), :]
        base[j, ROWS - 1 :, :] -= edge_in[1, pl.ds(j, 1), :]
        for v in range(8):
            rows = slice(8 * v, 8 * v + 8)
            added = unpack_block(lambda q: source[j, 8 * q : 8 * q + 8, :], slot_row[rows, :], slot_lane[rows, :], v)
            moved = base[j, rows, :] + ahead[j, rows, :] - behind[j + 1, rows, :]
            moved = moved - decay[rows, :] * spectrum_ref[j, rows, :]
            base[j, rows, :] = jnp.where(land_ref[rows, :] > 0, moved + added, 0.0)
        return carry

    def complete(c):
        first, number = OUT_PARTS[c]
        part = pl.ds(first, number)

        @pl.when(has_down)
        def _():
            remote(n.at[pl.ds(HALO + NY_DEV, HALO), part], up_in.at[:, part], send_cup.at[c], recv_cup.at[c], to(z - 1, y)).wait_recv()

            def add(j, carry):
                for f in range(HALO):
                    n[HALO + f, j] += up_in[f, j]
                return carry

            lax.fori_loop(first, first + number, add, 0, unroll=2)

        @pl.when(has_up)
        def _():
            remote(n.at[pl.ds(0, HALO), part], down_in.at[:, part], send_cdown.at[c], recv_cdown.at[c], to(z + 1, y)).wait_recv()

            def add(j, carry):
                for f in range(1, NY_DEV):
                    n[HALO + f, j] += down_in[f - 1, j]
                return carry

            lax.fori_loop(first, first + number, add, 0, unroll=2)

        for d in (2, 1, 3):
            back(d, c).start()

        def keep(j, carry):
            source[j, eight(y), :] = n[HALO + y, j]
            return carry

        lax.fori_loop(first, first + number, keep, 0, unroll=2)

    def result(c):
        part = pl.ds(*OUT_PARTS[c])
        return pltpu.make_async_copy(base.at[part], out_hbm.at[part], out_sem.at[c])

    def conclude(c):
        first, number = OUT_PARTS[c]
        for d in (1, 3, 2):
            f = (y + d) % NY_DEV
            at_source = source.at[pl.ds(first, number), eight(f), :]
            remote(n.at[HALO, pl.ds(first, number)], at_source, send_back.at[d, c], recv_back.at[f, c], to(z, f)).wait_recv()
        lax.fori_loop(first, first + number, finish, 0, unroll=6)
        result(c).start()

    complete(0)
    sums_come(2)
    column[y] = sums[0, 3] + sums[1, 3] - sums[0, 0]

    def to_columns(d):
        return remote(column.at[y], column.at[y], send_col.at[d], recv_col.at[y], to(z, (y + d) % NY_DEV))

    for d in (2, 1, 3):
        to_columns(d).start()

    complete(1)
    for d in (1, 3, 2):
        f = (y + d) % NY_DEV
        remote(column.at[f], column.at[f], send_col.at[d], recv_col.at[f], to(z, f)).wait_recv()
    mean = (column[0] + column[1] + column[2] + column[3]) * (1.0 / (NFREQ * NDIR))
    sums[0, 3] = mean * mean
    rate = const_ref[2 * NDIR + 2 * NFREQ + spec]
    for v in range(8):
        rows = slice(8 * v, 8 * v + 8)
        square = unpack_block(lambda q: sums[0, 3, 8 * q : 8 * q + 8, :], slot_row[rows, :], slot_lane[rows, :], v)
        decay[rows, :] = rate * square
    conclude(0)
    for c in range(2, len(OUT_PARTS)):
        complete(c)
        conclude(c - 1)
    conclude(len(OUT_PARTS) - 1)

    for c in range(len(IN_PARTS)):
        for d in range(1, NY_DEV):
            along_y(d, c).wait_send()

    @pl.when(has_up)
    def _():
        for c in range(len(IN_PARTS)):
            for f in range(1, NY_DEV):
                up(f, c).wait_send()
        for c in range(len(OUT_PARTS)):
            give_up(c).wait_send()

    @pl.when(has_down)
    def _():
        for c in range(len(IN_PARTS)):
            for f in range(HALO):
                down(f, c).wait_send()
        for c in range(len(OUT_PARTS)):
            give_down(c).wait_send()

    for stage in range(3):
        for way in range(2):
            there, _, copy = across(stage, way)

            @pl.when(there)
            def _():
                copy.wait_send()

    for d in range(1, NY_DEV):
        to_columns(d).wait_send()
        for c in range(len(OUT_PARTS)):
            back(d, c).wait_send()
    for c in range(len(OUT_PARTS)):
        result(c).wait()

    @pl.when(not_last)
    def _():
        edge(0).wait_send()

    @pl.when(not_first)
    def _():
        edge(1).wait_send()


def constants():
    heading = np.float32(2.0 * np.pi / NDIR) * np.arange(NDIR, dtype=np.float32)
    growth = 1.1 ** np.arange(NFREQ)
    parts = [np.cos(heading), np.sin(heading), 2.0 * np.pi * 0.04 * growth, np.sqrt(growth), 0.3 * (growth / growth[-1]) ** 2]
    return np.concatenate(parts).astype(np.float32)


def on_device(spectrum, sea_depth, current, depth_slope, wind_forcing, wind_angle, land_sea, quad_table, coupling):
    spectrum = spectrum.reshape(NDIR, ROWS, COLS)
    dma, parts, backs = pltpu.SemaphoreType.DMA, len(IN_PARTS), len(OUT_PARTS)
    tile, field, two = pltpu.VMEM((ROWS, COLS), jnp.int32), pltpu.VMEM((ROWS, COLS), F32), pltpu.VMEM((2, ROWS, COLS), F32)
    longer = pltpu.VMEM((NDIR + 1, ROWS, COLS), F32)
    edges = pltpu.VMEM((2, NDIR, COLS), F32)
    own_bins = pltpu.VMEM((PLANE_BINS, 8, COLS), F32)
    all_bins = pltpu.VMEM((NY_DEV + 2 * HALO, NDIR, 8, COLS), F32)
    halo = pltpu.VMEM((HALO, NDIR, 8, COLS), F32)
    packed = pltpu.VMEM((NDIR, PACKED, COLS), F32)
    out = pl.pallas_call(
        step_kernel,
        out_shape=jax.ShapeDtypeStruct((NDIR, ROWS, COLS), F32),
        in_specs=[pl.BlockSpec(memory_space=pltpu.HBM)] * 10,
        out_specs=pl.BlockSpec(memory_space=pltpu.HBM),
        scratch_shapes=[
            pltpu.SMEM((2 * NDIR + 3 * NFREQ,), F32), pltpu.SMEM((4, NFREQ * NDIR), jnp.int32), pltpu.SMEM((NFREQ * NDIR,), F32),
            pltpu.VMEM((NDIR, ROWS, COLS), F32), field, two, two, field, field, tile,
            pltpu.VMEM((7, ROWS, COLS), F32), pltpu.VMEM((NDIR, ROWS, COLS), F32), longer, longer, edges, edges,
            tile, tile, tile, pltpu.VMEM((PACKED, COLS), jnp.int32), tile,
            packed, pltpu.VMEM((NFREQ * NDIR, 8, COLS), F32), all_bins, own_bins, own_bins, halo, halo, packed,
            pltpu.VMEM((2, 4, PACKED, COLS), F32), pltpu.VMEM((2, 3, PACKED, COLS), F32),
            pltpu.VMEM((NY_DEV, PACKED, COLS), F32), field,
            pltpu.VMEM((4, NFREQ * NDIR), jnp.int32), pltpu.VMEM((4, 4, NFREQ * NDIR), F32), pltpu.SMEM((4, 4, 2 * COLS), F32),
            dma((10,)), dma((parts,)), dma, dma((backs,)),
            dma((parts,)), dma((NY_DEV, parts)), dma((NY_DEV, parts)),
            dma((HALO, parts)), dma((HALO, parts)), dma((HALO, parts)), dma((HALO, parts)),
            dma((2, 3)), dma((2, 3)), dma((2,)), dma((2,)),
            dma((backs,)), dma((backs,)), dma((backs,)), dma((backs,)), dma((NY_DEV, backs)), dma((NY_DEV, backs)),
            dma((NY_DEV,)), dma((NY_DEV,)),
        ],
        compiler_params=pltpu.CompilerParams(vmem_limit_bytes=60 << 20, collective_id=0, has_side_effects=True),
    )(jnp.asarray(constants()), quad_table, coupling, spectrum, sea_depth, current, depth_slope, wind_forcing, wind_angle, land_sea)
    return out.reshape(1, NDIR, ROWS, COLS)


def solution(mesh):
    return jax.shard_map(
        on_device,
        mesh=mesh,
        in_specs=(
            P("spec", None, "space", None),
            P("space", None),
            P(None, "space", None),
            P(None, "space", None),
            P("space", None),
            P("space", None),
            P("space", None),
            P(),
            P(),
        ),
        out_specs=P("spec", None, "space", None),
        check_vma=False,
    )
```

```python
import jax
import jax.numpy as jnp
import numpy as np
from jax import lax
from jax.experimental import pallas as pl
from jax.experimental.pallas import tpu as pltpu
from jax.sharding import PartitionSpec as P

NFREQ, NDIR, ROWS, COLS = 32, 36, 64, 128
NY_DEV = 4
PACKED = 32
PLANES = NFREQ // NY_DEV
HALO = 3
IN_PARTS = ((0, 12), (12, 12), (24, 12))
OUT_PARTS = ((0, 24), (24, 12))
PLANE_BINS = NY_DEV * NDIR
F32 = jnp.float32
VMEM = pl.BlockSpec(memory_space=pltpu.VMEM)
SMEM = pl.BlockSpec(memory_space=pltpu.SMEM)
ROW_SIGN = (1, -1, 1, -1)
ROW_DIRS = ((1, 2), (-3, -4), (-1, -2), (3, 4))


def iota(shape, axis):
    return lax.broadcasted_iota(jnp.int32, shape, axis)


def sea_positions(land):
    wet = land.astype(jnp.bfloat16)
    before = (iota((COLS, COLS), 0) < iota((COLS, COLS), 1)).astype(F32).astype(jnp.bfloat16)
    rank = jnp.dot(wet, before, preferred_element_type=F32)
    count = jnp.dot(wet, jnp.ones((COLS, COLS), jnp.bfloat16), preferred_element_type=F32)
    above = (iota((ROWS, ROWS), 0) > iota((ROWS, ROWS), 1)).astype(F32).astype(jnp.bfloat16)
    start = jnp.dot(above, count.astype(jnp.bfloat16), preferred_element_type=F32)
    return start.astype(jnp.int32), rank.astype(jnp.int32), count.astype(jnp.int32)


def packing(land_ref, lane_ref, row_ref, ends_ref):
    land = land_ref[...]
    start, rank, count = sea_positions(land)
    lanes = iota((ROWS, COLS), 1)
    code = jnp.where(land > 0, lanes | ((lanes - rank) << 8), 0)
    for bit in range(7):
        moved = pltpu.roll(code, COLS - (1 << bit), 1)
        comes = ((moved >> (8 + bit)) & 1) == 1
        stays = ((code >> (8 + bit)) & 1) == 0
        code = jnp.where(comes, moved, jnp.where(stays, code, 0))
    lane_ref[...] = jnp.take_along_axis(code & 127, (lanes - start) & 127, axis=1)
    ends_ref[...] = start + count
    slots = iota((PACKED, COLS), 0) * COLS + iota((PACKED, COLS), 1)

    def count_row(r, total):
        return total + (ends_ref[pl.ds(r, 1), :] <= slots).astype(jnp.int32)

    row_ref[...] = lax.fori_loop(0, ROWS, count_row, jnp.zeros((PACKED, COLS), jnp.int32), unroll=8)


def pack(spectrum_ref, lane_ref, row_ref, packed_ref, lo, hi, sums):
    def one(d, carry):
        carry, staged = list(carry), []
        for v in range(8):
            rows = slice(8 * v, 8 * v + 8)
            staged.append(jnp.take_along_axis(spectrum_ref[d, rows, :], lane_ref[rows, :], axis=1))
        for q in range(4):
            rows = slice(8 * q, 8 * q + 8)
            source = row_ref[rows, :]
            within, block = source & 7, source >> 3
            out = jnp.zeros((8, COLS), F32)
            for v in range(q, 8):
                out = jnp.where(block == v, jnp.take_along_axis(staged[v], within, axis=0), out)
            packed_ref[d, rows, :] = out
            carry[q] = carry[q] + out
        return tuple(carry)

    return lax.fori_loop(lo, hi, one, tuple(sums), unroll=6)


def unpacking(land_ref, slot_row_ref, slot_lane_ref):
    start, rank, _ = sea_positions(land_ref[...])
    lanes = iota((ROWS, COLS), 1)
    slot_row_ref[...] = (start + ((lanes - start) & 127)) >> 7
    slot_lane_ref[...] = (start + rank) & 127


def unpack_block(load, slot_row, slot_lane, v):
    within, block = slot_row & 7, slot_row >> 3
    staged = jnp.take_along_axis(load(0), within, axis=0)
    for q in range(1, min(v, 3) + 1):
        staged = jnp.where(block == q, jnp.take_along_axis(load(q), within, axis=0), staged)
    return jnp.take_along_axis(staged, slot_lane, axis=1)


def transport_fields(angular, root, depth_ref, current_ref, slope_ref, forcing_ref, angle_ref, fields):
    tanh_term = jnp.tanh(angular * angular / 9.81 * depth_ref[...])
    fields[0] = (0.025 * (9.81 / 2.0)) / angular * tanh_term
    fields[1] = 0.025 * current_ref[0]
    fields[2] = 0.025 * current_ref[1]
    turning = 0.2 * (1.0 - tanh_term)
    fields[3] = turning * slope_ref[0]
    fields[4] = turning * slope_ref[1]
    wind = 0.05 * root * forcing_ref[...]
    fields[5] = wind * jnp.cos(angle_ref[...])
    fields[6] = wind * jnp.sin(angle_ref[...])


def transport(trig_ref, spectrum_ref, land_ref, fields, base, ahead, behind, edges, lo, hi):
    rows, lanes = iota((ROWS, COLS), 0), iota((ROWS, COLS), 1)

    def one(j, carry):
        cosine, sine = trig_ref[j], trig_ref[NDIR + j]
        energy = jnp.where(land_ref[...] > 0, spectrum_ref[j], 0.0)
        group = fields[0]
        along = group * cosine + fields[1]
        fx, bx = jnp.maximum(along, 0.0) * energy, jnp.minimum(along, 0.0) * energy
        across = group * sine + fields[2]
        fy, by = jnp.maximum(across, 0.0) * energy, jnp.minimum(across, 0.0) * energy
        turn = sine * fields[3] - cosine * fields[4]
        ft, bt = jnp.maximum(turn, 0.0) * energy, jnp.minimum(turn, 0.0) * energy
        edges[0, pl.ds(j, 1), :] = fx[ROWS - 1 :, :]
        edges[1, pl.ds(j, 1), :] = bx[:1, :]
        prev_x = jnp.where(rows == 0, 0.0, pltpu.roll(fx, 1, 0))
        next_x = jnp.where(rows == ROWS - 1, 0.0, pltpu.roll(bx, ROWS - 1, 0))
        prev_y = jnp.where(lanes == 0, 0.0, pltpu.roll(fy, 1, 1))
        next_y = jnp.where(lanes == COLS - 1, 0.0, pltpu.roll(by, COLS - 1, 1))
        change = (fx + next_x - (prev_x + bx)) + (fy + next_y - (prev_y + by)) + (ft - bt)
        wind = jnp.maximum(cosine * fields[5] + sine * fields[6], 0.0) * energy
        base[j] = energy - change + wind
        ahead[j + 1] = ft
        behind[j] = bt
        return carry

    lax.fori_loop(lo, hi, one, 0, unroll=4)


def quad_masks(table, mask_out):
    shape = (4, NFREQ * NDIR)
    row, k = iota(shape, 0), iota(shape, 1)
    freq = (k * 1821) >> 16
    direction = k - freq * NDIR
    sign = 1 - 2 * (row & 1)
    near = jnp.clip(freq + 2 * sign, 0, NFREQ - 1)
    far = jnp.clip(freq + 3 * sign, 0, NFREQ - 1)
    far = jnp.where(far == near, -NFREQ, far)
    for which in range(2):
        turn = jnp.where(row == 0, ROW_DIRS[0][which], ROW_DIRS[1][which])
        turn = jnp.where(row == 2, ROW_DIRS[2][which], jnp.where(row == 3, ROW_DIRS[3][which], turn))
        there = direction + turn
        there = jnp.where(there < 0, there + NDIR, jnp.where(there >= NDIR, there - NDIR, there))
        for step, target in enumerate((near, far)):
            mask_out[step * 2 + which] = jnp.where(table == target * NDIR + there, 1.0, 0.0).astype(F32)


def quadruplets(table_ref, coupling_ref, x, q_one, q_two, n, z):
    def one(j, carry):
        for f in range(NY_DEV):
            k = z * PLANE_BINS + f * NDIR + j
            energy = x[k]
            a, b = x[table_ref[0, k]], x[table_ref[1, k]]
            c, d = x[table_ref[2, k]], x[table_ref[3, k]]
            scaled = coupling_ref[k] * energy
            first = scaled * (energy * (a + b) - 2.0 * a * b)
            second = scaled * (energy * (c + d) - 2.0 * c * d)
            q_one[f * NDIR + j] = first
            q_two[f * NDIR + j] = second
            n[HALO + f, j] = -2.0 * (first + second)
        return carry

    lax.fori_loop(0, NDIR, one, 0, unroll=4)


def scatter(mask_ref, shift, q_one, q_two, n, targets, lo, hi):
    def one(j, carry):
        source = {}
        for turns in ROW_DIRS:
            for turn in turns:
                at = j - turn
                source[turn] = jnp.where(at < 0, at + NDIR, jnp.where(at >= NDIR, at - NDIR, at))
        for t in targets:
            total = n[t, j] if HALO <= t < HALO + NY_DEV else None
            for row in range(4):
                q = q_one if row < 2 else q_two
                for step in range(2):
                    f = t - HALO - ROW_SIGN[row] * (2 + step)
                    if not 0 <= f < NY_DEV:
                        continue
                    for which in range(2):
                        s = source[ROW_DIRS[row][which]]
                        term = mask_ref[step * 2 + which, row, shift + f * NDIR + s] * q[f * NDIR + s]
                        total = term if total is None else total + term
            n[t, j] = total
        return carry

    lax.fori_loop(lo, hi, one, 0, unroll=3)


def step_kernel(
    const_hbm, table_hbm, coupling_hbm,
    spectrum_hbm, depth_hbm, current_hbm, slope_hbm, forcing_hbm, angle_hbm, land_hbm,
    out_hbm,
    const_ref, table_ref, coupling_ref,
    spectrum_ref, depth_ref, current_ref, slope_ref, forcing_ref, angle_ref, land_ref,
    fields, base, ahead, behind, edges, edge_in, slot_row, slot_lane, lane_ref, row_ref, ends_ref,
    packed, x, n, q_one, q_two, up_in, down_in, source, sums, sums_in, column, decay, table_v, mask_v, mask_ref,
    load_sem, part_sem, mask_sem, out_sem,
    own_sem, send_y, recv_y, send_up, recv_up, send_down, recv_down, send_mean, recv_mean, send_edge, recv_edge,
    send_cup, recv_cup, send_cdown, recv_cdown, send_back, recv_back, send_col, recv_col,
):
    space, spec = lax.axis_index("space"), lax.axis_index("spec")
    z, y = spec // NY_DEV, spec % NY_DEV
    has_up, has_down = z < PLANES - 1, z > 0
    not_first, not_last = space > 0, space < 7

    def to(plane, row):
        return {"spec": plane * NY_DEV + row}

    def remote(src, dst, send, recv, device):
        return pltpu.make_async_remote_copy(
            src_ref=src, dst_ref=dst, send_sem=send, recv_sem=recv, device_id=device, device_id_type=pl.DeviceIdType.MESH
        )

    def signal(device):
        pl.semaphore_signal(barrier, inc=1, device_id=device, device_id_type=pl.DeviceIdType.MESH)

    def spectrum_load(c):
        part = pl.ds(*IN_PARTS[c])
        return pltpu.make_async_copy(spectrum_hbm.at[part], spectrum_ref.at[part], part_sem.at[c])

    pairs = (
        (land_hbm, land_ref), (const_hbm, const_ref), (depth_hbm, depth_ref), (current_hbm, current_ref),
        (slope_hbm, slope_ref), (forcing_hbm, forcing_ref), (angle_hbm, angle_ref), (table_hbm, table_ref),
        (coupling_hbm, coupling_ref), (table_hbm, table_v),
    )
    loads = [pltpu.make_async_copy(src, dst, load_sem.at[i]) for i, (src, dst) in enumerate(pairs)]
    loads[0].start()
    for c in range(len(IN_PARTS)):
        spectrum_load(c).start()
    for load in loads[1:]:
        load.start()

    barrier = pltpu.get_barrier_semaphore()
    leads = space % 2 == 1
    follows = jnp.logical_not(leads)
    in_spec = NY_DEV - 1 + has_up.astype(jnp.int32) + has_down.astype(jnp.int32)
    in_space = not_first.astype(jnp.int32) + not_last.astype(jnp.int32)
    for d in range(1, NY_DEV):
        signal(to(z, (y + d) % NY_DEV))

    @pl.when(has_up)
    def _():
        signal(to(z + 1, y))

    @pl.when(has_down)
    def _():
        signal(to(z - 1, y))

    def greet():
        pl.semaphore_wait(barrier, in_spec + jnp.where(leads, 0, in_space))

        @pl.when(not_first)
        def _():
            signal({"space": space - 1})

        @pl.when(not_last)
        def _():
            signal({"space": space + 1})

    def bins(freq, c):
        return pl.ds(freq * NDIR + IN_PARTS[c][0], IN_PARTS[c][1])

    def eight(row):
        return pl.ds(pl.multiple_of(row * 8, 8), 8)

    def at(f, c):
        return x.at[bins(z * NY_DEV + f, c)]

    def along_y(d, c):
        row = (y + d) % NY_DEV
        src = packed.at[pl.ds(*IN_PARTS[c]), eight(row), :]
        return remote(src, at(y, c), send_y.at[d, c], recv_y.at[y, c], to(z, row))

    def from_y(d, c):
        f = (y + d) % NY_DEV
        return remote(at(f, c), at(f, c), send_y.at[d, c], recv_y.at[f, c], to(z, f))

    def up(f, c, src=None):
        src = at(f, c) if src is None else src
        return remote(src, at(f, c), send_up.at[f - 1, c], recv_up.at[f - 1, c], to(z + 1, y))

    def down(f, c, src=None):
        src = at(f, c) if src is None else src
        return remote(src, at(f, c), send_down.at[f, c], recv_down.at[f, c], to(z - 1, y))

    def forward(f, c, src=None):
        @pl.when(has_up & (f >= 1))
        def _():
            up(f, c, src).start()

        @pl.when(has_down & (f < HALO))
        def _():
            down(f, c, src).start()

    def own(c):
        return pltpu.make_async_copy(packed.at[pl.ds(*IN_PARTS[c]), eight(y), :], at(y, c), own_sem.at[c])

    loads[0].wait()
    packing(land_ref, lane_ref, row_ref, ends_ref)

    def send(c):
        forward(y, c, packed.at[pl.ds(*IN_PARTS[c]), eight(y), :])
        for d in (1, 3, 2):
            along_y(d, c).start()
        own(c).start()

    mine = [jnp.zeros((8, COLS), F32)] * 4
    for c, (first, number) in enumerate(IN_PARTS):
        spectrum_load(c).wait()
        mine = pack(spectrum_ref, lane_ref, row_ref, packed, first, first + number, mine)
        if c == 0:
            greet()

        @pl.when(leads)
        def _():
            send(c)

    for load in loads[1:]:
        load.wait()

    def across(stage, way):
        step = 1 << stage
        other = z + step if way == 0 else z - step
        there = (other < PLANES) if way == 0 else (other >= 0)
        comes = (z >= step) if way == 0 else (z + step < PLANES)
        copy = remote(
            sums.at[way, stage], sums_in.at[way, stage], send_mean.at[way, stage], recv_mean.at[way, stage], to(other, y)
        )
        return there, comes, copy

    def sums_out(stage):
        for way in range(2):
            there, _, copy = across(stage, way)

            @pl.when(there)
            def _():
                copy.start()

    def sums_come(stage):
        for way in range(2):
            _, comes, copy = across(stage, way)

            @pl.when(comes)
            def _():
                copy.wait_recv()
                sums[way, stage + 1] = sums[way, stage] + sums_in[way, stage]

            @pl.when(jnp.logical_not(comes))
            def _():
                sums[way, stage + 1] = sums[way, stage]

    for way in range(2):
        for q in range(4):
            sums[way, 0, 8 * q : 8 * q + 8, :] = mine[q]
    sums_out(0)
    def move():
        transport_fields(
            const_ref[2 * NDIR + spec], const_ref[2 * NDIR + NFREQ + spec],
            depth_ref, current_ref, slope_ref, forcing_ref, angle_ref, fields,
        )
        transport(const_ref, spectrum_ref, land_ref, fields, base, ahead, behind, edges, 0, NDIR)
        ahead[0] = ahead[NDIR]
        behind[NDIR] = behind[0]

    @pl.when(follows)
    def _():
        move()
        for c in range(len(IN_PARTS)):
            send(c)

    for c in range(len(IN_PARTS)):
        for d in (1, 3, 2):
            from_y(d, c).wait_recv()
            forward((y + d) % NY_DEV, c)
        own(c).wait()


    sums_come(0)
    sums_out(1)
    quad_masks(table_v[...], mask_v)
    shift = z * (PLANE_BINS - COLS)
    masks = pltpu.make_async_copy(mask_v.at[:, :, pl.ds(pl.multiple_of(z * COLS, COLS), 2 * COLS)], mask_ref, mask_sem)
    masks.start()
    unpacking(land_ref, slot_row, slot_lane)

    @pl.when(has_down)
    def _():
        for c in range(len(IN_PARTS)):
            for f in range(1, NY_DEV):
                remote(at(f - NY_DEV, c), at(f - NY_DEV, c), send_up.at[f - 1, c], recv_up.at[f - 1, c], to(z - 1, y)).wait_recv()

    @pl.when(has_up)
    def _():
        for c in range(len(IN_PARTS)):
            for f in range(HALO):
                remote(at(NY_DEV + f, c), at(NY_DEV + f, c), send_down.at[f, c], recv_down.at[f, c], to(z + 1, y)).wait_recv()

    quadruplets(table_ref, coupling_ref, x, q_one, q_two, n, z)
    masks.wait()

    @pl.when(follows)
    def _():
        sums_come(1)
        sums_out(2)

    def give_up(c):
        part = pl.ds(*OUT_PARTS[c])
        return remote(n.at[pl.ds(HALO + NY_DEV, HALO), part], up_in.at[:, part], send_cup.at[c], recv_cup.at[c], to(z + 1, y))

    def give_down(c):
        part = pl.ds(*OUT_PARTS[c])
        return remote(n.at[pl.ds(0, HALO), part], down_in.at[:, part], send_cdown.at[c], recv_cdown.at[c], to(z - 1, y))

    for c, (first, number) in enumerate(OUT_PARTS):
        scatter(mask_ref, shift, q_one, q_two, n, (0, 1, 2, 7, 8, 9), first, first + number)

        @pl.when(has_up)
        def _():
            give_up(c).start()

        @pl.when(has_down)
        def _():
            give_down(c).start()

    @pl.when(leads)
    def _():
        sums_come(1)
        sums_out(2)
        move()

    def edge(side):
        return remote(edges.at[side], edge_in.at[side], send_edge.at[side], recv_edge.at[side],
                      {"space": space + 1 if side == 0 else space - 1})

    @pl.when(leads)
    def _():
        pl.semaphore_wait(barrier, in_space)

    @pl.when(not_last)
    def _():
        edge(0).start()

    @pl.when(not_first)
    def _():
        edge(1).start()

    scatter(mask_ref, shift, q_one, q_two, n, (3, 4, 5, 6), 0, NDIR)

    @pl.when(z == 0)
    def _():
        def fold(j, carry):
            n[HALO, j] += n[0, j] + n[1, j] + n[2, j]
            return carry

        lax.fori_loop(0, NDIR, fold, 0)

    @pl.when(z == PLANES - 1)
    def _():
        def fold(j, carry):
            n[6, j] += n[7, j] + n[8, j] + n[9, j]
            return carry

        lax.fori_loop(0, NDIR, fold, 0)

    for side, there in ((0, not_first), (1, not_last)):
        @pl.when(there)
        def _():
            remote(edges.at[side], edge_in.at[side], send_edge.at[side], recv_edge.at[side],
                   {"space": space - 1 if side == 0 else space + 1}).wait_recv()

        @pl.when(jnp.logical_not(there))
        def _():
            edge_in[side] = jnp.zeros((NDIR, COLS), F32)

    def back(d, c):
        f = (y + d) % NY_DEV
        part = pl.ds(*OUT_PARTS[c])
        return remote(n.at[HALO + f, part], source.at[part, eight(y), :], send_back.at[d, c], recv_back.at[y, c], to(z, f))

    def finish(j, carry):
        base[j, 0:1, :] += edge_in[0, pl.ds(j, 1), :]
        base[j, ROWS - 1 :, :] -= edge_in[1, pl.ds(j, 1), :]
        for v in range(8):
            rows = slice(8 * v, 8 * v + 8)
            added = unpack_block(lambda q: source[j, 8 * q : 8 * q + 8, :], slot_row[rows, :], slot_lane[rows, :], v)
            moved = base[j, rows, :] + ahead[j, rows, :] - behind[j + 1, rows, :]
            moved = moved - decay[rows, :] * spectrum_ref[j, rows, :]
            base[j, rows, :] = jnp.where(land_ref[rows, :] > 0, moved + added, 0.0)
        return carry

    def complete(c):
        first, number = OUT_PARTS[c]
        part = pl.ds(first, number)

        @pl.when(has_down)
        def _():
            remote(n.at[pl.ds(HALO + NY_DEV, HALO), part], up_in.at[:, part], send_cup.at[c], recv_cup.at[c], to(z - 1, y)).wait_recv()

            def add(j, carry):
                for f in range(HALO):
                    n[HALO + f, j] += up_in[f, j]
                return carry

            lax.fori_loop(first, first + number, add, 0, unroll=2)

        @pl.when(has_up)
        def _():
            remote(n.at[pl.ds(0, HALO), part], down_in.at[:, part], send_cdown.at[c], recv_cdown.at[c], to(z + 1, y)).wait_recv()

            def add(j, carry):
                for f in range(1, NY_DEV):
                    n[HALO + f, j] += down_in[f - 1, j]
                return carry

            lax.fori_loop(first, first + number, add, 0, unroll=2)

        for d in (2, 1, 3):
            back(d, c).start()

        def keep(j, carry):
            source[j, eight(y), :] = n[HALO + y, j]
            return carry

        lax.fori_loop(first, first + number, keep, 0, unroll=2)

    def result(c):
        part = pl.ds(*OUT_PARTS[c])
        return pltpu.make_async_copy(base.at[part], out_hbm.at[part], out_sem.at[c])

    def conclude(c):
        first, number = OUT_PARTS[c]
        for d in (1, 3, 2):
            f = (y + d) % NY_DEV
            at_source = source.at[pl.ds(first, number), eight(f), :]
            remote(n.at[HALO, pl.ds(first, number)], at_source, send_back.at[d, c], recv_back.at[f, c], to(z, f)).wait_recv()
        lax.fori_loop(first, first + number, finish, 0, unroll=6)
        result(c).start()

    complete(0)
    sums_come(2)
    column[y] = sums[0, 3] + sums[1, 3] - sums[0, 0]

    def to_columns(d):
        return remote(column.at[y], column.at[y], send_col.at[d], recv_col.at[y], to(z, (y + d) % NY_DEV))

    for d in (2, 1, 3):
        to_columns(d).start()

    complete(1)
    for d in (1, 3, 2):
        f = (y + d) % NY_DEV
        remote(column.at[f], column.at[f], send_col.at[d], recv_col.at[f], to(z, f)).wait_recv()
    mean = (column[0] + column[1] + column[2] + column[3]) * (1.0 / (NFREQ * NDIR))
    sums[0, 3] = mean * mean
    rate = const_ref[2 * NDIR + 2 * NFREQ + spec]
    for v in range(8):
        rows = slice(8 * v, 8 * v + 8)
        square = unpack_block(lambda q: sums[0, 3, 8 * q : 8 * q + 8, :], slot_row[rows, :], slot_lane[rows, :], v)
        decay[rows, :] = rate * square
    conclude(0)
    for c in range(2, len(OUT_PARTS)):
        complete(c)
        conclude(c - 1)
    conclude(len(OUT_PARTS) - 1)

    for c in range(len(IN_PARTS)):
        for d in range(1, NY_DEV):
            along_y(d, c).wait_send()

    @pl.when(has_up)
    def _():
        for c in range(len(IN_PARTS)):
            for f in range(1, NY_DEV):
                up(f, c).wait_send()
        for c in range(len(OUT_PARTS)):
            give_up(c).wait_send()

    @pl.when(has_down)
    def _():
        for c in range(len(IN_PARTS)):
            for f in range(HALO):
                down(f, c).wait_send()
        for c in range(len(OUT_PARTS)):
            give_down(c).wait_send()

    for stage in range(3):
        for way in range(2):
            there, _, copy = across(stage, way)

            @pl.when(there)
            def _():
                copy.wait_send()

    for d in range(1, NY_DEV):
        to_columns(d).wait_send()
        for c in range(len(OUT_PARTS)):
            back(d, c).wait_send()
    for c in range(len(OUT_PARTS)):
        result(c).wait()

    @pl.when(not_last)
    def _():
        edge(0).wait_send()

    @pl.when(not_first)
    def _():
        edge(1).wait_send()


def constants():
    heading = np.float32(2.0 * np.pi / NDIR) * np.arange(NDIR, dtype=np.float32)
    growth = 1.1 ** np.arange(NFREQ)
    parts = [np.cos(heading), np.sin(heading), 2.0 * np.pi * 0.04 * growth, np.sqrt(growth), 0.3 * (growth / growth[-1]) ** 2]
    return np.concatenate(parts).astype(np.float32)


def on_device(spectrum, sea_depth, current, depth_slope, wind_forcing, wind_angle, land_sea, quad_table, coupling):
    spectrum = spectrum.reshape(NDIR, ROWS, COLS)
    dma, parts, backs = pltpu.SemaphoreType.DMA, len(IN_PARTS), len(OUT_PARTS)
    tile, field, two = pltpu.VMEM((ROWS, COLS), jnp.int32), pltpu.VMEM((ROWS, COLS), F32), pltpu.VMEM((2, ROWS, COLS), F32)
    longer = pltpu.VMEM((NDIR + 1, ROWS, COLS), F32)
    edges = pltpu.VMEM((2, NDIR, COLS), F32)
    own_bins = pltpu.VMEM((PLANE_BINS, 8, COLS), F32)
    all_bins = pltpu.VMEM((NY_DEV + 2 * HALO, NDIR, 8, COLS), F32)
    halo = pltpu.VMEM((HALO, NDIR, 8, COLS), F32)
    packed = pltpu.VMEM((NDIR, PACKED, COLS), F32)
    out = pl.pallas_call(
        step_kernel,
        out_shape=jax.ShapeDtypeStruct((NDIR, ROWS, COLS), F32),
        in_specs=[pl.BlockSpec(memory_space=pltpu.HBM)] * 10,
        out_specs=pl.BlockSpec(memory_space=pltpu.HBM),
        scratch_shapes=[
            pltpu.SMEM((2 * NDIR + 3 * NFREQ,), F32), pltpu.SMEM((4, NFREQ * NDIR), jnp.int32), pltpu.SMEM((NFREQ * NDIR,), F32),
            pltpu.VMEM((NDIR, ROWS, COLS), F32), field, two, two, field, field, tile,
            pltpu.VMEM((7, ROWS, COLS), F32), pltpu.VMEM((NDIR, ROWS, COLS), F32), longer, longer, edges, edges,
            tile, tile, tile, pltpu.VMEM((PACKED, COLS), jnp.int32), tile,
            packed, pltpu.VMEM((NFREQ * NDIR, 8, COLS), F32), all_bins, own_bins, own_bins, halo, halo, packed,
            pltpu.VMEM((2, 4, PACKED, COLS), F32), pltpu.VMEM((2, 3, PACKED, COLS), F32),
            pltpu.VMEM((NY_DEV, PACKED, COLS), F32), field,
            pltpu.VMEM((4, NFREQ * NDIR), jnp.int32), pltpu.VMEM((4, 4, NFREQ * NDIR), F32), pltpu.SMEM((4, 4, 2 * COLS), F32),
            dma((10,)), dma((parts,)), dma, dma((backs,)),
            dma((parts,)), dma((NY_DEV, parts)), dma((NY_DEV, parts)),
            dma((HALO, parts)), dma((HALO, parts)), dma((HALO, parts)), dma((HALO, parts)),
            dma((2, 3)), dma((2, 3)), dma((2,)), dma((2,)),
            dma((backs,)), dma((backs,)), dma((backs,)), dma((backs,)), dma((NY_DEV, backs)), dma((NY_DEV, backs)),
            dma((NY_DEV,)), dma((NY_DEV,)),
        ],
        compiler_params=pltpu.CompilerParams(vmem_limit_bytes=60 << 20, collective_id=0, has_side_effects=True),
    )(jnp.asarray(constants()), quad_table, coupling, spectrum, sea_depth, current, depth_slope, wind_forcing, wind_angle, land_sea)
    return out.reshape(1, NDIR, ROWS, COLS)


def solution(mesh):
    return jax.shard_map(
        on_device,
        mesh=mesh,
        in_specs=(
            P("spec", None, "space", None),
            P("space", None),
            P(None, "space", None),
            P(None, "space", None),
            P("space", None),
            P("space", None),
            P("space", None),
            P(),
            P(),
        ),
        out_specs=P("spec", None, "space", None),
        check_vma=False,
    )
```

```python
import jax
import jax.numpy as jnp
import numpy as np
from jax import lax
from jax.experimental import pallas as pl
from jax.experimental.pallas import tpu as pltpu
from jax.sharding import PartitionSpec as P

NFREQ, NDIR, ROWS, COLS = 32, 36, 64, 128
NY_DEV = 4
PACKED = 32
PLANES = NFREQ // NY_DEV
HALO = 3
IN_PARTS = ((0, 12), (12, 12), (24, 12))
OUT_PARTS = ((0, 24), (24, 12))
PLANE_BINS = NY_DEV * NDIR
F32 = jnp.float32
VMEM = pl.BlockSpec(memory_space=pltpu.VMEM)
SMEM = pl.BlockSpec(memory_space=pltpu.SMEM)
ROW_SIGN = (1, -1, 1, -1)
ROW_DIRS = ((1, 2), (-3, -4), (-1, -2), (3, 4))


def iota(shape, axis):
    return lax.broadcasted_iota(jnp.int32, shape, axis)


def sea_positions(land):
    wet = land.astype(jnp.bfloat16)
    before = (iota((COLS, COLS), 0) < iota((COLS, COLS), 1)).astype(F32).astype(jnp.bfloat16)
    rank = jnp.dot(wet, before, preferred_element_type=F32)
    count = jnp.dot(wet, jnp.ones((COLS, COLS), jnp.bfloat16), preferred_element_type=F32)
    above = (iota((ROWS, ROWS), 0) > iota((ROWS, ROWS), 1)).astype(F32).astype(jnp.bfloat16)
    start = jnp.dot(above, count.astype(jnp.bfloat16), preferred_element_type=F32)
    return start.astype(jnp.int32), rank.astype(jnp.int32), count.astype(jnp.int32)


def packing(land_ref, lane_ref, row_ref, ends_ref):
    land = land_ref[...]
    start, rank, count = sea_positions(land)
    lanes = iota((ROWS, COLS), 1)
    code = jnp.where(land > 0, lanes | ((lanes - rank) << 8), 0)
    for bit in range(7):
        moved = pltpu.roll(code, COLS - (1 << bit), 1)
        comes = ((moved >> (8 + bit)) & 1) == 1
        stays = ((code >> (8 + bit)) & 1) == 0
        code = jnp.where(comes, moved, jnp.where(stays, code, 0))
    lane_ref[...] = jnp.take_along_axis(code & 127, (lanes - start) & 127, axis=1)
    ends_ref[...] = start + count
    slots = iota((PACKED, COLS), 0) * COLS + iota((PACKED, COLS), 1)

    def count_row(r, total):
        return total + (ends_ref[pl.ds(r, 1), :] <= slots).astype(jnp.int32)

    row_ref[...] = lax.fori_loop(0, ROWS, count_row, jnp.zeros((PACKED, COLS), jnp.int32), unroll=8)


def pack(spectrum_ref, lane_ref, row_ref, packed_ref, lo, hi, sums):
    def one(d, carry):
        carry, staged = list(carry), []
        for v in range(8):
            rows = slice(8 * v, 8 * v + 8)
            staged.append(jnp.take_along_axis(spectrum_ref[d, rows, :], lane_ref[rows, :], axis=1))
        for q in range(4):
            rows = slice(8 * q, 8 * q + 8)
            source = row_ref[rows, :]
            within, block = source & 7, source >> 3
            out = jnp.zeros((8, COLS), F32)
            for v in range(q, 8):
                out = jnp.where(block == v, jnp.take_along_axis(staged[v], within, axis=0), out)
            packed_ref[d, rows, :] = out
            carry[q] = carry[q] + out
        return tuple(carry)

    return lax.fori_loop(lo, hi, one, tuple(sums), unroll=6)


def unpacking(land_ref, slot_row_ref, slot_lane_ref):
    start, rank, _ = sea_positions(land_ref[...])
    lanes = iota((ROWS, COLS), 1)
    slot_row_ref[...] = (start + ((lanes - start) & 127)) >> 7
    slot_lane_ref[...] = (start + rank) & 127


def unpack_block(load, slot_row, slot_lane, v):
    within, block = slot_row & 7, slot_row >> 3
    staged = jnp.take_along_axis(load(0), within, axis=0)
    for q in range(1, min(v, 3) + 1):
        staged = jnp.where(block == q, jnp.take_along_axis(load(q), within, axis=0), staged)
    return jnp.take_along_axis(staged, slot_lane, axis=1)


def transport_fields(angular, root, depth_ref, current_ref, slope_ref, forcing_ref, angle_ref, fields):
    tanh_term = jnp.tanh(angular * angular / 9.81 * depth_ref[...])
    fields[0] = (0.025 * (9.81 / 2.0)) / angular * tanh_term
    fields[1] = 0.025 * current_ref[0]
    fields[2] = 0.025 * current_ref[1]
    turning = 0.2 * (1.0 - tanh_term)
    fields[3] = turning * slope_ref[0]
    fields[4] = turning * slope_ref[1]
    wind = 0.05 * root * forcing_ref[...]
    fields[5] = wind * jnp.cos(angle_ref[...])
    fields[6] = wind * jnp.sin(angle_ref[...])


def transport(trig_ref, spectrum_ref, land_ref, fields, base, ahead, behind, edges, lo, hi):
    rows, lanes = iota((ROWS, COLS), 0), iota((ROWS, COLS), 1)

    def one(j, carry):
        cosine, sine = trig_ref[j], trig_ref[NDIR + j]
        energy = jnp.where(land_ref[...] > 0, spectrum_ref[j], 0.0)
        group = fields[0]
        along = group * cosine + fields[1]
        fx, bx = jnp.maximum(along, 0.0) * energy, jnp.minimum(along, 0.0) * energy
        across = group * sine + fields[2]
        fy, by = jnp.maximum(across, 0.0) * energy, jnp.minimum(across, 0.0) * energy
        turn = sine * fields[3] - cosine * fields[4]
        ft, bt = jnp.maximum(turn, 0.0) * energy, jnp.minimum(turn, 0.0) * energy
        edges[0, pl.ds(j, 1), :] = fx[ROWS - 1 :, :]
        edges[1, pl.ds(j, 1), :] = bx[:1, :]
        prev_x = jnp.where(rows == 0, 0.0, pltpu.roll(fx, 1, 0))
        next_x = jnp.where(rows == ROWS - 1, 0.0, pltpu.roll(bx, ROWS - 1, 0))
        prev_y = jnp.where(lanes == 0, 0.0, pltpu.roll(fy, 1, 1))
        next_y = jnp.where(lanes == COLS - 1, 0.0, pltpu.roll(by, COLS - 1, 1))
        change = (fx + next_x - (prev_x + bx)) + (fy + next_y - (prev_y + by)) + (ft - bt)
        wind = jnp.maximum(cosine * fields[5] + sine * fields[6], 0.0) * energy
        base[j] = energy - change + wind
        ahead[j + 1] = ft
        behind[j] = bt
        return carry

    lax.fori_loop(lo, hi, one, 0, unroll=4)


def quad_masks(table, mask_out):
    shape = (4, NFREQ * NDIR)
    row, k = iota(shape, 0), iota(shape, 1)
    freq = (k * 1821) >> 16
    direction = k - freq * NDIR
    sign = 1 - 2 * (row & 1)
    near = jnp.clip(freq + 2 * sign, 0, NFREQ - 1)
    far = jnp.clip(freq + 3 * sign, 0, NFREQ - 1)
    far = jnp.where(far == near, -NFREQ, far)
    for which in range(2):
        turn = jnp.where(row == 0, ROW_DIRS[0][which], ROW_DIRS[1][which])
        turn = jnp.where(row == 2, ROW_DIRS[2][which], jnp.where(row == 3, ROW_DIRS[3][which], turn))
        there = direction + turn
        there = jnp.where(there < 0, there + NDIR, jnp.where(there >= NDIR, there - NDIR, there))
        for step, target in enumerate((near, far)):
            mask_out[step * 2 + which] = jnp.where(table == target * NDIR + there, 1.0, 0.0).astype(F32)


def quadruplets(table_ref, coupling_ref, x, q_one, q_two, n, z):
    def one(j, carry):
        for f in range(NY_DEV):
            k = z * PLANE_BINS + f * NDIR + j
            energy = x[k]
            a, b = x[table_ref[0, k]], x[table_ref[1, k]]
            c, d = x[table_ref[2, k]], x[table_ref[3, k]]
            scaled = coupling_ref[k] * energy
            first = scaled * (energy * (a + b) - 2.0 * a * b)
            second = scaled * (energy * (c + d) - 2.0 * c * d)
            q_one[f * NDIR + j] = first
            q_two[f * NDIR + j] = second
            n[HALO + f, j] = -2.0 * (first + second)
        return carry

    lax.fori_loop(0, NDIR, one, 0, unroll=4)


def scatter(mask_ref, shift, q_one, q_two, n, targets, lo, hi):
    def one(j, carry):
        source = {}
        for turns in ROW_DIRS:
            for turn in turns:
                at = j - turn
                source[turn] = jnp.where(at < 0, at + NDIR, jnp.where(at >= NDIR, at - NDIR, at))
        for t in targets:
            total = n[t, j] if HALO <= t < HALO + NY_DEV else None
            for row in range(4):
                q = q_one if row < 2 else q_two
                for step in range(2):
                    f = t - HALO - ROW_SIGN[row] * (2 + step)
                    if not 0 <= f < NY_DEV:
                        continue
                    for which in range(2):
                        s = source[ROW_DIRS[row][which]]
                        term = mask_ref[step * 2 + which, row, shift + f * NDIR + s] * q[f * NDIR + s]
                        total = term if total is None else total + term
            n[t, j] = total
        return carry

    lax.fori_loop(lo, hi, one, 0, unroll=3)


def step_kernel(
    const_hbm, table_hbm, coupling_hbm,
    spectrum_hbm, depth_hbm, current_hbm, slope_hbm, forcing_hbm, angle_hbm, land_hbm,
    out_hbm,
    const_ref, table_ref, coupling_ref,
    spectrum_ref, depth_ref, current_ref, slope_ref, forcing_ref, angle_ref, land_ref,
    fields, base, ahead, behind, edges, edge_in, slot_row, slot_lane, lane_ref, row_ref, ends_ref,
    packed, x, n, q_one, q_two, up_in, down_in, source, sums, sums_in, column, decay, table_v, mask_v, mask_ref,
    load_sem, part_sem, mask_sem, out_sem,
    own_sem, send_y, recv_y, send_up, recv_up, send_down, recv_down, send_mean, recv_mean, send_edge, recv_edge,
    send_cup, recv_cup, send_cdown, recv_cdown, send_back, recv_back, send_col, recv_col,
):
    space, spec = lax.axis_index("space"), lax.axis_index("spec")
    z, y = spec // NY_DEV, spec % NY_DEV
    has_up, has_down = z < PLANES - 1, z > 0
    not_first, not_last = space > 0, space < 7

    def to(plane, row):
        return {"spec": plane * NY_DEV + row}

    def remote(src, dst, send, recv, device):
        return pltpu.make_async_remote_copy(
            src_ref=src, dst_ref=dst, send_sem=send, recv_sem=recv, device_id=device, device_id_type=pl.DeviceIdType.MESH
        )

    def signal(device):
        pl.semaphore_signal(barrier, inc=1, device_id=device, device_id_type=pl.DeviceIdType.MESH)

    def spectrum_load(c):
        part = pl.ds(*IN_PARTS[c])
        return pltpu.make_async_copy(spectrum_hbm.at[part], spectrum_ref.at[part], part_sem.at[c])

    pairs = (
        (land_hbm, land_ref), (const_hbm, const_ref), (depth_hbm, depth_ref), (current_hbm, current_ref),
        (slope_hbm, slope_ref), (forcing_hbm, forcing_ref), (angle_hbm, angle_ref), (table_hbm, table_ref),
        (coupling_hbm, coupling_ref), (table_hbm, table_v),
    )
    loads = [pltpu.make_async_copy(src, dst, load_sem.at[i]) for i, (src, dst) in enumerate(pairs)]
    loads[0].start()
    for c in range(len(IN_PARTS)):
        spectrum_load(c).start()
    for load in loads[1:]:
        load.start()

    barrier = pltpu.get_barrier_semaphore()
    leads = space % 2 == 1
    follows = jnp.logical_not(leads)
    in_spec = NY_DEV - 1 + has_up.astype(jnp.int32) + has_down.astype(jnp.int32)
    in_space = not_first.astype(jnp.int32) + not_last.astype(jnp.int32)
    for d in range(1, NY_DEV):
        signal(to(z, (y + d) % NY_DEV))

    @pl.when(has_up)
    def _():
        signal(to(z + 1, y))

    @pl.when(has_down)
    def _():
        signal(to(z - 1, y))

    def greet():
        pl.semaphore_wait(barrier, in_spec + jnp.where(leads, 0, in_space))

        @pl.when(not_first)
        def _():
            signal({"space": space - 1})

        @pl.when(not_last)
        def _():
            signal({"space": space + 1})

    def bins(freq, c):
        return pl.ds(freq * NDIR + IN_PARTS[c][0], IN_PARTS[c][1])

    def eight(row):
        return pl.ds(pl.multiple_of(row * 8, 8), 8)

    def at(f, c):
        return x.at[bins(z * NY_DEV + f, c)]

    def along_y(d, c):
        row = (y + d) % NY_DEV
        src = packed.at[pl.ds(*IN_PARTS[c]), eight(row), :]
        return remote(src, at(y, c), send_y.at[d, c], recv_y.at[y, c], to(z, row))

    def from_y(d, c):
        f = (y + d) % NY_DEV
        return remote(at(f, c), at(f, c), send_y.at[d, c], recv_y.at[f, c], to(z, f))

    def up(f, c, src=None):
        src = at(f, c) if src is None else src
        return remote(src, at(f, c), send_up.at[f - 1, c], recv_up.at[f - 1, c], to(z + 1, y))

    def down(f, c, src=None):
        src = at(f, c) if src is None else src
        return remote(src, at(f, c), send_down.at[f, c], recv_down.at[f, c], to(z - 1, y))

    def forward(f, c, src=None):
        @pl.when(has_up & (f >= 1))
        def _():
            up(f, c, src).start()

        @pl.when(has_down & (f < HALO))
        def _():
            down(f, c, src).start()

    def own(c):
        return pltpu.make_async_copy(packed.at[pl.ds(*IN_PARTS[c]), eight(y), :], at(y, c), own_sem.at[c])

    loads[0].wait()
    packing(land_ref, lane_ref, row_ref, ends_ref)

    def send(c):
        forward(y, c, packed.at[pl.ds(*IN_PARTS[c]), eight(y), :])
        for d in (1, 3, 2):
            along_y(d, c).start()
        own(c).start()

    mine = [jnp.zeros((8, COLS), F32)] * 4
    for c, (first, number) in enumerate(IN_PARTS):
        spectrum_load(c).wait()
        mine = pack(spectrum_ref, lane_ref, row_ref, packed, first, first + number, mine)
        if c == 0:
            greet()

        @pl.when(leads)
        def _():
            send(c)

    for load in loads[1:]:
        load.wait()

    def across(stage, way):
        step = 1 << stage
        other = z + step if way == 0 else z - step
        there = (other < PLANES) if way == 0 else (other >= 0)
        comes = (z >= step) if way == 0 else (z + step < PLANES)
        copy = remote(
            sums.at[way, stage], sums_in.at[way, stage], send_mean.at[way, stage], recv_mean.at[way, stage], to(other, y)
        )
        return there, comes, copy

    def sums_out(stage):
        for way in range(2):
            there, _, copy = across(stage, way)

            @pl.when(there)
            def _():
                copy.start()

    def sums_come(stage):
        for way in range(2):
            _, comes, copy = across(stage, way)

            @pl.when(comes)
            def _():
                copy.wait_recv()
                sums[way, stage + 1] = sums[way, stage] + sums_in[way, stage]

            @pl.when(jnp.logical_not(comes))
            def _():
                sums[way, stage + 1] = sums[way, stage]

    for way in range(2):
        for q in range(4):
            sums[way, 0, 8 * q : 8 * q + 8, :] = mine[q]
    sums_out(0)
    def move():
        transport_fields(
            const_ref[2 * NDIR + spec], const_ref[2 * NDIR + NFREQ + spec],
            depth_ref, current_ref, slope_ref, forcing_ref, angle_ref, fields,
        )
        transport(const_ref, spectrum_ref, land_ref, fields, base, ahead, behind, edges, 0, NDIR)
        ahead[0] = ahead[NDIR]
        behind[NDIR] = behind[0]

    @pl.when(follows)
    def _():
        move()
        for c in range(len(IN_PARTS)):
            send(c)

    for c in range(len(IN_PARTS)):
        for d in (1, 3, 2):
            from_y(d, c).wait_recv()
            forward((y + d) % NY_DEV, c)
        own(c).wait()
        if c == 1:
            sums_come(0)
            sums_out(1)


    quad_masks(table_v[...], mask_v)
    shift = z * (PLANE_BINS - COLS)
    masks = pltpu.make_async_copy(mask_v.at[:, :, pl.ds(pl.multiple_of(z * COLS, COLS), 2 * COLS)], mask_ref, mask_sem)
    masks.start()
    unpacking(land_ref, slot_row, slot_lane)

    @pl.when(has_down)
    def _():
        for c in range(len(IN_PARTS)):
            for f in range(1, NY_DEV):
                remote(at(f - NY_DEV, c), at(f - NY_DEV, c), send_up.at[f - 1, c], recv_up.at[f - 1, c], to(z - 1, y)).wait_recv()

    @pl.when(has_up)
    def _():
        for c in range(len(IN_PARTS)):
            for f in range(HALO):
                remote(at(NY_DEV + f, c), at(NY_DEV + f, c), send_down.at[f, c], recv_down.at[f, c], to(z + 1, y)).wait_recv()

    quadruplets(table_ref, coupling_ref, x, q_one, q_two, n, z)
    masks.wait()
    sums_come(1)
    sums_out(2)

    def give_up(c):
        part = pl.ds(*OUT_PARTS[c])
        return remote(n.at[pl.ds(HALO + NY_DEV, HALO), part], up_in.at[:, part], send_cup.at[c], recv_cup.at[c], to(z + 1, y))

    def give_down(c):
        part = pl.ds(*OUT_PARTS[c])
        return remote(n.at[pl.ds(0, HALO), part], down_in.at[:, part], send_cdown.at[c], recv_cdown.at[c], to(z - 1, y))

    for c, (first, number) in enumerate(OUT_PARTS):
        scatter(mask_ref, shift, q_one, q_two, n, (0, 1, 2, 7, 8, 9), first, first + number)

        @pl.when(has_up)
        def _():
            give_up(c).start()

        @pl.when(has_down)
        def _():
            give_down(c).start()

    @pl.when(leads)
    def _():
        move()

    def edge(side):
        return remote(edges.at[side], edge_in.at[side], send_edge.at[side], recv_edge.at[side],
                      {"space": space + 1 if side == 0 else space - 1})

    @pl.when(leads)
    def _():
        pl.semaphore_wait(barrier, in_space)

    @pl.when(not_last)
    def _():
        edge(0).start()

    @pl.when(not_first)
    def _():
        edge(1).start()

    scatter(mask_ref, shift, q_one, q_two, n, (3, 4, 5, 6), 0, NDIR)

    @pl.when(z == 0)
    def _():
        def fold(j, carry):
            n[HALO, j] += n[0, j] + n[1, j] + n[2, j]
            return carry

        lax.fori_loop(0, NDIR, fold, 0)

    @pl.when(z == PLANES - 1)
    def _():
        def fold(j, carry):
            n[6, j] += n[7, j] + n[8, j] + n[9, j]
            return carry

        lax.fori_loop(0, NDIR, fold, 0)

    for side, there in ((0, not_first), (1, not_last)):
        @pl.when(there)
        def _():
            remote(edges.at[side], edge_in.at[side], send_edge.at[side], recv_edge.at[side],
                   {"space": space - 1 if side == 0 else space + 1}).wait_recv()

        @pl.when(jnp.logical_not(there))
        def _():
            edge_in[side] = jnp.zeros((NDIR, COLS), F32)

    def back(d, c):
        f = (y + d) % NY_DEV
        part = pl.ds(*OUT_PARTS[c])
        return remote(n.at[HALO + f, part], source.at[part, eight(y), :], send_back.at[d, c], recv_back.at[y, c], to(z, f))

    def finish(j, carry):
        base[j, 0:1, :] += edge_in[0, pl.ds(j, 1), :]
        base[j, ROWS - 1 :, :] -= edge_in[1, pl.ds(j, 1), :]
        for v in range(8):
            rows = slice(8 * v, 8 * v + 8)
            added = unpack_block(lambda q: source[j, 8 * q : 8 * q + 8, :], slot_row[rows, :], slot_lane[rows, :], v)
            moved = base[j, rows, :] + ahead[j, rows, :] - behind[j + 1, rows, :]
            moved = moved - decay[rows, :] * spectrum_ref[j, rows, :]
            base[j, rows, :] = jnp.where(land_ref[rows, :] > 0, moved + added, 0.0)
        return carry

    def complete(c):
        first, number = OUT_PARTS[c]
        part = pl.ds(first, number)

        @pl.when(has_down)
        def _():
            remote(n.at[pl.ds(HALO + NY_DEV, HALO), part], up_in.at[:, part], send_cup.at[c], recv_cup.at[c], to(z - 1, y)).wait_recv()

            def add(j, carry):
                for f in range(HALO):
                    n[HALO + f, j] += up_in[f, j]
                return carry

            lax.fori_loop(first, first + number, add, 0, unroll=2)

        @pl.when(has_up)
        def _():
            remote(n.at[pl.ds(0, HALO), part], down_in.at[:, part], send_cdown.at[c], recv_cdown.at[c], to(z + 1, y)).wait_recv()

            def add(j, carry):
                for f in range(1, NY_DEV):
                    n[HALO + f, j] += down_in[f - 1, j]
                return carry

            lax.fori_loop(first, first + number, add, 0, unroll=2)

        for d in (2, 1, 3):
            back(d, c).start()

        def keep(j, carry):
            source[j, eight(y), :] = n[HALO + y, j]
            return carry

        lax.fori_loop(first, first + number, keep, 0, unroll=2)

    def result(c):
        part = pl.ds(*OUT_PARTS[c])
        return pltpu.make_async_copy(base.at[part], out_hbm.at[part], out_sem.at[c])

    def conclude(c):
        first, number = OUT_PARTS[c]
        for d in (1, 3, 2):
            f = (y + d) % NY_DEV
            at_source = source.at[pl.ds(first, number), eight(f), :]
            remote(n.at[HALO, pl.ds(first, number)], at_source, send_back.at[d, c], recv_back.at[f, c], to(z, f)).wait_recv()
        lax.fori_loop(first, first + number, finish, 0, unroll=6)
        result(c).start()

    complete(0)
    sums_come(2)
    column[y] = sums[0, 3] + sums[1, 3] - sums[0, 0]

    def to_columns(d):
        return remote(column.at[y], column.at[y], send_col.at[d], recv_col.at[y], to(z, (y + d) % NY_DEV))

    for d in (2, 1, 3):
        to_columns(d).start()

    complete(1)
    for d in (1, 3, 2):
        f = (y + d) % NY_DEV
        remote(column.at[f], column.at[f], send_col.at[d], recv_col.at[f], to(z, f)).wait_recv()
    mean = (column[0] + column[1] + column[2] + column[3]) * (1.0 / (NFREQ * NDIR))
    sums[0, 3] = mean * mean
    rate = const_ref[2 * NDIR + 2 * NFREQ + spec]
    for v in range(8):
        rows = slice(8 * v, 8 * v + 8)
        square = unpack_block(lambda q: sums[0, 3, 8 * q : 8 * q + 8, :], slot_row[rows, :], slot_lane[rows, :], v)
        decay[rows, :] = rate * square
    conclude(0)
    for c in range(2, len(OUT_PARTS)):
        complete(c)
        conclude(c - 1)
    conclude(len(OUT_PARTS) - 1)

    for c in range(len(IN_PARTS)):
        for d in range(1, NY_DEV):
            along_y(d, c).wait_send()

    @pl.when(has_up)
    def _():
        for c in range(len(IN_PARTS)):
            for f in range(1, NY_DEV):
                up(f, c).wait_send()
        for c in range(len(OUT_PARTS)):
            give_up(c).wait_send()

    @pl.when(has_down)
    def _():
        for c in range(len(IN_PARTS)):
            for f in range(HALO):
                down(f, c).wait_send()
        for c in range(len(OUT_PARTS)):
            give_down(c).wait_send()

    for stage in range(3):
        for way in range(2):
            there, _, copy = across(stage, way)

            @pl.when(there)
            def _():
                copy.wait_send()

    for d in range(1, NY_DEV):
        to_columns(d).wait_send()
        for c in range(len(OUT_PARTS)):
            back(d, c).wait_send()
    for c in range(len(OUT_PARTS)):
        result(c).wait()

    @pl.when(not_last)
    def _():
        edge(0).wait_send()

    @pl.when(not_first)
    def _():
        edge(1).wait_send()


def constants():
    heading = np.float32(2.0 * np.pi / NDIR) * np.arange(NDIR, dtype=np.float32)
    growth = 1.1 ** np.arange(NFREQ)
    parts = [np.cos(heading), np.sin(heading), 2.0 * np.pi * 0.04 * growth, np.sqrt(growth), 0.3 * (growth / growth[-1]) ** 2]
    return np.concatenate(parts).astype(np.float32)


def on_device(spectrum, sea_depth, current, depth_slope, wind_forcing, wind_angle, land_sea, quad_table, coupling):
    spectrum = spectrum.reshape(NDIR, ROWS, COLS)
    dma, parts, backs = pltpu.SemaphoreType.DMA, len(IN_PARTS), len(OUT_PARTS)
    tile, field, two = pltpu.VMEM((ROWS, COLS), jnp.int32), pltpu.VMEM((ROWS, COLS), F32), pltpu.VMEM((2, ROWS, COLS), F32)
    longer = pltpu.VMEM((NDIR + 1, ROWS, COLS), F32)
    edges = pltpu.VMEM((2, NDIR, COLS), F32)
    own_bins = pltpu.VMEM((PLANE_BINS, 8, COLS), F32)
    all_bins = pltpu.VMEM((NY_DEV + 2 * HALO, NDIR, 8, COLS), F32)
    halo = pltpu.VMEM((HALO, NDIR, 8, COLS), F32)
    packed = pltpu.VMEM((NDIR, PACKED, COLS), F32)
    out = pl.pallas_call(
        step_kernel,
        out_shape=jax.ShapeDtypeStruct((NDIR, ROWS, COLS), F32),
        in_specs=[pl.BlockSpec(memory_space=pltpu.HBM)] * 10,
        out_specs=pl.BlockSpec(memory_space=pltpu.HBM),
        scratch_shapes=[
            pltpu.SMEM((2 * NDIR + 3 * NFREQ,), F32), pltpu.SMEM((4, NFREQ * NDIR), jnp.int32), pltpu.SMEM((NFREQ * NDIR,), F32),
            pltpu.VMEM((NDIR, ROWS, COLS), F32), field, two, two, field, field, tile,
            pltpu.VMEM((7, ROWS, COLS), F32), pltpu.VMEM((NDIR, ROWS, COLS), F32), longer, longer, edges, edges,
            tile, tile, tile, pltpu.VMEM((PACKED, COLS), jnp.int32), tile,
            packed, pltpu.VMEM((NFREQ * NDIR, 8, COLS), F32), all_bins, own_bins, own_bins, halo, halo, packed,
            pltpu.VMEM((2, 4, PACKED, COLS), F32), pltpu.VMEM((2, 3, PACKED, COLS), F32),
            pltpu.VMEM((NY_DEV, PACKED, COLS), F32), field,
            pltpu.VMEM((4, NFREQ * NDIR), jnp.int32), pltpu.VMEM((4, 4, NFREQ * NDIR), F32), pltpu.SMEM((4, 4, 2 * COLS), F32),
            dma((10,)), dma((parts,)), dma, dma((backs,)),
            dma((parts,)), dma((NY_DEV, parts)), dma((NY_DEV, parts)),
            dma((HALO, parts)), dma((HALO, parts)), dma((HALO, parts)), dma((HALO, parts)),
            dma((2, 3)), dma((2, 3)), dma((2,)), dma((2,)),
            dma((backs,)), dma((backs,)), dma((backs,)), dma((backs,)), dma((NY_DEV, backs)), dma((NY_DEV, backs)),
            dma((NY_DEV,)), dma((NY_DEV,)),
        ],
        compiler_params=pltpu.CompilerParams(vmem_limit_bytes=60 << 20, collective_id=0, has_side_effects=True),
    )(jnp.asarray(constants()), quad_table, coupling, spectrum, sea_depth, current, depth_slope, wind_forcing, wind_angle, land_sea)
    return out.reshape(1, NDIR, ROWS, COLS)


def solution(mesh):
    return jax.shard_map(
        on_device,
        mesh=mesh,
        in_specs=(
            P("spec", None, "space", None),
            P("space", None),
            P(None, "space", None),
            P(None, "space", None),
            P("space", None),
            P("space", None),
            P("space", None),
            P(),
            P(),
        ),
        out_specs=P("spec", None, "space", None),
        check_vma=False,
    )
```
